32 devices in a mesh: dp: 32 (over z, y, x, core).
Axes of the slice: x: 2, y: 2, z: 4, core: 2. Of those that a mesh axis runs over, the one named last changes fastest.
Arguments:
- fields: bfloat16 [32, 4, 1024, 384], P('dp'), may hold values from -6 to 6
- conditions: bfloat16 [32, 4, 384], P('dp'), may hold values from -6 to 6
- step_counts: int32 [32], P('dp'), may hold values from 1 to 4, as said below
- cotangent: bfloat16 [32, 4, 1024, 384], P('dp'), may hold values from -6 to 6
- w_ada: bfloat16 [384, 2304], P('dp'), may hold values from -0.15625 to 0.15625
- b_ada: bfloat16 [2304], P('dp'), may hold values from -3 to 3
- w_qkv: bfloat16 [384, 1152], P('dp'), may hold values from -0.3125 to 0.3125
- w_out: bfloat16 [384, 384], P('dp'), may hold values from -1.25 to 1.25
- b_out: bfloat16 [384], P('dp'), may hold values from -2 to 2
- w_up: bfloat16 [384, 1536], P('dp'), may hold values from -0.3125 to 0.3125
- b_up: bfloat16 [1536], P('dp'), may hold values from -3 to 3
- w_down: bfloat16 [1536, 384], P('dp'), may hold values from -0.15625 to 0.15625
- b_down: bfloat16 [384], P('dp'), may hold values from -2 to 2
Outputs:
- layer_output: bfloat16 [32, 4, 1024, 384], P('dp')
- field_grad: float32 [32, 4, 1024, 384], P('dp')
- grad_w_ada: float32 [384, 2304], P('dp')
- grad_b_ada: float32 [2304], P('dp')
- grad_w_qkv: float32 [384, 1152], P('dp')
- grad_w_out: float32 [384, 384], P('dp')
- grad_b_out: float32 [384], P('dp')
- grad_w_up: float32 [384, 1536], P('dp')
- grad_b_up: float32 [1536], P('dp')
- grad_w_down: float32 [1536, 384], P('dp')
- grad_b_down: float32 [384], P('dp')
The draws below stay inside these ranges and needn't reach their ends.
Inputs may be any that keep to these rules, and one draw needn't show every extreme that they name: `step_counts`: each item has at least one step; some item has 4 steps and some item has one.
All inputs are finite; a program needn't handle non-finite values.
Results may differ from the reference program's by a relative error of at most 0.02.
Values may be sent and summed in bfloat16 or wider, within the bound.
No kernel may reach another device: no remote copies, remote signals or barrier semaphores. Data moves between devices by JAX's collectives and lax.ppermute only.
A program may use at most 192 MiB of HBM per device.

```python
import jax
import jax.numpy as jnp
from jax import lax

D = 384
HEADS = 6
HEAD = 64
FF = 1536
STEPS = 4
PATCHES = 1024
QBLOCK = 512
ITEMS = 32


def draw_step_counts(key, part):
    key = jax.random.fold_in(key, 11)
    key_base, key_long, key_pick, key_other = jax.random.split(key, 4)
    base = jax.random.randint(key_base, (ITEMS,), 1, 3)
    longer = jax.random.randint(key_long, (ITEMS,), 0, 6) == 0
    counts = jnp.where(longer, STEPS, base)
    pick = jax.random.randint(key_pick, (), 0, ITEMS)
    other = (pick + 1 + jax.random.randint(key_other, (), 0, ITEMS - 1)) % ITEMS
    item_position_index = jnp.arange(ITEMS, dtype=jnp.int32)
    counts = jnp.where(item_position_index == pick, STEPS, counts)
    counts = jnp.where(item_position_index == other, 1, counts)
    return counts.astype(jnp.int32)


def block_scale(own_key, extent, cuts, smallest, top_value):
    gain, own = 1.0, jax.random.fold_in(own_key, 6)
    for position, parts in cuts:
        heights = jnp.exp(jax.random.uniform(jax.random.fold_in(own, position), (parts,), jnp.float32, smallest / len(cuts), top_value / len(cuts)))
        gain = gain * jnp.repeat(heights, extent[position] // parts).reshape([-1 if axis == position else 1 for axis in range(len(extent))])
    return gain


def scatter_about(stream_key, extent, spread, bound, shards=(), kind=jnp.bfloat16):
    gain = block_scale(stream_key, extent, shards, -0.22, 0.18) if shards else 1.0
    result = jax.random.normal(stream_key, extent, jnp.float32) * spread * gain
    return jnp.minimum(jnp.maximum(result, -bound), bound).astype(kind)


def setup_inputs(seed: int = 0) -> dict:
    key_list = jax.random.split(jax.random.key(seed), 14)
    return {
        "fields": scatter_about(key_list[0], (ITEMS, STEPS, PATCHES, D), 1.0, 6.0, ((0, 32),)),
        "conditions": scatter_about(key_list[1], (ITEMS, STEPS, D), 1.0, 6.0, ((0, 32),)),
        "step_counts": draw_step_counts(jax.random.fold_in(key_list[13], 71), 0),
        "cotangent": scatter_about(key_list[3], (ITEMS, STEPS, PATCHES, D), 1.0, 6.0, ((0, 32),)),
        "w_ada": scatter_about(key_list[4], (D, 6 * D), (4 * D) ** -0.5, 0.15625, ((0, 32),)),
        "b_ada": scatter_about(key_list[5], (6 * D,), 0.5, 3.0, ((0, 32),)),
        "w_qkv": scatter_about(key_list[6], (D, 3 * D), D ** -0.5, 0.3125, ((0, 32),)),
        "w_out": scatter_about(key_list[7], (D, D), (D // 16) ** -0.5, 1.25, ((0, 32),)),
        "b_out": scatter_about(key_list[8], (D,), 0.3, 2.0, ((0, 32),)),
        "w_up": scatter_about(key_list[9], (D, FF), D ** -0.5, 0.3125, ((0, 32),)),
        "b_up": scatter_about(key_list[10], (FF,), 0.5, 3.0, ((0, 32),)),
        "w_down": scatter_about(key_list[11], (FF, D), FF ** -0.5, 0.15625, ((0, 32),)),
        "b_down": scatter_about(key_list[12], (D,), 0.3, 2.0, ((0, 32),)),
    }


@jax.custom_vjp
def low(v):
    return lax.optimization_barrier(v.astype(jnp.bfloat16)).astype(jnp.float32)

@jax.custom_vjp
def low_back(v):
    return v

def low_keep(v):
    return (low(v), None)

def low_pass(kept, grad):
    return (grad,)

def back_keep(v):
    return (v, None)

def back_low(kept, grad):
    return (low(grad),)
low.defvjp(low_keep, low_pass)
low_back.defvjp(back_keep, back_low)
eps = 1e-06
highest = lax.Precision.HIGHEST

def matmul(left, right):
    return jnp.dot(left, right, precision=highest)

def layer_norm(value):
    mean = lax.optimization_barrier(jnp.mean(value, -1, keepdims=True))
    cent = value - mean
    var = lax.optimization_barrier(jnp.mean(cent * cent, -1, keepdims=True))
    return cent * lax.rsqrt(var + eps)

def attend_block(query_blk, keys, values):
    scores = jnp.einsum('bhe,lhe->hbl', query_blk, keys, precision=highest) * 0.125
    scores = low_back(scores)
    top = lax.optimization_barrier(jnp.max(scores, -1, keepdims=True))
    expo = jnp.exp(scores - top)
    probs = low(expo / lax.optimization_barrier(jnp.sum(expo, -1, keepdims=True)))
    return jnp.einsum('hbl,lhe->bhe', probs, values, precision=highest)

def one_step(params, field, cond):
    w_ada, b_ada, w_qkv, w_out, b_out, w_up, b_up, w_down, b_down = params
    cond_act = low(jax.nn.silu(cond))
    modul = matmul(cond_act[None, :], w_ada)[0] + b_ada
    shift1, first_scale_vector, gate1, shift2, scale2, second_gate_vector = jnp.split(modul, 6)
    h_first = low(layer_norm(field) * (1.0 + first_scale_vector) + shift1)
    qkv = low_back(low(matmul(h_first, w_qkv)))
    query, keys, values = jnp.split(qkv, 3, axis=-1)
    query = query.reshape(PATCHES // QBLOCK, QBLOCK, HEADS, HEAD)
    keys = keys.reshape(PATCHES, HEADS, HEAD)
    values = values.reshape(PATCHES, HEADS, HEAD)
    block_fn = jax.checkpoint(lambda blk: attend_block(blk, keys, values))
    attended = lax.map(block_fn, query).reshape(PATCHES, D)
    attended = low_back(low(attended))
    branch1 = low_back(matmul(attended, w_out) + b_out)
    middle_residual_state = field + gate1 * branch1
    h_second = low(layer_norm(middle_residual_state) * (1.0 + scale2) + shift2)
    pre = low_back(matmul(h_second, w_up) + b_up)
    hidden = low(jax.nn.gelu(pre, approximate=False))
    second_branch_output = low_back(matmul(hidden, w_down) + b_down)
    return middle_residual_state + second_gate_vector * second_branch_output

def reference(fields, conditions, step_counts, cotangent, w_ada, b_ada, w_qkv, w_out, b_out, w_up, b_up, w_down, b_down):
    params = tuple((p.astype(jnp.float32) for p in (w_ada, b_ada, w_qkv, w_out, b_out, w_up, b_up, w_down, b_down)))
    live_all = (jnp.arange(STEPS, dtype=jnp.int32)[None, :] < step_counts[:, None]).astype(jnp.float32)

    def item_fn(carry, inputs):
        field_item, cond_item, grad_item, live = inputs
        field_f = field_item.astype(jnp.float32)
        cond_f = cond_item.astype(jnp.float32)
        grad_f = grad_item.astype(jnp.float32) * live[:, None, None]

        def forward(weights, fields_in):
            return jax.vmap(lambda xs, cs: one_step(weights, xs, cs))(fields_in, cond_f)
        layer_result_output, pull = jax.vjp(forward, params, field_f)
        grad_params, field_input_gradient = pull(grad_f)
        carry = jax.tree.map(lambda a, b: a + b, carry, grad_params)
        masked = (layer_result_output * live[:, None, None]).astype(jnp.bfloat16)
        return (carry, (masked, field_input_gradient * live[:, None, None]))
    zeros = tuple((jnp.zeros_like(p) for p in params))
    totals, (layer_output, field_grad) = lax.scan(item_fn, zeros, (fields, conditions, cotangent, live_all))
    return (layer_output, field_grad) + tuple(totals)
```

```python
import functools
import math

import jax
import jax.numpy as jnp
from jax import lax
from jax.experimental import pallas as pl
from jax.experimental.pallas import tpu as pltpu
from jax.sharding import PartitionSpec as P

HEAD = 64
PAIR = 2 * HEAD
EPS = 1e-6
LOG2E = 1.4426950408889634
VMEM_LIMIT = 60 * 2**20
bf16 = jnp.bfloat16
f32 = jnp.float32


def dot(left, right, left_dim=1, right_dim=0):
    return lax.dot_general(
        left, right, (((left_dim,), (right_dim,)), ((), ())), preferred_element_type=f32
    )


def norm(value):
    mean = jnp.mean(value, -1, keepdims=True)
    cent = value - mean
    var = jnp.mean(cent * cent, -1, keepdims=True)
    rstd = lax.rsqrt(var + EPS)
    return cent * rstd, rstd


def row_sum(value):
    return jnp.sum(value, 0, keepdims=True)


def up_to(value, unit):
    return -(-value // unit) * unit


KEEP, TAKE, CHIP, CORE = range(4)


def is_live(flags, slot, steps):
    return jnp.where(slot < steps, slot < flags[KEEP], flags[TAKE] > 0)


def last_live(flags, slot, steps):
    return jnp.where(is_live(flags, slot, steps), slot, jnp.minimum(slot, flags[KEEP] - 1))


def own_slot(flags, slot):
    return jnp.minimum(slot, flags[KEEP] - 1)


def each_shard(flags, mine_ref, other_ref):
    chips = mine_ref.shape[0]
    first = flags[CORE] == 0
    for chip in range(chips):
        place = jnp.bitwise_xor(flags[CHIP], chip)
        mine = mine_ref[place].astype(f32)
        other = other_ref[place].astype(f32)
        yield 2 * chip, jnp.where(first, mine, other)
        yield 2 * chip + 1, jnp.where(first, other, mine)


def place_columns(dest, device, block, start, rows, count, width):
    for part in range(count):
        dest[device * rows : (device + 1) * rows, part * width : (part + 1) * width] = block[
            start + part * rows : start + (part + 1) * rows
        ]


def attend_forward_body(
    steps, flags, own_x, far_x, cond, mine, other,
    qkv, expo, att, inv, mod, bias, w_f32, w_qkv,
):
    slot = pl.program_id(0)
    pair = pl.program_id(1)
    live = is_live(flags, slot, steps)
    length, width = att.shape[1:]
    devices = 2 * mine.shape[0]
    rows = width // devices

    @pl.when((slot == 0) & (pair == 0))
    def _():
        total = jnp.zeros((12, width), f32)
        for device, block in each_shard(flags, mine, other):
            place_columns(w_f32, device, block, 0, rows, 6, width)
            total = total + block[9 * rows : 9 * rows + 12]
        for part in range(6):
            cols = slice(part * width, (part + 1) * width)
            mod[:, cols] = dot(cond[...], w_f32[:, cols].astype(bf16)) + total[part : part + 1]
            bias[:, cols] = total[6 + part : 7 + part]
        for device, block in each_shard(flags, mine, other):
            place_columns(w_f32, device, block, 6 * rows, rows, 3, width)
        w_qkv[...] = w_f32[:, : 3 * width].astype(bf16)

    row_block = 256

    @pl.when(live & (pair == 0))
    def _():
        shift = mod[pl.ds(slot, 1), :width]
        scale = 1.0 + mod[pl.ds(slot, 1), width : 2 * width]

        def project(ref):
            @pl.loop(0, length // row_block)
            def _(i):
                r = pl.ds(pl.multiple_of(i * row_block, row_block), row_block)
                normed, _ = norm(ref[0, r, :].astype(f32))
                h1 = (normed * scale + shift).astype(bf16)
                qkv[0, r, :] = dot(h1, w_qkv[...]).astype(bf16)

        @pl.when(slot < steps)
        def _():
            project(own_x)

        @pl.when(slot >= steps)
        def _():
            project(far_x)

    @pl.when(live)
    def _():
        c0 = pl.multiple_of(pair * PAIR, PAIR)
        keys = qkv[0, :, pl.ds(pl.multiple_of(width + pair * PAIR, PAIR), PAIR)]
        values = qkv[0, :, pl.ds(pl.multiple_of(2 * width + pair * PAIR, PAIR), PAIR)]
        values_ones = jnp.concatenate([values, jnp.ones_like(values)], 1)
        first = lax.broadcasted_iota(jnp.int32, (row_block, PAIR), 1) < HEAD
        for i in range(length // row_block):
            r = pl.ds(i * row_block, row_block)
            query = qkv[0, r, pl.ds(c0, PAIR)]
            outs = []
            for head in range(2):
                sel = first if head == 0 else jnp.logical_not(first)
                scores = dot(jnp.where(sel, query, jnp.zeros_like(query)), keys, 1, 1)
                top = jnp.max(scores, -1, keepdims=True)
                e = jnp.exp2((scores - top) * (0.125 * LOG2E)).astype(bf16)
                expo[0, head, r, :] = e
                outs.append(dot(e, values_ones))
            out = jnp.where(first, outs[0][:, :PAIR], outs[1][:, :PAIR])
            inverse = 1.0 / jnp.where(first, outs[0][:, PAIR:], outs[1][:, PAIR:])
            att[0, r, pl.ds(c0, PAIR)] = (out * inverse).astype(bf16)
            inv[0, r, pl.ds(c0, PAIR)] = inverse


def attend_forward(flags, own_x, far_x, cond, mine, other):
    steps, length, width = own_x.shape
    slots = steps + 1
    pairs = width // PAIR

    def const(*zeros):
        return lambda s, p, flags: zeros

    def whole(s, p, flags):
        return (last_live(flags, s, steps), 0, 0)

    def expo_at(s, p, flags):
        at = last_live(flags, s, steps)
        return (at, jnp.where(at == s, p, pairs - 1), 0, 0)

    spec = pltpu.PrefetchScalarGridSpec(
        num_scalar_prefetch=1,
        grid=(slots, pairs),
        in_specs=[
            pl.BlockSpec((1, length, width), lambda s, p, flags: (own_slot(flags, s), 0, 0)),
            pl.BlockSpec((1, length, width), const(0, 0, 0)),
            pl.BlockSpec(cond.shape, const(0, 0)),
            pl.BlockSpec(mine.shape, const(0, 0, 0)),
            pl.BlockSpec(other.shape, const(0, 0, 0)),
        ],
        out_specs=[
            pl.BlockSpec((1, length, 3 * width), whole),
            pl.BlockSpec((1, 2, length, length), expo_at),
            pl.BlockSpec((1, length, width), whole),
            pl.BlockSpec((1, length, width), whole),
            pl.BlockSpec((8, 6 * width), const(0, 0)),
            pl.BlockSpec((1, 6 * width), const(0, 0)),
        ],
        scratch_shapes=[
            pltpu.VMEM((width, 6 * width), f32),
            pltpu.VMEM((width, 3 * width), bf16),
        ],
    )
    shape = jax.ShapeDtypeStruct
    return pl.pallas_call(
        functools.partial(attend_forward_body, steps),
        grid_spec=spec,
        out_shape=[
            shape((slots, length, 3 * width), bf16),
            shape((slots, 2 * pairs, length, length), bf16),
            shape((slots, length, width), bf16),
            shape((slots, length, width), f32),
            shape((8, 6 * width), f32),
            shape((1, 6 * width), f32),
        ],
        compiler_params=pltpu.CompilerParams(vmem_limit_bytes=VMEM_LIMIT),
        cost_estimate=pl.CostEstimate(
            flops=6 * 10**9, bytes_accessed=40 * 10**6, transcendentals=2 * 10**7
        ),
        name="attend_forward",
    )(flags, own_x, far_x, cond, mine, other)


def feed_forward_body(
    steps, flags, own_x, far_x, own_g, far_g, att, inv, mod, bias, mine, other,
    own_out, far_out, grad_x1, grad_att, grad_mod, packed, bias_sum,
    x_s, g_s, w_out, w_up, w_down, sum_out, sum_up, sum_down_t, down_f32,
):
    slot = pl.program_id(0)
    step = pl.program_id(1)
    live = is_live(flags, slot, steps)
    width = x_s.shape[1]
    hidden_units = w_up.shape[1]
    ratio = hidden_units // width
    chips = mine.shape[0]
    rows = width // (2 * chips)

    @pl.when((slot == 0) & (step == 0))
    def _():
        for device, block in each_shard(flags, mine, other):
            place_columns(sum_out, device, block, 0, rows, 1, width)
            place_columns(sum_up, device, block, rows, rows, ratio, width)
            place_columns(
                down_f32, device, block, (1 + ratio) * rows, ratio * rows, 1, width
            )
        w_out[...] = sum_out[...].astype(bf16)
        w_up[...] = sum_up[...].astype(bf16)
        w_down[...] = down_f32[...].astype(bf16)
        for ref in (sum_out, sum_up, sum_down_t, bias_sum):
            ref[...] = jnp.zeros_like(ref)

    @pl.when(step == 0)
    def _():
        grad_mod[...] = jnp.zeros_like(grad_mod)

    @pl.when((slot < steps) & jnp.logical_not(live))
    def _():
        own_out[...] = jnp.zeros_like(own_out)

    @pl.when(live)
    def _():
        @pl.when(slot < steps)
        def _():
            x_s[...] = own_x[0].astype(f32)
            g_s[...] = own_g[0].astype(f32)

        @pl.when(slot >= steps)
        def _():
            x_s[...] = far_x[0].astype(f32)
            g_s[...] = far_g[0].astype(f32)

        def vector(part):
            return mod[pl.ds(slot, 1), part * width : (part + 1) * width]

        gate1, shift2, scale2, gate2 = vector(2), vector(3), 1.0 + vector(4), vector(5)
        b_out = bias[:, :width]
        b_up = bias[:, width : width + hidden_units]
        b_down = bias[:, width + hidden_units :]
        attended = att[0]
        branch1 = dot(attended, w_out[...]) + b_out
        x1 = x_s[...] + gate1 * branch1
        normed2, rstd = norm(x1)
        h2 = (normed2 * scale2 + shift2).astype(bf16)
        pre = dot(h2, w_up[...]) + b_up
        cdf = 0.5 * (1.0 + lax.erf(pre * (1 / math.sqrt(2.0))))
        hidden = (pre * cdf).astype(bf16)
        slope = cdf + pre * jnp.exp2(pre * pre * (-0.5 * LOG2E)) * (1 / math.sqrt(2 * math.pi))
        branch2 = dot(hidden, w_down[...]) + b_down
        result = (x1 + gate2 * branch2).astype(bf16)

        @pl.when(slot < steps)
        def _():
            own_out[0] = result

        @pl.when(slot >= steps)
        def _():
            far_out[0] = result

        grad = g_s[...]
        grad_b2 = (gate2 * grad).astype(bf16)
        grad_pre = (dot(grad_b2, w_down[...], 1, 1) * slope).astype(bf16)
        grad_h2 = dot(grad_pre, w_up[...], 1, 1)
        grad_n = grad_h2 * scale2
        g_x1 = grad + rstd * (
            grad_n
            - jnp.mean(grad_n, -1, keepdims=True)
            - normed2 * jnp.mean(grad_n * normed2, -1, keepdims=True)
        )
        grad_b1 = (gate1 * g_x1).astype(bf16)
        grad_x1[0] = g_x1
        grad_att[0] = (dot(grad_b1, w_out[...], 1, 1) * inv[0]).astype(bf16)
        grad_mod[0, 2:3] += row_sum(g_x1 * branch1)
        grad_mod[0, 3:4] += row_sum(grad_h2)
        grad_mod[0, 4:5] += row_sum(grad_h2 * normed2)
        grad_mod[0, 5:6] += row_sum(grad * branch2)
        sum_out[...] += dot(attended, grad_b1, 0, 0)
        sum_up[...] += dot(h2, grad_pre, 0, 0)
        sum_down_t[...] += dot(grad_b2, hidden, 0, 0)
        bias_sum[:, :width] += row_sum(grad_b1.astype(f32))
        bias_sum[:, width : width + hidden_units] += row_sum(grad_pre.astype(f32))
        bias_sum[:, width + hidden_units :] += row_sum(grad_b2.astype(f32))

    @pl.when((slot == steps) & (step == pl.num_programs(1) - 1))
    def _():
        down_f32[...] = sum_down_t[...].T
        for device in range(2 * chips):
            place = (
                jnp.bitwise_xor(flags[CORE], device & 1) * chips
                + jnp.bitwise_xor(flags[CHIP], device >> 1)
            )
            span = slice(device * rows, (device + 1) * rows)
            packed[place, :rows] = sum_out[span]
            for part in range(ratio):
                packed[place, (1 + part) * rows : (2 + part) * rows] = sum_up[
                    span, part * width : (part + 1) * width
                ]
            packed[place, (1 + ratio) * rows : (1 + 2 * ratio) * rows] = down_f32[
                device * ratio * rows : (device + 1) * ratio * rows
            ]


def feed_forward(flags, own_x, far_x, own_g, far_g, att, inv, mod, bias, mine, other, hidden_units):
    steps, length, width = own_x.shape
    slots = steps + 1
    row_block = 512
    blocks = length // row_block
    chips = mine.shape[0]
    rows = width // (2 * chips)
    ratio = hidden_units // width
    packed_rows = up_to((1 + 2 * ratio) * rows, 8)

    def const(*zeros):
        return lambda s, b, flags: zeros

    def own(s, b, flags):
        return (own_slot(flags, s), jnp.where(s < flags[KEEP], b, blocks - 1), 0)

    def far(s, b, flags):
        return (0, jnp.where(s < steps, 0, b), 0)

    def at(s, b, flags):
        live = last_live(flags, s, steps)
        return (live, jnp.where(live == s, b, blocks - 1), 0)

    def own_result(s, b, flags):
        return (jnp.minimum(s, steps - 1), jnp.where(s < steps, b, blocks - 1), 0)

    def block(where):
        return pl.BlockSpec((1, row_block, width), where)

    def fixed(array_shape):
        return pl.BlockSpec(array_shape, const(*[0] * len(array_shape)))

    spec = pltpu.PrefetchScalarGridSpec(
        num_scalar_prefetch=1,
        grid=(slots, blocks),
        in_specs=[
            block(own), block(far), block(own), block(far), block(at), block(at),
            fixed(mod.shape), fixed(bias.shape), fixed(mine.shape), fixed(other.shape),
        ],
        out_specs=[
            block(own_result), block(far), block(at), block(at),
            pl.BlockSpec((1, 8, width), lambda s, b, flags: (s, 0, 0)),
            fixed((2 * chips, packed_rows, width)),
            fixed(bias.shape),
        ],
        scratch_shapes=[
            pltpu.VMEM((row_block, width), f32),
            pltpu.VMEM((row_block, width), f32),
            pltpu.VMEM((width, width), bf16),
            pltpu.VMEM((width, hidden_units), bf16),
            pltpu.VMEM((hidden_units, width), bf16),
            pltpu.VMEM((width, width), f32),
            pltpu.VMEM((width, hidden_units), f32),
            pltpu.VMEM((width, hidden_units), f32),
            pltpu.VMEM((hidden_units, width), f32),
        ],
    )
    shape = jax.ShapeDtypeStruct
    return pl.pallas_call(
        functools.partial(feed_forward_body, steps),
        grid_spec=spec,
        out_shape=[
            shape((steps, length, width), bf16),
            shape((1, length, width), bf16),
            shape((slots, length, width), f32),
            shape((slots, length, width), bf16),
            shape((slots, 8, width), f32),
            shape((2 * chips, packed_rows, width), f32),
            shape(bias.shape, f32),
        ],
        compiler_params=pltpu.CompilerParams(vmem_limit_bytes=VMEM_LIMIT),
        cost_estimate=pl.CostEstimate(
            flops=20 * 10**9, bytes_accessed=40 * 10**6, transcendentals=10**7
        ),
        name="feed_forward",
    )(flags, own_x, far_x, own_g, far_g, att, inv, mod, bias, mine, other)


def attend_backward_body(
    steps, flags, own_x, far_x, qkv, expo, att, grad_att, grad_x1, mod, mine, other,
    own_grad, far_grad, grad_mod, packed, w_f32, w_qkv, g_qkv, keys_t, values_t,
):
    slot = pl.program_id(0)
    pair = pl.program_id(1)
    last_pair = pl.num_programs(1) - 1
    live = is_live(flags, slot, steps)
    length, width = att.shape[1:]
    chips = mine.shape[0]
    rows = width // (2 * chips)
    row_block = 512

    @pl.when((slot == 0) & (pair == 0))
    def _():
        for device, block in each_shard(flags, mine, other):
            place_columns(w_f32, device, block, 6 * rows, rows, 3, width)
        w_qkv[...] = w_f32[...].astype(bf16)
        w_f32[...] = jnp.zeros_like(w_f32)

    @pl.when(pair == 0)
    def _():
        grad_mod[...] = jnp.zeros_like(grad_mod)

    @pl.when((slot < steps) & jnp.logical_not(live))
    def _():
        own_grad[...] = jnp.zeros_like(own_grad)

    @pl.when(live)
    def _():
        c0 = pl.multiple_of(pair * PAIR, PAIR)
        c1 = pl.multiple_of(width + pair * PAIR, PAIR)
        c2 = pl.multiple_of(2 * width + pair * PAIR, PAIR)
        keys = qkv[0, :, pl.ds(c1, PAIR)]
        values = qkv[0, :, pl.ds(c2, PAIR)]
        values_ones = jnp.concatenate([values, jnp.ones_like(values)], 1)
        lane = lax.broadcasted_iota(jnp.int32, (row_block, PAIR), 1)
        first = lane < HEAD
        for i in range(length // row_block):
            r = pl.ds(i * row_block, row_block)
            query = qkv[0, r, pl.ds(c0, PAIR)]
            g_att = grad_att[0, r, pl.ds(c0, PAIR)]
            product = g_att.astype(f32) * att[0, r, pl.ds(c0, PAIR)].astype(f32)
            query_t = query.T
            g_att_t = g_att.T
            grads_q = []
            for head in range(2):
                sel = first if head == 0 else jnp.logical_not(first)
                delta = jnp.sum(jnp.where(sel, product, 0.0), -1, keepdims=True)
                high = delta.astype(bf16).astype(f32)
                extra = jnp.where(
                    lane == 0, -high, jnp.where(lane == 1, high - delta, 0.0)
                ).astype(bf16)
                left = jnp.concatenate([jnp.where(sel, g_att, jnp.zeros_like(g_att)), extra], 1)
                e = expo[0, head, r, :]
                grad_s = e * dot(left, values_ones, 1, 1).astype(bf16)
                grads_q.append(dot(grad_s, keys))
                span = slice(head * HEAD, (head + 1) * HEAD)
                add_k = dot(query_t[span], grad_s)
                add_v = dot(g_att_t[span], e)
                if i == 0:
                    keys_t[span] = add_k
                    values_t[span] = add_v
                else:
                    keys_t[span] += add_k
                    values_t[span] += add_v
            g_qkv[r, pl.ds(c0, PAIR)] = (
                jnp.where(first, grads_q[0], grads_q[1]) * 0.125
            ).astype(bf16)
        g_qkv[:, pl.ds(c1, PAIR)] = (keys_t[...] * 0.125).astype(bf16).T
        g_qkv[:, pl.ds(c2, PAIR)] = values_t[...].astype(bf16).T

    @pl.when(live & (pair == last_pair))
    def _():
        shift = mod[pl.ds(slot, 1), :width]
        scale = 1.0 + mod[pl.ds(slot, 1), width : 2 * width]

        def finish(x_ref, out_ref):
            for i in range(length // row_block):
                r = pl.ds(i * row_block, row_block)
                normed, rstd = norm(x_ref[0, r, :].astype(f32))
                h1 = (normed * scale + shift).astype(bf16)
                grad = g_qkv[r, :]
                grad_h1 = dot(grad, w_qkv[...], 1, 1)
                w_f32[...] += dot(h1, grad, 0, 0)
                grad_mod[0, 0:1] += row_sum(grad_h1)
                grad_mod[0, 1:2] += row_sum(grad_h1 * normed)
                grad_n = grad_h1 * scale
                out_ref[0, r, :] = (
                    grad_x1[0, r, :]
                    + rstd
                    * (
                        grad_n
                        - jnp.mean(grad_n, -1, keepdims=True)
                        - normed * jnp.mean(grad_n * normed, -1, keepdims=True)
                    )
                ).astype(out_ref.dtype)

        @pl.when(slot < steps)
        def _():
            finish(own_x, own_grad)

        @pl.when(slot >= steps)
        def _():
            finish(far_x, far_grad)

    @pl.when((slot == steps) & (pair == last_pair))
    def _():
        for device in range(2 * chips):
            place = (
                jnp.bitwise_xor(flags[CORE], device & 1) * chips
                + jnp.bitwise_xor(flags[CHIP], device >> 1)
            )
            for part in range(3):
                packed[place, part * rows : (part + 1) * rows] = w_f32[
                    device * rows : (device + 1) * rows, part * width : (part + 1) * width
                ]


def attend_backward(flags, own_x, far_x, qkv, expo, att, grad_att, grad_x1, mod, mine, other):
    steps, length, width = own_x.shape
    slots = steps + 1
    pairs = width // PAIR
    chips = mine.shape[0]
    packed_rows = up_to(3 * width // (2 * chips), 8)

    def const(*zeros):
        return lambda s, p, flags: zeros

    def whole(s, p, flags):
        return (last_live(flags, s, steps), 0, 0)

    def expo_at(s, p, flags):
        at = last_live(flags, s, steps)
        return (at, jnp.where(at == s, p, pairs - 1), 0, 0)

    def block(where):
        return pl.BlockSpec((1, length, width), where)

    def fixed(array_shape):
        return pl.BlockSpec(array_shape, const(*[0] * len(array_shape)))

    spec = pltpu.PrefetchScalarGridSpec(
        num_scalar_prefetch=1,
        grid=(slots, pairs),
        in_specs=[
            block(lambda s, p, flags: (own_slot(flags, s), 0, 0)),
            block(const(0, 0, 0)),
            pl.BlockSpec((1, length, 3 * width), whole),
            pl.BlockSpec((1, 2, length, length), expo_at),
            block(whole), block(whole), block(whole),
            fixed(mod.shape), fixed(mine.shape), fixed(other.shape),
        ],
        out_specs=[
            block(lambda s, p, flags: (jnp.minimum(s, steps - 1), 0, 0)),
            block(const(0, 0, 0)),
            pl.BlockSpec((1, 8, width), lambda s, p, flags: (s, 0, 0)),
            fixed((2 * chips, packed_rows, width)),
        ],
        scratch_shapes=[
            pltpu.VMEM((width, 3 * width), f32),
            pltpu.VMEM((width, 3 * width), bf16),
            pltpu.VMEM((length, 3 * width), bf16),
            pltpu.VMEM((PAIR, length), f32),
            pltpu.VMEM((PAIR, length), f32),
        ],
    )
    shape = jax.ShapeDtypeStruct
    return pl.pallas_call(
        functools.partial(attend_backward_body, steps),
        grid_spec=spec,
        out_shape=[
            shape((steps, length, width), f32),
            shape((1, length, width), bf16),
            shape((slots, 8, width), f32),
            shape((2 * chips, packed_rows, width), f32),
        ],
        compiler_params=pltpu.CompilerParams(vmem_limit_bytes=VMEM_LIMIT),
        cost_estimate=pl.CostEstimate(
            flops=20 * 10**9, bytes_accessed=60 * 10**6, transcendentals=0
        ),
        name="attend_backward",
    )(flags, own_x, far_x, qkv, expo, att, grad_att, grad_x1, mod, mine, other)


def swap(array, mask):
    count = lax.axis_size("dp")
    return lax.ppermute(array, "dp", [(i, i ^ mask) for i in range(count)])


def chip_groups(devices):
    bits = (devices // 2).bit_length() - 1
    if bits == 4:
        return ((2, 3), (1,), (0,))
    return tuple((b,) for b in reversed(range(bits)))


def group_masks(group):
    return [sum(((k >> i) & 1) << b for i, b in enumerate(group)) for k in range(1, 1 << len(group))]


def gather_chips(block):
    held = block[None]
    for group in reversed(chip_groups(lax.axis_size("dp"))):
        held = jnp.concatenate([held] + [swap(held, mask << 1) for mask in group_masks(group)], 0)
    return held


def scatter_core(packed):
    half = packed.shape[0] // 2
    return packed[:half] + swap(packed[half:].astype(bf16), 1).astype(f32)


def scatter_group(held, group):
    masks = group_masks(group)
    part = held.shape[0] // (len(masks) + 1)
    total = held[:part]
    for k, mask in enumerate(masks):
        total = total + swap(held[(k + 1) * part : (k + 2) * part].astype(bf16), mask << 1).astype(f32)
    return total


def body(
    fields, conditions, step_counts, cotangent,
    w_ada, b_ada, w_qkv, w_out, b_out, w_up, b_up, w_down, b_down,
):
    devices = lax.axis_size("dp")
    me = lax.axis_index("dp")
    steps, length, width = fields.shape[1:]
    hidden_units = w_up.shape[1]
    ratio = hidden_units // width
    rows = width // devices
    fields, conditions, cotangent = fields[0], conditions[0], cotangent[0]

    count = step_counts[0]
    head = jnp.concatenate([conditions, jnp.full((4, width), count, bf16)], 0)
    other_head = swap(head, 1)
    other_count = other_head[steps, 0].astype(jnp.int32)
    give = count - other_count >= 2
    take = other_count - count >= 2
    keep = count - give.astype(jnp.int32)
    flags = jnp.stack([keep, take.astype(jnp.int32), me >> 1, me & 1]).astype(jnp.int32)
    far_x = swap(lax.dynamic_index_in_dim(fields, count - 1, 0), 1)
    far_g = swap(lax.dynamic_index_in_dim(cotangent, count - 1, 0), 1)
    far_cond = lax.dynamic_index_in_dim(other_head, other_count - 1, 0)
    cond = jnp.concatenate([conditions, far_cond, jnp.zeros((7 - steps, width), bf16)], 0)
    cond_act = jax.nn.silu(cond.astype(f32)).astype(bf16)

    def columns(shard):
        return [shard[:, i : i + width] for i in range(0, shard.shape[1], width)]

    def whole_bias(shard):
        spread = jnp.where(jnp.arange(devices)[:, None] == me, shard[None, :], jnp.zeros((), bf16))
        return spread.reshape(-1, width)

    biases = [whole_bias(b) for b in (b_ada, b_out, b_up, b_down)]
    first = columns(w_ada) + columns(w_qkv) + biases
    first.append(jnp.zeros((-(9 * rows + 12) % 16, width), bf16))
    second = columns(w_out) + columns(w_up) + [w_down]
    second.append(jnp.zeros((-(1 + 2 * ratio) * rows % 16, width), bf16))
    mine_a = gather_chips(jnp.concatenate(first, 0))
    other_a = swap(mine_a, 1)
    mine_b = gather_chips(jnp.concatenate(second, 0))
    other_b = swap(mine_b, 1)

    qkv, expo, att, inv, mod, bias = attend_forward(
        flags, fields, far_x, cond_act, mine_a, other_a
    )
    own_out, far_out, grad_x1, grad_att, grad_mod2, packed2, bias_sum = feed_forward(
        flags, fields, far_x, cotangent, far_g, att, inv, mod, bias, mine_b, other_b, hidden_units
    )
    groups = chip_groups(devices)
    held2 = scatter_core(packed2)
    for group in groups:
        held2 = scatter_group(held2, group)
    own_grad, far_grad, grad_mod1, packed1 = attend_backward(
        flags, fields, far_x, qkv, expo, att, grad_att, grad_x1, mod, mine_a, other_a
    )
    held1 = scatter_core(packed1)
    for group in groups:
        held1 = scatter_group(held1, group)
    sums1, sums2 = held1[0], held2[0]

    grad_mod = (grad_mod1 + grad_mod2)[:, :6].reshape(-1, width)
    note = jnp.concatenate([grad_mod, bias_sum.reshape(-1, width), cond_act.astype(f32)], 0)
    note = note.astype(bf16)
    slots = steps + 1
    note = jnp.concatenate([note, jnp.zeros((-note.shape[0] % 16, width), bf16)], 0)
    mine_n = gather_chips(note)
    notes = jnp.concatenate([mine_n, swap(mine_n, 1)], 0)
    all_mod = notes[:, : 6 * slots].reshape(devices * slots, 6 * width)
    all_bias = jnp.sum(notes[:, 6 * slots : 6 * slots + 6].astype(f32), 0).reshape(-1)
    all_cond = notes[:, 6 * slots + 6 : 7 * slots + 6].reshape(devices * slots, width)
    own_cond = lax.dynamic_slice_in_dim(all_cond, me * rows, rows, 1)
    grad_ada = jnp.einsum("sm,sn->mn", own_cond, all_mod, preferred_element_type=f32)
    sum_ada = jnp.sum(all_mod.astype(f32), 0)

    def own_part(vector):
        size = vector.shape[0] // devices
        return lax.dynamic_slice_in_dim(vector, me * size, size, 0)

    back_out = swap(far_out, 1)
    back_grad = swap(far_grad, 1).astype(f32)

    def put_back(array, back):
        now = lax.dynamic_index_in_dim(array, count - 1, 0)
        return lax.dynamic_update_index_in_dim(array, jnp.where(give, back, now), count - 1, 0)

    def from_columns(block, start, parts):
        return jnp.concatenate(
            [block[start + i * rows : start + (i + 1) * rows] for i in range(parts)], 1
        )

    return (
        put_back(own_out, back_out)[None],
        put_back(own_grad, back_grad)[None],
        grad_ada,
        own_part(sum_ada),
        from_columns(sums1, 0, 3),
        sums2[:rows],
        own_part(all_bias[:width]),
        from_columns(sums2, rows, ratio),
        own_part(all_bias[width : width + hidden_units]),
        sums2[(1 + ratio) * rows : (1 + 2 * ratio) * rows],
        own_part(all_bias[width + hidden_units :]),
    )


def solution(mesh):
    item, matrix, vector = P("dp", None, None, None), P("dp", None), P("dp")
    return jax.shard_map(
        body,
        mesh=mesh,
        in_specs=(
            item, P("dp", None, None), vector, item,
            matrix, vector, matrix, matrix, vector, matrix, vector, matrix, vector,
        ),
        out_specs=(
            item, item, matrix, vector, matrix, matrix, vector, matrix, vector, matrix, vector,
        ),
        check_vma=False,
    )
```

```python
import functools
import math

import jax
import jax.numpy as jnp
from jax import lax
from jax.experimental import pallas as pl
from jax.experimental.pallas import tpu as pltpu
from jax.sharding import PartitionSpec as P

HEAD = 64
PAIR = 2 * HEAD
EPS = 1e-6
LOG2E = 1.4426950408889634
VMEM_LIMIT = 60 * 2**20
bf16 = jnp.bfloat16
f32 = jnp.float32
shape_of = jax.ShapeDtypeStruct


def dot(left, right, left_dim=1, right_dim=0):
    return lax.dot_general(
        left, right, (((left_dim,), (right_dim,)), ((), ())), preferred_element_type=f32
    )


def norm(value):
    mean = jnp.mean(value, -1, keepdims=True)
    cent = value - mean
    var = jnp.mean(cent * cent, -1, keepdims=True)
    rstd = lax.rsqrt(var + EPS)
    return cent * rstd, rstd


def row_sum(value):
    return jnp.sum(value, 0, keepdims=True)


def up_to(value, unit):
    return -(-value // unit) * unit


def call(body, grid, in_specs, out_specs, out_shape, scratch, name, flops, args):
    return pl.pallas_call(
        body,
        grid_spec=pltpu.PrefetchScalarGridSpec(
            num_scalar_prefetch=1,
            grid=grid,
            in_specs=in_specs,
            out_specs=out_specs,
            scratch_shapes=scratch,
        ),
        out_shape=out_shape,
        compiler_params=pltpu.CompilerParams(vmem_limit_bytes=VMEM_LIMIT),
        cost_estimate=pl.CostEstimate(flops=flops, bytes_accessed=10**7, transcendentals=0),
        name=name,
    )(*args)


def fixed(shape):
    return pl.BlockSpec(shape, lambda *at: (0,) * len(shape))


anywhere = pl.BlockSpec(memory_space=pl.ANY)

KEEP, TAKE, PLACE, CORE, ME = range(5)


def own_slot(flags, slot):
    return jnp.minimum(slot, flags[KEEP] - 1)


def is_live(flags, slot):
    return slot < flags[KEEP] + flags[TAKE]


def live_at(flags, slot, block, blocks):
    live = flags[KEEP] + flags[TAKE]
    return jnp.minimum(slot, live - 1), jnp.where(slot < live, block, blocks - 1)


def result_slot(flags, slot, steps):
    after = jnp.clip(slot - flags[TAKE], flags[KEEP] - 1, steps - 1)
    return jnp.where(slot < flags[KEEP], slot, after)


def kinds(flags, slot, steps):
    own = slot < flags[KEEP]
    far = (slot == flags[KEEP]) & (flags[TAKE] > 0)
    return own, far, jnp.logical_not(own | far) & (slot - flags[TAKE] < steps)


def pack_body(flags, ada, qkv, out, up, down, bias, first, second, first_s, second_s):
    rows, width = out.shape
    me = flags[ME]
    first_s[...] = jnp.zeros_like(first_s)
    second_s[...] = jnp.zeros_like(second_s)

    def put(dest, start, ref):
        for part in range(ref.shape[1] // width):
            dest[start + part * rows : start + (part + 1) * rows] = ref[
                :, part * width : (part + 1) * width
            ].astype(f32)

    put(first_s, 0, ada)
    put(first_s, 6 * rows, qkv)
    put(second_s, 0, out)
    put(second_s, rows, up)
    after = rows + up.shape[1] * rows // width
    second_s[after : after + down.shape[0]] = down[...].astype(f32)
    source = lax.broadcasted_iota(jnp.int32, (bias.shape[1], width), 0)
    lane = lax.broadcasted_iota(jnp.int32, (bias.shape[1], width), 1)
    start = 0
    for i, count in enumerate((6 * rows, rows, up.shape[1] * rows // width, rows)):
        at = lax.rem(me * count, width) + source - start
        at = jnp.where(at >= width, at - width, at)
        hit = (source >= start) & (source < start + count) & (at == lane)
        first_s[9 * rows + i : 9 * rows + i + 1] = dot(bias[...], jnp.where(hit, 1.0, 0.0).astype(bf16))
        start += count
    first[...] = first_s[...].astype(bf16)
    second[...] = second_s[...].astype(bf16)


def pack_shards(flags, ada, qkv, out, up, down, bias):
    rows, width = out.shape
    sizes = (up_to(9 * rows + 4, 16), up_to(rows + up.shape[1] * rows // width + down.shape[0], 16))
    args = (flags, ada, qkv, out, up, down, bias)
    return call(
        pack_body, (1,), [fixed(a.shape) for a in args[1:]], [fixed((n, width)) for n in sizes],
        [shape_of((n, width), bf16) for n in sizes], [pltpu.VMEM((n, width), f32) for n in sizes],
        "pack_shards", 10**7, args,
    )


def each_shard(flags, mine_ref, other_ref):
    first = flags[CORE] == 0
    chips = mine_ref.shape[0]
    for chip in range(chips):
        mine = mine_ref[chip_order(chip, chips)].astype(f32)
        other = other_ref[chip_order(chip, chips)].astype(f32)
        yield 2 * chip, jnp.where(first, mine, other)
        yield 2 * chip + 1, jnp.where(first, other, mine)


def place_columns(dest, device, block, start, rows, count, width):
    for part in range(count):
        dest[device * rows : (device + 1) * rows, part * width : (part + 1) * width] = block[
            start + part * rows : start + (part + 1) * rows
        ]


def attend_pair(qkv, pair, expo, att, inv):
    length = att.shape[-2]
    row_block = 256
    keys = qkv[0, 1, pair]
    values = qkv[0, 2, pair]
    values_ones = jnp.concatenate([values, jnp.ones_like(values)], 1)
    first = lax.broadcasted_iota(jnp.int32, (row_block, PAIR), 1) < HEAD
    for i in range(length // row_block):
        r = pl.ds(i * row_block, row_block)
        query = qkv[0, 0, pair, r, :]
        outs = []
        for head in range(2):
            sel = first if head == 0 else jnp.logical_not(first)
            scores = dot(jnp.where(sel, query, jnp.zeros_like(query)), keys, 1, 1)
            top = jnp.max(scores, -1, keepdims=True)
            e = jnp.exp2((scores - top) * (0.125 * LOG2E)).astype(bf16)
            expo[0, head, r, :] = e
            outs.append(dot(e, values_ones))
        out = jnp.where(first, outs[0][:, :PAIR], outs[1][:, :PAIR])
        inverse = 1.0 / jnp.where(first, outs[0][:, PAIR:], outs[1][:, PAIR:])
        att[0, 0, r, :] = (out * inverse).astype(bf16)
        inv[0, 0, r, :] = inverse


def project_body(
    flags, own_x, far_x, cond, mine, other,
    qkv, expo, att, inv, mod, bias, w_qkv, w_f32, bias_f32,
):
    slot = pl.program_id(0)
    pair = pl.program_id(1)
    length, width = own_x.shape[1:]
    devices = 2 * mine.shape[0]
    rows = width // devices
    pairs = width // PAIR

    @pl.when((slot == 0) & (pair == 0))
    def _():
        bias_f32[...] = jnp.zeros_like(bias_f32)
        lane = lax.broadcasted_iota(jnp.int32, (1, width), 1)
        for device, block in each_shard(flags, mine, other):
            place_columns(w_f32, device, block, 0, rows, 6, width)
            start = 0
            for i, count in enumerate((6 * rows, rows, bias_f32.shape[0] * rows - 8 * rows, rows)):
                low, high = device * count, (device + 1) * count
                for part in range(low // width, (high - 1) // width + 1):
                    at = lane + part * width
                    bias_f32[start + part : start + part + 1] += jnp.where(
                        (at >= low) & (at < high), block[9 * rows + i : 9 * rows + i + 1], 0.0
                    )
                start += devices * count // width
        for part in range(6):
            cols = slice(part * width, (part + 1) * width)
            mod[:, cols] = dot(cond[...], w_f32[:, cols].astype(bf16)) + bias_f32[part : part + 1]
        for part in range(bias_f32.shape[0] - 6):
            bias[:, part * width : (part + 1) * width] = bias_f32[6 + part : 7 + part]
        for device, block in each_shard(flags, mine, other):
            place_columns(w_f32, device, block, 6 * rows, rows, 3, width)
        w_qkv[...] = w_f32[:, : 3 * width].astype(bf16)

    @pl.when((pair == 0) & is_live(flags, slot))
    def _():
        shift = mod[pl.ds(slot, 1), :width]
        scale = 1.0 + mod[pl.ds(slot, 1), width : 2 * width]
        row_block = 256

        def project(ref):
            @pl.loop(0, length // row_block)
            def _(i):
                r = pl.ds(pl.multiple_of(i * row_block, row_block), row_block)
                normed, _ = norm(ref[0, r, :].astype(f32))
                h1 = (normed * scale + shift).astype(bf16)
                result = dot(h1, w_qkv[...]).astype(bf16)
                for kind in range(3):
                    for p in range(pairs):
                        at = kind * width + p * PAIR
                        qkv[0, kind, p, r, :] = result[:, at : at + PAIR]

        @pl.when(slot < flags[KEEP])
        def _():
            project(own_x)

        @pl.when(slot >= flags[KEEP])
        def _():
            project(far_x)

    @pl.when(is_live(flags, slot))
    def _():
        attend_pair(qkv, pair, expo, att, inv)


def project_attend(flags, own_x, far_x, cond, mine, other, bias_rows):
    steps, length, width = own_x.shape
    pairs = width // PAIR
    here = pairs - 1
    args = (flags, own_x, far_x, cond, mine, other)

    def at(s, p, flags):
        return live_at(flags, s, p, here) + (0, 0)

    whole = pl.BlockSpec((1, 3, pairs, length, PAIR), lambda s, p, flags: (at(s, p, flags)[0], 0, 0, 0, 0))
    part = pl.BlockSpec((1, 1, length, PAIR), at)
    return call(
        project_body,
        (steps, here),
        [
            pl.BlockSpec((1, length, width), lambda s, p, flags: (own_slot(flags, s), 0, 0)),
        ] + [fixed(a.shape) for a in args[2:]],
        [
            whole,
            pl.BlockSpec((1, 2, length, length), at),
            part, part,
            fixed((8, 6 * width)), fixed((1, (bias_rows - 6) * width)), fixed((width, 3 * width)),
        ],
        [
            shape_of((steps, 3, pairs, length, PAIR), bf16),
            shape_of((steps, 2 * here, length, length), bf16),
            shape_of((steps, here, length, PAIR), bf16),
            shape_of((steps, here, length, PAIR), f32),
            shape_of((8, 6 * width), f32),
            shape_of((1, (bias_rows - 6) * width), f32),
            shape_of((width, 3 * width), bf16),
        ],
        [pltpu.VMEM((width, 6 * width), f32), pltpu.VMEM((bias_rows, width), f32)],
        "project_attend", 20 * 10**9, args,
    )


def attend_last_body(flags, qkv, expo, att, inv):
    @pl.when(is_live(flags, pl.program_id(0)))
    def _():
        attend_pair(qkv, 0, expo, att, inv)


def attend_last(flags, qkv):
    steps, _, pairs, length, _ = qkv.shape

    def at(part):
        return lambda s, flags: (live_at(flags, s, 0, 1)[0],) + part

    part = pl.BlockSpec((1, 1, length, PAIR), at((0, 0, 0)))
    return call(
        attend_last_body,
        (steps,),
        [pl.BlockSpec((1, 3, 1, length, PAIR), at((0, pairs - 1, 0, 0)))],
        [pl.BlockSpec((1, 2, length, length), at((0, 0, 0))), part, part],
        [
            shape_of((steps, 2, length, length), bf16),
            shape_of((steps, 1, length, PAIR), bf16),
            shape_of((steps, 1, length, PAIR), f32),
        ],
        [],
        "attend_last", 10 * 10**9, (flags, qkv),
    )


def pack_chunk(flags, device, chunk, keep, send):
    place = jnp.bitwise_xor(flags[PLACE], chip_order(device >> 1, keep.shape[0]))

    @pl.when(flags[CORE] == (device & 1))
    def _():
        keep[place] = chunk[...]

    @pl.when(flags[CORE] != (device & 1))
    def _():
        send[place] = chunk[...].astype(bf16)


def feed_forward_body(
    flags, own_x, far_x, own_g, far_g, att_a, att_b, inv_a, inv_b, mod, bias, mine, other,
    own_out, far_out, grad_x1, grad_att, grad_mod, keep, send, bias_sum,
    x_s, g_s, w_out, w_up, w_down, sum_out, sum_up, sum_down_t, down_f32, chunk,
):
    slot = pl.program_id(0)
    step = pl.program_id(1)
    own, far, dead = kinds(flags, slot, pl.num_programs(0) - 1)
    width = x_s.shape[1]
    hidden_units = w_up.shape[1]
    ratio = hidden_units // width
    chips = mine.shape[0]
    rows = width // (2 * chips)

    @pl.when((slot == 0) & (step == 0))
    def _():
        for device, block in each_shard(flags, mine, other):
            place_columns(sum_out, device, block, 0, rows, 1, width)
            place_columns(sum_up, device, block, rows, rows, ratio, width)
            place_columns(
                down_f32, device, block, (1 + ratio) * rows, ratio * rows, 1, width
            )
        w_out[...] = sum_out[...].astype(bf16)
        w_up[...] = sum_up[...].astype(bf16)
        w_down[...] = down_f32[...].astype(bf16)
        for ref in (sum_out, sum_up, sum_down_t, bias_sum, chunk, grad_mod):
            ref[...] = jnp.zeros_like(ref)

    @pl.when(dead)
    def _():
        own_out[...] = jnp.zeros_like(own_out)

    @pl.when(own)
    def _():
        x_s[...] = own_x[0].astype(f32)
        g_s[...] = own_g[0].astype(f32)

    @pl.when(far)
    def _():
        x_s[...] = far_x[0].astype(f32)
        g_s[...] = far_g[0].astype(f32)

    @pl.when(is_live(flags, slot))
    def _():
        def vector(part):
            return mod[pl.ds(slot, 1), part * width : (part + 1) * width]

        gate1, shift2, scale2, gate2 = vector(2), vector(3), 1.0 + vector(4), vector(5)
        b_out = bias[:, :width]
        b_up = bias[:, width : width + hidden_units]
        b_down = bias[:, width + hidden_units :]

        def lanes(ref_a, ref_b):
            return jnp.concatenate([ref_a[0, p] for p in range(ref_a.shape[1])] + [ref_b[0, 0]], 1)

        attended = lanes(att_a, att_b)
        branch1 = dot(attended, w_out[...]) + b_out
        x1 = x_s[...] + gate1 * branch1
        normed2, rstd = norm(x1)
        h2 = (normed2 * scale2 + shift2).astype(bf16)
        pre = dot(h2, w_up[...]) + b_up
        cdf = 0.5 * (1.0 + lax.erf(pre * (1 / math.sqrt(2.0))))
        hidden = (pre * cdf).astype(bf16)
        slope = cdf + pre * jnp.exp2(pre * pre * (-0.5 * LOG2E)) * (1 / math.sqrt(2 * math.pi))
        branch2 = dot(hidden, w_down[...]) + b_down
        result = (x1 + gate2 * branch2).astype(bf16)

        @pl.when(own)
        def _():
            own_out[0] = result

        @pl.when(far)
        def _():
            far_out[0] = result

        grad = g_s[...]
        grad_b2 = (gate2 * grad).astype(bf16)
        grad_pre = (dot(grad_b2, w_down[...], 1, 1) * slope).astype(bf16)
        grad_h2 = dot(grad_pre, w_up[...], 1, 1)
        grad_n = grad_h2 * scale2
        g_x1 = grad + rstd * (
            grad_n
            - jnp.mean(grad_n, -1, keepdims=True)
            - normed2 * jnp.mean(grad_n * normed2, -1, keepdims=True)
        )
        grad_b1 = (gate1 * g_x1).astype(bf16)
        grad_x1[0] = g_x1
        g_att = (dot(grad_b1, w_out[...], 1, 1) * lanes(inv_a, inv_b)).astype(bf16)
        for p in range(width // PAIR):
            grad_att[0, p] = g_att[:, p * PAIR : (p + 1) * PAIR]

        def add_mod(part, value):
            grad_mod[pl.ds(slot, 1), part * width : (part + 1) * width] += row_sum(value)

        add_mod(0, g_x1 * branch1)
        add_mod(1, grad_h2)
        add_mod(2, grad_h2 * normed2)
        add_mod(3, grad * branch2)
        sum_out[...] += dot(attended, grad_b1, 0, 0)
        sum_up[...] += dot(h2, grad_pre, 0, 0)
        sum_down_t[...] += dot(grad_b2, hidden, 0, 0)
        bias_sum[:, :width] += row_sum(grad_b1.astype(f32))
        bias_sum[:, width : width + hidden_units] += row_sum(grad_pre.astype(f32))
        bias_sum[:, width + hidden_units :] += row_sum(grad_b2.astype(f32))

    @pl.when((slot == pl.num_programs(0) - 1) & (step == pl.num_programs(1) - 1))
    def _():
        down_f32[...] = sum_down_t[...].T
        for device in range(2 * chips):
            span = slice(device * rows, (device + 1) * rows)
            chunk[:rows] = sum_out[span]
            for part in range(ratio):
                chunk[(1 + part) * rows : (2 + part) * rows] = sum_up[
                    span, part * width : (part + 1) * width
                ]
            chunk[(1 + ratio) * rows : (1 + 2 * ratio) * rows] = down_f32[
                device * ratio * rows : (device + 1) * ratio * rows
            ]
            pack_chunk(flags, device, chunk, keep, send)


def feed_forward(
    flags, own_x, far_x, own_g, far_g, att_a, att_b, inv_a, inv_b, mod, bias, mine, other,
    hidden_units,
):
    steps, length, width = own_x.shape
    row_block = 512
    blocks = length // row_block
    chips = mine.shape[0]
    rows = width // (2 * chips)
    ratio = hidden_units // width
    packed_rows = up_to((1 + 2 * ratio) * rows, 16)

    def own(s, b, flags):
        return (own_slot(flags, s), jnp.where(s < flags[KEEP], b, blocks - 1), 0)

    def far(s, b, flags):
        keep = flags[KEEP]
        return (0, jnp.where(s < keep, 0, jnp.where(s == keep, b, blocks - 1)), 0)

    def live(s, b, flags):
        return live_at(flags, s, b, blocks) + (0,)

    def live_parts(s, b, flags):
        at, part = live_at(flags, s, b, blocks)
        return (at, 0, part, 0)

    def own_result(s, b, flags):
        own, _, dead = kinds(flags, s, steps)
        return (result_slot(flags, s, steps), jnp.where(own | dead, b, blocks - 1), 0)

    def block(where):
        return pl.BlockSpec((1, row_block, width), where)

    def parts(count):
        return pl.BlockSpec((1, count, row_block, PAIR), live_parts)

    pairs = width // PAIR
    args = (
        flags, own_x, far_x, own_g, far_g, att_a, att_b, inv_a, inv_b, mod, bias, mine, other,
    )
    return call(
        feed_forward_body,
        (steps + 1, blocks),
        [
            block(own), block(far), block(own), block(far),
            parts(pairs - 1), parts(1), parts(pairs - 1), parts(1),
        ] + [fixed(a.shape) for a in args[9:]],
        [
            block(own_result), block(far), block(live), parts(pairs),
            fixed((8, 4 * width)),
            fixed((chips, packed_rows, width)), fixed((chips, packed_rows, width)),
            fixed(bias.shape),
        ],
        [
            shape_of((steps, length, width), bf16),
            shape_of((1, length, width), bf16),
            shape_of((steps, length, width), f32),
            shape_of((steps, pairs, length, PAIR), bf16),
            shape_of((8, 4 * width), f32),
            shape_of((chips, packed_rows, width), f32),
            shape_of((chips, packed_rows, width), bf16),
            shape_of(bias.shape, f32),
        ],
        [
            pltpu.VMEM((row_block, width), f32),
            pltpu.VMEM((row_block, width), f32),
            pltpu.VMEM((width, width), bf16),
            pltpu.VMEM((width, hidden_units), bf16),
            pltpu.VMEM((hidden_units, width), bf16),
            pltpu.VMEM((width, width), f32),
            pltpu.VMEM((width, hidden_units), f32),
            pltpu.VMEM((width, hidden_units), f32),
            pltpu.VMEM((hidden_units, width), f32),
            pltpu.VMEM((packed_rows, width), f32),
        ],
        "feed_forward", 60 * 10**9, args,
    )


def attend_backward_body(flags, *refs):
    @pl.when(is_live(flags, pl.program_id(0)))
    def _():
        attend_backward_pair(*refs)


def attend_backward_pair(qkv, expo, att, grad_att, after, g_qkv, keys_t, values_t):
    length = att.shape[2]
    row_block = 512
    keys = qkv[0, 1, 0]
    values = qkv[0, 2, 0]
    values_ones = jnp.concatenate([values, jnp.ones_like(values)], 1)
    lane = lax.broadcasted_iota(jnp.int32, (row_block, PAIR), 1)
    first = lane < HEAD
    for i in range(length // row_block):
        r = pl.ds(i * row_block, row_block)
        query = qkv[0, 0, 0, r, :]
        g_att = grad_att[0, 0, r, :]
        product = g_att.astype(f32) * att[0, 0, r, :].astype(f32)
        query_t = query.T
        g_att_t = g_att.T
        grads_q = []
        for head in range(2):
            sel = first if head == 0 else jnp.logical_not(first)
            delta = jnp.sum(jnp.where(sel, product, 0.0), -1, keepdims=True)
            high = delta.astype(bf16).astype(f32)
            extra = jnp.where(
                lane == 0, -high, jnp.where(lane == 1, high - delta, 0.0)
            ).astype(bf16)
            left = jnp.concatenate([jnp.where(sel, g_att, jnp.zeros_like(g_att)), extra], 1)
            e = expo[0, head, r, :]
            grad_s = e * dot(left, values_ones, 1, 1).astype(bf16)
            grads_q.append(dot(grad_s, keys))
            span = slice(head * HEAD, (head + 1) * HEAD)
            add_k = dot(query_t[span], grad_s)
            add_v = dot(g_att_t[span], e)
            if i == 0:
                keys_t[span] = add_k
                values_t[span] = add_v
            else:
                keys_t[span] += add_k
                values_t[span] += add_v
        g_qkv[0, 0, r, :] = (jnp.where(first, grads_q[0], grads_q[1]) * 0.125).astype(bf16)
    g_qkv[0, 1] = (keys_t[...] * 0.125).astype(bf16).T
    g_qkv[0, 2] = values_t[...].astype(bf16).T


def attend_backward(flags, qkv, expo, att, grad_att, pair, part, after):
    steps, _, _, length, _ = qkv.shape

    def at(*part):
        return lambda s, flags: (live_at(flags, s, 0, 1)[0],) + part

    return call(
        attend_backward_body,
        (steps,),
        [
            pl.BlockSpec((1, 3, 1, length, PAIR), at(0, pair, 0, 0)),
            pl.BlockSpec((1, 2, length, length), at(part, 0, 0)),
            pl.BlockSpec((1, 1, length, PAIR), at(part, 0, 0)),
            pl.BlockSpec((1, 1, length, PAIR), at(pair, 0, 0)),
            anywhere,
        ],
        pl.BlockSpec((1, 3, length, PAIR), at(0, 0, 0)),
        shape_of((steps, 3, length, PAIR), bf16),
        [pltpu.VMEM((PAIR, length), f32), pltpu.VMEM((PAIR, length), f32)],
        "attend_backward", 20 * 10**9, (flags, qkv, expo, att, grad_att, after),
    )


def finish_body(
    flags, own_x, far_x, grad_x1, mod, w_qkv, after, *refs
):
    pairs = own_x.shape[2] // PAIR
    g_parts = refs[:pairs]
    own_grad, far_grad, grad_mod, keep, send, sum_qkv, chunk = refs[pairs:]
    slot = pl.program_id(0)
    step = pl.program_id(1)
    own, far, dead = kinds(flags, slot, pl.num_programs(0) - 1)
    width = own_x.shape[2]
    chips = keep.shape[0]
    rows = width // (2 * chips)

    @pl.when((slot == 0) & (step == 0))
    def _():
        for ref in (sum_qkv, chunk, grad_mod):
            ref[...] = jnp.zeros_like(ref)

    @pl.when(dead)
    def _():
        own_grad[...] = jnp.zeros_like(own_grad)

    def finish(x_ref, out_ref):
        shift = mod[pl.ds(slot, 1), :width]
        scale = 1.0 + mod[pl.ds(slot, 1), width : 2 * width]
        normed, rstd = norm(x_ref[0].astype(f32))
        h1 = (normed * scale + shift).astype(bf16)
        grad = jnp.concatenate([ref[0, kind] for kind in range(3) for ref in g_parts], 1)
        grad_h1 = dot(grad, w_qkv[...], 1, 1)
        sum_qkv[...] += dot(h1, grad, 0, 0)
        grad_mod[pl.ds(slot, 1), :width] += row_sum(grad_h1)
        grad_mod[pl.ds(slot, 1), width:] += row_sum(grad_h1 * normed)
        grad_n = grad_h1 * scale
        out_ref[0] = (
            grad_x1[0]
            + rstd
            * (
                grad_n
                - jnp.mean(grad_n, -1, keepdims=True)
                - normed * jnp.mean(grad_n * normed, -1, keepdims=True)
            )
        ).astype(out_ref.dtype)

    @pl.when(own)
    def _():
        finish(own_x, own_grad)

    @pl.when(far)
    def _():
        finish(far_x, far_grad)

    @pl.when((slot == pl.num_programs(0) - 1) & (step == pl.num_programs(1) - 1))
    def _():
        for device in range(2 * chips):
            for part in range(3):
                chunk[part * rows : (part + 1) * rows] = sum_qkv[
                    device * rows : (device + 1) * rows, part * width : (part + 1) * width
                ]
            pack_chunk(flags, device, chunk, keep, send)


def finish(flags, own_x, far_x, grad_x1, mod, w_qkv, after, g_parts, chips):
    steps, length, width = own_x.shape
    row_block = 512
    blocks = length // row_block
    packed_rows = up_to(3 * width // (2 * chips), 8)

    def own(s, b, flags):
        return (own_slot(flags, s), jnp.where(s < flags[KEEP], b, blocks - 1), 0)

    def far(s, b, flags):
        keep = flags[KEEP]
        return (0, jnp.where(s < keep, 0, jnp.where(s == keep, b, blocks - 1)), 0)

    def live(s, b, flags):
        return live_at(flags, s, b, blocks) + (0,)

    def live_parts(s, b, flags):
        at, part = live_at(flags, s, b, blocks)
        return (at, 0, part, 0)

    def own_result(s, b, flags):
        own, _, dead = kinds(flags, s, steps)
        return (result_slot(flags, s, steps), jnp.where(own | dead, b, blocks - 1), 0)

    def block(where):
        return pl.BlockSpec((1, row_block, width), where)

    return call(
        finish_body,
        (steps + 1, blocks),
        [block(own), block(far), block(live), fixed(mod.shape), fixed(w_qkv.shape), anywhere]
        + [pl.BlockSpec((1, 3, row_block, PAIR), live_parts) for _ in g_parts],
        [
            block(own_result), block(far), fixed((8, 2 * width)),
            fixed((chips, packed_rows, width)), fixed((chips, packed_rows, width)),
        ],
        [
            shape_of((steps, length, width), f32),
            shape_of((1, length, width), bf16),
            shape_of((8, 2 * width), f32),
            shape_of((chips, packed_rows, width), f32),
            shape_of((chips, packed_rows, width), bf16),
        ],
        [pltpu.VMEM((width, 3 * width), f32), pltpu.VMEM((packed_rows, width), f32)],
        "finish", 10 * 10**9,
        (flags, own_x, far_x, grad_x1, mod, w_qkv, after, *g_parts),
    )


def swap(array, mask):
    count = lax.axis_size("dp")
    return lax.ppermute(array, "dp", [(i, i ^ mask) for i in range(count)])


def tie(value, *others):
    return lax.optimization_barrier((value,) + others)[0]


def chip_groups(chips):
    bits = chips.bit_length() - 1
    return tuple(tuple(range(max(top - 2, 0), top)) for top in range(bits, 0, -2))


def chip_order(chip, chips):
    place, low = 0, 0
    for group in chip_groups(chips):
        place = place | ((chip >> group[0]) & ((1 << len(group)) - 1)) << low
        low += len(group)
    return place


def group_masks(group):
    return [sum(((k >> i) & 1) << b for i, b in enumerate(group)) for k in range(1, 1 << len(group))]


def gather_group(held, group, chip, after=None):
    size = 1 << len(group)
    place = (chip >> group[0]) & (size - 1)
    pieces = [held] + [swap(held, mask << 1) for mask in group_masks(group)]
    if after is not None:
        pieces = lax.optimization_barrier(tuple(pieces) + (after,))[:-1]
    joined = jnp.zeros((size,) + held.shape, held.dtype)
    for k, piece in enumerate(pieces):
        joined = lax.dynamic_update_index_in_dim(joined, piece, place ^ k, 0)
    return joined.reshape((-1,) + held.shape[1:])


def reduce_group(group, sums, notes):
    masks = group_masks(group)
    width = sums[0].shape[-1]
    parts = [held.shape[0] // (len(masks) + 1) for held in sums]
    totals = [held[:part] for held, part in zip(sums, parts)]
    joined = [[note] for note in notes]
    for k, mask in enumerate(masks):
        pieces = [held[(k + 1) * n : (k + 2) * n].astype(bf16) for held, n in zip(sums, parts)]
        pieces += notes
        got = swap(jnp.concatenate([p.reshape(-1, width) for p in pieces], 0), mask << 1)
        start = 0
        for i, piece in enumerate(pieces):
            size = math.prod(piece.shape[:-1])
            block = got[start : start + size].reshape(piece.shape)
            start += size
            if i < len(sums):
                totals[i] = totals[i] + block.astype(f32)
            else:
                joined[i - len(sums)].append(block)
    return totals, [jnp.concatenate(blocks, 0) for blocks in joined]


def body(
    fields, conditions, step_counts, cotangent,
    w_ada, b_ada, w_qkv, w_out, b_out, w_up, b_up, w_down, b_down,
):
    devices = lax.axis_size("dp")
    chips = devices // 2
    me = lax.axis_index("dp").astype(jnp.int32)
    chip, core = me >> 1, me & 1
    steps, length, width = fields.shape[1:]
    hidden_units = w_up.shape[1]
    ratio = hidden_units // width
    rows = width // devices
    fields, conditions, cotangent = fields[0], conditions[0], cotangent[0]
    groups = chip_groups(chips)

    place = chip_order(chip, chips)
    here = jnp.stack([me, me, place, core, me])
    biases = jnp.concatenate([b_ada, b_out, b_up, b_down])[None]
    first, second = pack_shards(here, w_ada, w_qkv, w_out, w_up, w_down, biases)
    mine_a = first[None]
    stages = []
    for group in groups:
        mine_a = gather_group(mine_a, group, chip)
        stages.append(mine_a)
    mine_b = second[None]
    for i, group in enumerate(groups[:-1]):
        mine_b = gather_group(tie(mine_b, stages[i]), group, chip)

    count = step_counts[0]
    head = jnp.concatenate([conditions, jnp.full((4, width), count, bf16)], 0)
    other_head = swap(tie(head, first), 1)
    other_count = other_head[steps, 0].astype(jnp.int32)
    give = count - other_count >= 2
    take = (other_count - count >= 2).astype(jnp.int32)
    keep = count - give.astype(jnp.int32)
    flags = jnp.stack([keep, take, place, core, me])
    late_fields, late_cotangent = tie(fields, stages[0]), tie(cotangent, stages[0])
    far_x = swap(lax.dynamic_index_in_dim(late_fields, count - 1, 0), 1)
    far_g = swap(lax.dynamic_index_in_dim(late_cotangent, count - 1, 0), 1)
    far_cond = lax.dynamic_index_in_dim(other_head, other_count - 1, 0)
    cond = jnp.concatenate([conditions, jnp.zeros((8 - steps, width), bf16)], 0)
    cond = jnp.where((jnp.arange(8) == keep)[:, None] & (take > 0), far_cond, cond)
    cond_act = jax.nn.silu(cond.astype(f32)).astype(bf16)

    other_a = swap(tie(mine_a, mine_b, far_x, far_g, cond_act, flags), 1)
    mine_b = tie(mine_b, mine_a)
    qkv, expo_a, att_a, inv_a, mod, bias, full_qkv = project_attend(
        flags, fields, far_x, cond_act, mine_a, other_a, 8 + ratio
    )
    mine_b = gather_group(mine_b, groups[-1], chip, mod)
    other_b = swap(mine_b, 1)
    expo_b, att_b, inv_b = attend_last(tie(flags, mine_b), qkv)
    own_out, far_out, grad_x1, grad_att, grad_mod2, keep2, send2, bias_sum = feed_forward(
        flags, fields, far_x, cotangent, far_g, att_a, att_b, inv_a, inv_b, mod, bias,
        mine_b, other_b, hidden_units,
    )

    held2 = keep2 + swap(send2, 1).astype(f32)
    note2 = jnp.concatenate(
        [grad_mod2[:steps].reshape(-1, width), bias_sum.reshape(-1, width), cond_act[:steps]], 0
    ).astype(bf16)
    note2 = jnp.concatenate([note2, jnp.zeros((-note2.shape[0] % 8, width), bf16)], 0)[None]
    back_out = swap(far_out, 1)
    down_groups = tuple(reversed(groups))
    pairs = width // PAIR
    early, late = down_groups[: pairs - 1], down_groups[pairs - 1 :]
    after = [keep2]
    for group in early:
        after.append(held2)
        (held2,), (note2,) = reduce_group(group, [held2], [tie(note2, held2)])
    g_parts = []
    for pair in range(pairs):
        last = pair == pairs - 1
        g_parts.append(
            attend_backward(
                flags, qkv, expo_b if last else expo_a, att_b if last else att_a,
                grad_att, pair, 0 if last else pair, after[pair],
            )
        )
    own_grad, far_grad, grad_mod1, keep1, send1 = finish(
        flags, fields, far_x, grad_x1, mod, full_qkv, held2, g_parts, chips
    )
    held1 = keep1 + swap(send1, 1).astype(f32)
    back_grad = swap(far_grad, 1).astype(f32)
    note1 = grad_mod1[:steps].astype(bf16).reshape(1, -1, width)
    for group in early:
        (held1,), (note1,) = reduce_group(group, [held1], [tie(note1, held1)])
    for group in late:
        (held1, held2), (note1, note2) = reduce_group(group, [held1, held2], [note1, note2])
    sums1, sums2 = held1[0], held2[0]
    notes = jnp.concatenate([note1, note2], 1)
    notes = jnp.concatenate([notes, swap(notes, 1)], 0)
    note1, note2 = notes[:, : note1.shape[1]], notes[:, note1.shape[1] :]

    mod1 = note1.reshape(-1, 2 * width)
    mod2 = note2[:, : 4 * steps].reshape(-1, 4 * width)
    all_mod = jnp.concatenate([mod1, mod2], 1)
    bias_rows = 2 + ratio
    all_bias = jnp.sum(note2[:, 4 * steps : 4 * steps + bias_rows].astype(f32), 0).reshape(-1)
    all_cond = note2[:, 4 * steps + bias_rows : 5 * steps + bias_rows].reshape(-1, width)
    own_cond = lax.dynamic_slice_in_dim(all_cond, me * rows, rows, 1)
    grad_ada = jnp.einsum("sm,sn->mn", own_cond, all_mod, preferred_element_type=f32)
    sum_ada = jnp.sum(all_mod.astype(f32), 0)

    def own_part(vector):
        size = vector.shape[0] // devices
        return lax.dynamic_slice_in_dim(vector, me * size, size, 0)

    def put_back(array, back):
        now = lax.optimization_barrier(lax.dynamic_index_in_dim(array, count - 1, 0))
        return lax.dynamic_update_index_in_dim(array, jnp.where(give, back, now), count - 1, 0)

    def from_columns(block, start, parts):
        return jnp.concatenate(
            [block[start + i * rows : start + (i + 1) * rows] for i in range(parts)], 1
        )

    return (
        put_back(own_out, back_out)[None],
        put_back(own_grad, back_grad)[None],
        grad_ada,
        own_part(sum_ada),
        from_columns(sums1, 0, 3),
        sums2[:rows],
        own_part(all_bias[:width]),
        from_columns(sums2, rows, ratio),
        own_part(all_bias[width : width + hidden_units]),
        sums2[(1 + ratio) * rows : (1 + 2 * ratio) * rows],
        own_part(all_bias[width + hidden_units :]),
    )


def solution(mesh):
    item, matrix, vector = P("dp", None, None, None), P("dp", None), P("dp")
    return jax.shard_map(
        body,
        mesh=mesh,
        in_specs=(
            item, P("dp", None, None), vector, item,
            matrix, vector, matrix, matrix, vector, matrix, vector, matrix, vector,
        ),
        out_specs=(
            item, item, matrix, vector, matrix, matrix, vector, matrix, vector, matrix, vector,
        ),
        check_vma=False,
    )
```

```python
import functools
import math

import jax
import jax.numpy as jnp
from jax import lax
from jax.experimental import pallas as pl
from jax.experimental.pallas import tpu as pltpu
from jax.sharding import PartitionSpec as P

HEAD = 64
PAIR = 2 * HEAD
EPS = 1e-6
LOG2E = 1.4426950408889634
VMEM_LIMIT = 60 * 2**20
bf16 = jnp.bfloat16
f32 = jnp.float32
shape_of = jax.ShapeDtypeStruct


def dot(left, right, left_dim=1, right_dim=0):
    return lax.dot_general(
        left, right, (((left_dim,), (right_dim,)), ((), ())), preferred_element_type=f32
    )


def norm(value):
    mean = jnp.mean(value, -1, keepdims=True)
    cent = value - mean
    var = jnp.mean(cent * cent, -1, keepdims=True)
    rstd = lax.rsqrt(var + EPS)
    return cent * rstd, rstd


def row_sum(value):
    return jnp.sum(value, 0, keepdims=True)


def up_to(value, unit):
    return -(-value // unit) * unit


def call(body, grid, in_specs, out_specs, out_shape, scratch, name, flops, args):
    return pl.pallas_call(
        body,
        grid_spec=pltpu.PrefetchScalarGridSpec(
            num_scalar_prefetch=1,
            grid=grid,
            in_specs=in_specs,
            out_specs=out_specs,
            scratch_shapes=scratch,
        ),
        out_shape=out_shape,
        compiler_params=pltpu.CompilerParams(vmem_limit_bytes=VMEM_LIMIT),
        cost_estimate=pl.CostEstimate(flops=flops, bytes_accessed=10**7, transcendentals=0),
        name=name,
    )(*args)


anywhere = pl.BlockSpec(memory_space=pl.ANY)


def fetch(pieces, dest, sems):
    copies = [pltpu.make_async_copy(p, dest.at[k], sems.at[k]) for k, p in enumerate(pieces)]
    for copy in copies:
        copy.start()
    for copy in copies:
        copy.wait()


def fixed(shape):
    return pl.BlockSpec(shape, lambda *at: (0,) * len(shape))


KEEP, TAKE, PLACE, CORE = range(4)


def own_slot(flags, slot):
    return jnp.minimum(slot, flags[KEEP] - 1)


def is_live(flags, slot):
    return slot < flags[KEEP] + flags[TAKE]


def live_at(flags, slot, block, blocks):
    live = flags[KEEP] + flags[TAKE]
    return jnp.minimum(slot, live - 1), jnp.where(slot < live, block, blocks - 1)


def result_slot(flags, slot, steps):
    after = jnp.clip(slot - flags[TAKE], flags[KEEP] - 1, steps - 1)
    return jnp.where(slot < flags[KEEP], slot, after)


def kinds(flags, slot, steps):
    own = slot < flags[KEEP]
    far = (slot == flags[KEEP]) & (flags[TAKE] > 0)
    return own, far, jnp.logical_not(own | far) & (slot - flags[TAKE] < steps)


def pack_body(ada, qkv, out, up, down, bias, first, second, first_s, second_s):
    rows, width = out.shape
    me = lax.axis_index("dp").astype(jnp.int32)
    first_s[...] = jnp.zeros_like(first_s)
    second_s[...] = jnp.zeros_like(second_s)

    def put(dest, start, ref):
        for part in range(ref.shape[1] // width):
            dest[start + part * rows : start + (part + 1) * rows] = ref[
                :, part * width : (part + 1) * width
            ].astype(f32)

    put(first_s, 0, ada)
    put(first_s, 6 * rows, qkv)
    put(second_s, 0, out)
    put(second_s, rows, up)
    after = rows + up.shape[1] * rows // width
    second_s[after : after + down.shape[0]] = down[...].astype(f32)
    source = lax.broadcasted_iota(jnp.int32, (bias.shape[1], width), 0)
    lane = lax.broadcasted_iota(jnp.int32, (bias.shape[1], width), 1)
    start = 0
    for i, count in enumerate((6 * rows, rows, up.shape[1] * rows // width, rows)):
        at = lax.rem(me * count, width) + source - start
        at = jnp.where(at >= width, at - width, at)
        hit = (source >= start) & (source < start + count) & (at == lane)
        first_s[9 * rows + i : 9 * rows + i + 1] = dot(bias[...], jnp.where(hit, 1.0, 0.0).astype(bf16))
        start += count
    first[...] = first_s[...].astype(bf16)
    second[...] = second_s[...].astype(bf16)


def pack_shards(*args):
    _, _, out, up, down, _ = args
    rows, width = out.shape
    sizes = (up_to(9 * rows + 4, 16), up_to(rows + up.shape[1] * rows // width + down.shape[0] + 4, 16))
    return pl.pallas_call(
        pack_body,
        out_shape=[shape_of((n, width), bf16) for n in sizes],
        scratch_shapes=[pltpu.VMEM((n, width), f32) for n in sizes],
        name="pack_shards",
    )(*args)


def each_shard(flags, chips, blocks_of):
    first = flags[CORE] == 0
    for chip in range(chips):
        mine, other = blocks_of(jnp.bitwise_xor(flags[PLACE], chip_order(chip, chips)))
        mine, other = mine.astype(f32), other.astype(f32)
        yield 2 * chip, jnp.where(first, mine, other)
        yield 2 * chip + 1, jnp.where(first, other, mine)


def place_columns(dest, device, block, start, rows, count, width):
    for part in range(count):
        dest[device * rows : (device + 1) * rows, part * width : (part + 1) * width] = block[
            start + part * rows : start + (part + 1) * rows
        ]


def attend_pair(qkv, pair, expo, att, inv):
    length = att.shape[-2]
    row_block = 256
    keys = qkv[0, 1, pair]
    values = qkv[0, 2, pair]
    values_ones = jnp.concatenate([values, jnp.ones_like(values)], 1)
    first = lax.broadcasted_iota(jnp.int32, (row_block, PAIR), 1) < HEAD
    for i in range(length // row_block):
        r = pl.ds(i * row_block, row_block)
        query = qkv[0, 0, pair, r, :]
        outs = []
        for head in range(2):
            sel = first if head == 0 else jnp.logical_not(first)
            scores = dot(jnp.where(sel, query, jnp.zeros_like(query)), keys, 1, 1)
            top = jnp.max(scores, -1, keepdims=True)
            e = jnp.exp2((scores - top) * (0.125 * LOG2E)).astype(bf16)
            expo[0, head, r, :] = e
            outs.append(dot(e, values_ones))
        out = jnp.where(first, outs[0][:, :PAIR], outs[1][:, :PAIR])
        inverse = 1.0 / jnp.where(first, outs[0][:, PAIR:], outs[1][:, PAIR:])
        att[0, 0, r, :] = (out * inverse).astype(bf16)
        inv[0, 0, r, :] = inverse


def attend_forward_body(flags, own_x, far_x, cond, *refs):
    pieces = refs[:-11]
    qkv, expo, att, inv, mod, bias, w_qkv, w_f32, bias_f32, shards, sems = refs[-11:]
    slot = pl.program_id(0)
    pair = pl.program_id(1)
    length, width = own_x.shape[1:]
    group, others = shards.shape[1:3]
    chips = group * others
    rows = width // (2 * chips)
    pairs = width // PAIR

    def blocks_of(place):
        at = lax.div(place, others), lax.rem(place, others)
        return shards[(0, *at)], shards[(1, *at)]

    @pl.when((slot == 0) & (pair == 0))
    def _():
        fetch(pieces[:group], shards.at[0], sems.at[0])
        fetch(pieces[group:], shards.at[1], sems.at[1])
        bias_f32[...] = jnp.zeros_like(bias_f32)
        lane = lax.broadcasted_iota(jnp.int32, (1, width), 1)
        for device, block in each_shard(flags, chips, blocks_of):
            place_columns(w_f32, device, block, 0, rows, 6, width)
            start = 0
            for i, count in enumerate((6 * rows, rows, bias_f32.shape[0] * rows - 8 * rows, rows)):
                low, high = device * count, (device + 1) * count
                for part in range(low // width, (high - 1) // width + 1):
                    at = lane + part * width
                    bias_f32[start + part : start + part + 1] += jnp.where(
                        (at >= low) & (at < high), block[9 * rows + i : 9 * rows + i + 1], 0.0
                    )
                start += 2 * chips * count // width
        for part in range(6):
            cols = slice(part * width, (part + 1) * width)
            mod[:, cols] = dot(cond[...], w_f32[:, cols].astype(bf16)) + bias_f32[part : part + 1]
        for part in range(bias_f32.shape[0] - 6):
            bias[:, part * width : (part + 1) * width] = bias_f32[6 + part : 7 + part]
        for device, block in each_shard(flags, chips, blocks_of):
            place_columns(w_f32, device, block, 6 * rows, rows, 3, width)
        w_qkv[...] = w_f32[:, : 3 * width].astype(bf16)

    @pl.when((pair == 0) & is_live(flags, slot))
    def _():
        shift = mod[pl.ds(slot, 1), :width]
        scale = 1.0 + mod[pl.ds(slot, 1), width : 2 * width]
        row_block = 256

        def project(ref):
            @pl.loop(0, length // row_block)
            def _(i):
                r = pl.ds(pl.multiple_of(i * row_block, row_block), row_block)
                normed, _ = norm(ref[0, r, :].astype(f32))
                h1 = (normed * scale + shift).astype(bf16)
                result = dot(h1, w_qkv[...]).astype(bf16)
                for kind in range(3):
                    for p in range(pairs):
                        at = kind * width + p * PAIR
                        qkv[0, kind, p, r, :] = result[:, at : at + PAIR]

        @pl.when(slot < flags[KEEP])
        def _():
            project(own_x)

        @pl.when(slot >= flags[KEEP])
        def _():
            project(far_x)

    @pl.when(is_live(flags, slot))
    def _():
        attend_pair(qkv, pair, expo, att, inv)


def attend_forward(flags, own_x, far_x, cond, mine, other, bias_rows):
    steps, length, width = own_x.shape
    pairs = width // PAIR
    shards_shape = (2, len(mine)) + mine[0].shape
    args = (flags, own_x, far_x, cond, *mine, *other)

    def at(s, p, flags):
        return live_at(flags, s, p, pairs) + (0, 0)

    whole = pl.BlockSpec((1, 3, pairs, length, PAIR), lambda s, p, flags: (at(s, p, flags)[0], 0, 0, 0, 0))
    part = pl.BlockSpec((1, 1, length, PAIR), at)
    return call(
        attend_forward_body,
        (steps, pairs),
        [
            pl.BlockSpec((1, length, width), lambda s, p, flags: (own_slot(flags, s), 0, 0)),
            fixed(far_x.shape), fixed(cond.shape),
        ] + [anywhere] * (2 * len(mine)),
        [
            whole,
            pl.BlockSpec((1, 2, length, length), at),
            part, part,
            fixed((8, 6 * width)), fixed((1, (bias_rows - 6) * width)), fixed((width, 3 * width)),
        ],
        [
            shape_of((steps, 3, pairs, length, PAIR), bf16),
            shape_of((steps, 2 * pairs, length, length), bf16),
            shape_of((steps, pairs, length, PAIR), bf16),
            shape_of((steps, pairs, length, PAIR), f32),
            shape_of((8, 6 * width), f32),
            shape_of((1, (bias_rows - 6) * width), f32),
            shape_of((width, 3 * width), bf16),
        ],
        [
            pltpu.VMEM((width, 6 * width), f32),
            pltpu.VMEM((bias_rows, width), f32),
            pltpu.VMEM(shards_shape, bf16),
            pltpu.SemaphoreType.DMA((2, len(mine))),
        ],
        "attend_forward", 30 * 10**9, args,
    )


def pack_chunk(flags, device, chunk, keep, send):
    place = jnp.bitwise_xor(flags[PLACE], chip_order(device >> 1, keep.shape[0]))

    @pl.when(flags[CORE] == (device & 1))
    def _():
        keep[place] = chunk[...]

    @pl.when(flags[CORE] != (device & 1))
    def _():
        send[place] = chunk[...].astype(bf16)


def feed_forward_body(
    steps, flags, own_x, far_x, own_g, far_g, att, inv, mod, bias, *refs
):
    (
        own_out, far_out, grad_x1, grad_att, note, keep, send,
        x_s, g_s, w_out, w_up, w_down, sum_out, sum_up, sum_down_t, down_f32, chunk, bias_sum,
        grad_mod, note_s, shards, sems,
    ) = refs[-22:]
    pieces = refs[:-22]
    slot = pl.program_id(0)
    step = pl.program_id(1)
    own, far, dead = kinds(flags, slot, pl.num_programs(0) - 1)
    width = x_s.shape[1]
    hidden_units = w_up.shape[1]
    ratio = hidden_units // width
    group, _, others = shards.shape[:3]
    chips = group * others
    rows = width // (2 * chips)

    def blocks_of(place):
        part, place = lax.div(place, others), lax.rem(place, others)
        return shards[part, 0, place], shards[part, 1, place]

    @pl.when((slot == 0) & (step == 0))
    def _():
        fetch(pieces, shards, sems)
        for device, block in each_shard(flags, chips, blocks_of):
            place_columns(sum_out, device, block, 0, rows, 1, width)
            place_columns(sum_up, device, block, rows, rows, ratio, width)
            place_columns(
                down_f32, device, block, (1 + ratio) * rows, ratio * rows, 1, width
            )
        w_out[...] = sum_out[...].astype(bf16)
        w_up[...] = sum_up[...].astype(bf16)
        w_down[...] = down_f32[...].astype(bf16)
        for ref in (sum_out, sum_up, sum_down_t, bias_sum, chunk, grad_mod):
            ref[...] = jnp.zeros_like(ref)

    @pl.when(dead)
    def _():
        own_out[...] = jnp.zeros_like(own_out)

    @pl.when(own)
    def _():
        x_s[...] = own_x[0].astype(f32)
        g_s[...] = own_g[0].astype(f32)

    @pl.when(far)
    def _():
        x_s[...] = far_x[0].astype(f32)
        g_s[...] = far_g[0].astype(f32)

    @pl.when(is_live(flags, slot))
    def _():
        def vector(part):
            return mod[pl.ds(slot, 1), part * width : (part + 1) * width]

        gate1, shift2, scale2, gate2 = vector(2), vector(3), 1.0 + vector(4), vector(5)
        b_out = bias[:, :width]
        b_up = bias[:, width : width + hidden_units]
        b_down = bias[:, width + hidden_units :]

        def lanes(ref):
            return jnp.concatenate([ref[0, p] for p in range(ref.shape[1])], 1)

        attended = lanes(att)
        branch1 = dot(attended, w_out[...]) + b_out
        x1 = x_s[...] + gate1 * branch1
        normed2, rstd = norm(x1)
        h2 = (normed2 * scale2 + shift2).astype(bf16)
        pre = dot(h2, w_up[...]) + b_up
        cdf = 0.5 * (1.0 + lax.erf(pre * (1 / math.sqrt(2.0))))
        hidden = (pre * cdf).astype(bf16)
        slope = cdf + pre * jnp.exp2(pre * pre * (-0.5 * LOG2E)) * (1 / math.sqrt(2 * math.pi))
        branch2 = dot(hidden, w_down[...]) + b_down
        result = (x1 + gate2 * branch2).astype(bf16)

        @pl.when(own)
        def _():
            own_out[0] = result

        @pl.when(far)
        def _():
            far_out[0] = result

        grad = g_s[...]
        grad_b2 = (gate2 * grad).astype(bf16)
        grad_pre = (dot(grad_b2, w_down[...], 1, 1) * slope).astype(bf16)
        grad_h2 = dot(grad_pre, w_up[...], 1, 1)
        grad_n = grad_h2 * scale2
        g_x1 = grad + rstd * (
            grad_n
            - jnp.mean(grad_n, -1, keepdims=True)
            - normed2 * jnp.mean(grad_n * normed2, -1, keepdims=True)
        )
        grad_b1 = (gate1 * g_x1).astype(bf16)
        grad_x1[0] = g_x1
        g_att = (dot(grad_b1, w_out[...], 1, 1) * lanes(inv)).astype(bf16)
        for p in range(width // PAIR):
            grad_att[0, p] = g_att[:, p * PAIR : (p + 1) * PAIR]

        def add_mod(part, value):
            grad_mod[pl.ds(slot, 1), part * width : (part + 1) * width] += row_sum(value)

        add_mod(0, g_x1 * branch1)
        add_mod(1, grad_h2)
        add_mod(2, grad_h2 * normed2)
        add_mod(3, grad * branch2)
        sum_out[...] += dot(attended, grad_b1, 0, 0)
        sum_up[...] += dot(h2, grad_pre, 0, 0)
        sum_down_t[...] += dot(grad_b2, hidden, 0, 0)
        bias_sum[:, :width] += row_sum(grad_b1.astype(f32))
        bias_sum[:, width : width + hidden_units] += row_sum(grad_pre.astype(f32))
        bias_sum[:, width + hidden_units :] += row_sum(grad_b2.astype(f32))

    @pl.when((slot == pl.num_programs(0) - 1) & (step == pl.num_programs(1) - 1))
    def _():
        down_f32[...] = sum_down_t[...].T
        for device in range(2 * chips):
            span = slice(device * rows, (device + 1) * rows)
            chunk[:rows] = sum_out[span]
            for part in range(ratio):
                chunk[(1 + part) * rows : (2 + part) * rows] = sum_up[
                    span, part * width : (part + 1) * width
                ]
            chunk[(1 + ratio) * rows : (1 + 2 * ratio) * rows] = down_f32[
                device * ratio * rows : (device + 1) * ratio * rows
            ]
            up_row = 1 + device * ratio * rows // width
            for i, part in enumerate((0, up_row, 1 + ratio)):
                at = (1 + 2 * ratio) * rows + i
                chunk[at : at + 1] = bias_sum[:, part * width : (part + 1) * width]
            pack_chunk(flags, device, chunk, keep, send)
        note_s[...] = jnp.zeros_like(note_s)
        for row in range(4 * steps):
            part = row % 4
            note_s[row : row + 1] = grad_mod[
                row // 4 : row // 4 + 1, part * width : (part + 1) * width
            ]
        note[...] = note_s[...].astype(bf16)


def feed_forward(
    flags, own_x, far_x, own_g, far_g, att, inv, mod, bias, shards, hidden_units
):
    steps, length, width = own_x.shape
    row_block = 512
    blocks = length // row_block
    group, others = len(shards), shards[0].shape[1]
    rows = width // (2 * group * others)
    ratio = hidden_units // width
    packed_rows = up_to((1 + 2 * ratio) * rows + 3, 16)
    sum_shape = (group * others, packed_rows, width)
    note_shape = (up_to(4 * steps, 16), width)

    def own(s, b, flags):
        return (own_slot(flags, s), jnp.where(s < flags[KEEP], b, blocks - 1), 0)

    def far(s, b, flags):
        keep = flags[KEEP]
        return (0, jnp.where(s < keep, 0, jnp.where(s == keep, b, blocks - 1)), 0)

    def live(s, b, flags):
        return live_at(flags, s, b, blocks) + (0,)

    def live_parts(s, b, flags):
        at, part = live_at(flags, s, b, blocks)
        return (at, 0, part, 0)

    def own_result(s, b, flags):
        own, _, dead = kinds(flags, s, steps)
        return (result_slot(flags, s, steps), jnp.where(own | dead, b, blocks - 1), 0)

    def block(where):
        return pl.BlockSpec((1, row_block, width), where)

    def parts(count):
        return pl.BlockSpec((1, count, row_block, PAIR), live_parts)

    pairs = width // PAIR
    args = (flags, own_x, far_x, own_g, far_g, att, inv, mod, bias, *shards)
    return call(
        functools.partial(feed_forward_body, steps),
        (steps + 1, blocks),
        [
            block(own), block(far), block(own), block(far), parts(pairs), parts(pairs),
            fixed(mod.shape), fixed(bias.shape),
        ] + [anywhere] * group,
        [
            block(own_result), block(far), block(live), parts(pairs),
            fixed(note_shape), fixed(sum_shape), fixed(sum_shape),
        ],
        [
            shape_of((steps, length, width), bf16),
            shape_of((1, length, width), bf16),
            shape_of((steps, length, width), f32),
            shape_of((steps, pairs, length, PAIR), bf16),
            shape_of(note_shape, bf16),
            shape_of(sum_shape, f32),
            shape_of(sum_shape, bf16),
        ],
        [
            pltpu.VMEM((row_block, width), f32),
            pltpu.VMEM((row_block, width), f32),
            pltpu.VMEM((width, width), bf16),
            pltpu.VMEM((width, hidden_units), bf16),
            pltpu.VMEM((hidden_units, width), bf16),
            pltpu.VMEM((width, width), f32),
            pltpu.VMEM((width, hidden_units), f32),
            pltpu.VMEM((width, hidden_units), f32),
            pltpu.VMEM((hidden_units, width), f32),
            pltpu.VMEM((packed_rows, width), f32),
            pltpu.VMEM(bias.shape, f32),
            pltpu.VMEM((8, 4 * width), f32),
            pltpu.VMEM(note_shape, f32),
            pltpu.VMEM((group,) + shards[0].shape, bf16),
            pltpu.SemaphoreType.DMA((group,)),
        ],
        "feed_forward", 60 * 10**9, args,
    )


def attend_backward_pair(qkv, expo, att, grad_att, g_qkv, keys_t, values_t):
    length = att.shape[2]
    row_block = 512
    keys = qkv[0, 1, 0]
    values = qkv[0, 2, 0]
    values_ones = jnp.concatenate([values, jnp.ones_like(values)], 1)
    lane = lax.broadcasted_iota(jnp.int32, (row_block, PAIR), 1)
    first = lane < HEAD
    for i in range(length // row_block):
        r = pl.ds(i * row_block, row_block)
        query = qkv[0, 0, 0, r, :]
        g_att = grad_att[0, 0, r, :]
        product = g_att.astype(f32) * att[0, 0, r, :].astype(f32)
        query_t = query.T
        g_att_t = g_att.T
        grads_q = []
        for head in range(2):
            sel = first if head == 0 else jnp.logical_not(first)
            delta = jnp.sum(jnp.where(sel, product, 0.0), -1, keepdims=True)
            high = delta.astype(bf16).astype(f32)
            extra = jnp.where(
                lane == 0, -high, jnp.where(lane == 1, high - delta, 0.0)
            ).astype(bf16)
            left = jnp.concatenate([jnp.where(sel, g_att, jnp.zeros_like(g_att)), extra], 1)
            e = expo[0, head, r, :]
            grad_s = e * dot(left, values_ones, 1, 1).astype(bf16)
            grads_q.append(dot(grad_s, keys))
            span = slice(head * HEAD, (head + 1) * HEAD)
            add_k = dot(query_t[span], grad_s)
            add_v = dot(g_att_t[span], e)
            if i == 0:
                keys_t[span] = add_k
                values_t[span] = add_v
            else:
                keys_t[span] += add_k
                values_t[span] += add_v
        g_qkv[0, r, :] = (jnp.where(first, grads_q[0], grads_q[1]) * 0.125).astype(bf16)
    g_qkv[1] = (keys_t[...] * 0.125).astype(bf16).T
    g_qkv[2] = values_t[...].astype(bf16).T


def first_pairs_body(flags, qkv, expo, att, grad_att, g_qkv, keys_t, values_t):
    @pl.when(is_live(flags, pl.program_id(0)))
    def _():
        attend_backward_pair(qkv, expo, att, grad_att, g_qkv.at[0, 0], keys_t, values_t)


def first_pairs(flags, qkv, expo, att, grad_att):
    steps, _, pairs, length, _ = qkv.shape
    pairs -= 1

    def part(s, p, flags):
        return live_at(flags, s, p, pairs) + (0, 0)

    def qkv_at(s, p, flags):
        at, pair = live_at(flags, s, p, pairs)
        return (at, 0, pair, 0, 0)

    heads = pl.BlockSpec((1, 1, length, PAIR), part)
    return call(
        first_pairs_body,
        (steps, pairs),
        [
            pl.BlockSpec((1, 3, 1, length, PAIR), qkv_at),
            pl.BlockSpec((1, 2, length, length), part),
            heads, heads,
        ],
        pl.BlockSpec((1, 1, 3, length, PAIR), lambda s, p, flags: part(s, p, flags) + (0,)),
        shape_of((steps, pairs, 3, length, PAIR), bf16),
        [pltpu.VMEM((PAIR, length), f32), pltpu.VMEM((PAIR, length), f32)],
        "first_pairs", 40 * 10**9, (flags, qkv, expo, att, grad_att),
    )


def finish_body(
    steps, flags, own_x, far_x, qkv, expo, att, grad_att, grad_x1, mod, w_qkv, g_first,
    own_grad, far_grad, note, keep, send, g_last, keys_t, values_t, sum_qkv, chunk, grad_mod, note_s,
):
    slot = pl.program_id(0)
    own, far, dead = kinds(flags, slot, steps)
    length, width = own_x.shape[1:]
    chips = keep.shape[0]
    rows = width // (2 * chips)

    @pl.when(slot == 0)
    def _():
        for ref in (sum_qkv, chunk, grad_mod):
            ref[...] = jnp.zeros_like(ref)

    @pl.when(dead)
    def _():
        own_grad[...] = jnp.zeros_like(own_grad)

    @pl.when(is_live(flags, slot))
    def _():
        attend_backward_pair(qkv, expo, att, grad_att, g_last, keys_t, values_t)

    def finish(x_ref, out_ref):
        shift = mod[pl.ds(slot, 1), :width]
        scale = 1.0 + mod[pl.ds(slot, 1), width : 2 * width]
        row_block = 512
        for i in range(length // row_block):
            r = pl.ds(i * row_block, row_block)
            normed, rstd = norm(x_ref[0, r, :].astype(f32))
            h1 = (normed * scale + shift).astype(bf16)
            grad = []
            for kind in range(3):
                grad += [g_first[0, p, kind, r, :] for p in range(g_first.shape[1])]
                grad.append(g_last[kind, r, :])
            grad = jnp.concatenate(grad, 1)
            grad_h1 = dot(grad, w_qkv[...], 1, 1)
            sum_qkv[...] += dot(h1, grad, 0, 0)
            grad_mod[pl.ds(slot, 1), :width] += row_sum(grad_h1)
            grad_mod[pl.ds(slot, 1), width:] += row_sum(grad_h1 * normed)
            grad_n = grad_h1 * scale
            out_ref[0, r, :] = (
                grad_x1[0, r, :]
                + rstd
                * (
                    grad_n
                    - jnp.mean(grad_n, -1, keepdims=True)
                    - normed * jnp.mean(grad_n * normed, -1, keepdims=True)
                )
            ).astype(out_ref.dtype)

    @pl.when(own)
    def _():
        finish(own_x, own_grad)

    @pl.when(far)
    def _():
        finish(far_x, far_grad)

    @pl.when(slot == steps)
    def _():
        for device in range(2 * chips):
            for part in range(3):
                chunk[part * rows : (part + 1) * rows] = sum_qkv[
                    device * rows : (device + 1) * rows, part * width : (part + 1) * width
                ]
            pack_chunk(flags, device, chunk, keep, send)
        note_s[...] = jnp.zeros_like(note_s)
        for row in range(2 * steps):
            part = row % 2
            note_s[row : row + 1] = grad_mod[
                row // 2 : row // 2 + 1, part * width : (part + 1) * width
            ]
        note[...] = note_s[...].astype(bf16)


def finish(flags, own_x, far_x, qkv, expo, att, grad_att, grad_x1, mod, w_qkv, g_first, chips):
    steps, length, width = own_x.shape
    last = width // PAIR - 1
    sum_shape = (chips, up_to(3 * width // (2 * chips), 8), width)
    note_shape = (up_to(2 * steps, 8), width)

    def at(*part):
        return lambda s, flags: (live_at(flags, s, 0, 1)[0],) + part

    def block(where):
        return pl.BlockSpec((1, length, width), where)

    heads = pl.BlockSpec((1, 1, length, PAIR), at(last, 0, 0))
    return call(
        functools.partial(finish_body, steps),
        (steps + 1,),
        [
            block(lambda s, flags: (own_slot(flags, s), 0, 0)),
            block(lambda s, flags: (0, 0, 0)),
            pl.BlockSpec((1, 3, 1, length, PAIR), at(0, last, 0, 0)),
            pl.BlockSpec((1, 2, length, length), at(last, 0, 0)),
            heads, heads, block(at(0, 0)), fixed(mod.shape), fixed(w_qkv.shape),
            pl.BlockSpec((1, last, 3, length, PAIR), at(0, 0, 0, 0)),
        ],
        [
            block(lambda s, flags: (result_slot(flags, s, steps), 0, 0)),
            block(lambda s, flags: (0, 0, 0)),
            fixed(note_shape), fixed(sum_shape), fixed(sum_shape),
        ],
        [
            shape_of((steps, length, width), f32),
            shape_of((1, length, width), bf16),
            shape_of(note_shape, bf16),
            shape_of(sum_shape, f32),
            shape_of(sum_shape, bf16),
        ],
        [
            pltpu.VMEM((3, length, PAIR), bf16),
            pltpu.VMEM((PAIR, length), f32),
            pltpu.VMEM((PAIR, length), f32),
            pltpu.VMEM((width, 3 * width), f32),
            pltpu.VMEM(sum_shape[1:], f32),
            pltpu.VMEM((8, 2 * width), f32),
            pltpu.VMEM(note_shape, f32),
        ],
        "finish", 40 * 10**9,
        (flags, own_x, far_x, qkv, expo, att, grad_att, grad_x1, mod, w_qkv, g_first),
    )


def swap(array, mask):
    count = lax.axis_size("dp")
    return lax.ppermute(array, "dp", [(i, i ^ mask) for i in range(count)])


def tie(value, *others):
    return lax.optimization_barrier((value,) + others)[0]


def chip_groups(chips):
    bits = chips.bit_length() - 1
    return tuple(tuple(range(max(top - 2, 0), top)) for top in range(bits, 0, -2))


def chip_order(chip, chips):
    place, low = 0, 0
    for group in chip_groups(chips):
        place = place | ((chip >> group[0]) & ((1 << len(group)) - 1)) << low
        low += len(group)
    return place


def group_masks(group):
    return [sum(((k >> i) & 1) << b for i, b in enumerate(group)) for k in range(1, 1 << len(group))]


def gather_group(held, group):
    return [held] + [swap(held, mask << 1) for mask in group_masks(group)]


def stage_body(adds, sends, with_notes, held, notes, *refs):
    adds, outs = refs[:adds], refs[adds:]
    parts, rows, _ = held.shape
    size = parts * rows
    keep, joined, outs = outs[0], outs[1], outs[2:]
    own = notes.shape[0]
    joined[:own] = notes[...]
    if adds[0].shape[0] > size:
        for k, add in enumerate(adds):
            joined[(k + 1) * own : (k + 2) * own] = add[size:]
    count = parts // (sends + 1)
    for part in range(parts):
        total = held[part]
        for add in adds:
            total = total + add[part * rows : (part + 1) * rows].astype(f32)
        if part < count:
            keep[part] = total
        else:
            at = part % count * rows
            outs[part // count - 1][at : at + rows] = total.astype(bf16)
    if with_notes:
        for out in outs:
            out[count * rows :] = joined[...]


def stage(held, notes, adds, sends=0, with_notes=True):
    parts, rows, width = held.shape
    extra = adds[0].shape[0] - parts * rows
    count = parts // (sends + 1)
    joined = notes.shape[0] + len(adds) * extra
    size = count * rows + (joined if with_notes else 0)
    keep, joined, *outs = pl.pallas_call(
        functools.partial(stage_body, len(adds), sends, with_notes),
        out_shape=[shape_of((count, rows, width), f32), shape_of((joined, width), bf16)]
        + [shape_of((size, width), bf16)] * sends,
        name="stage",
    )(held, notes, *adds)
    return keep, joined, outs


def reduce_start(group, sums, notes):
    masks = group_masks(group)
    parts = [held.shape[0] // (len(masks) + 1) for held in sums]
    got = []
    for k, mask in enumerate(masks):
        pieces = [held[(k + 1) * n : (k + 2) * n].astype(bf16) for held, n in zip(sums, parts)]
        pieces += notes
        width = pieces[0].shape[-1]
        got.append(swap(jnp.concatenate([p.reshape(-1, width) for p in pieces], 0), mask << 1))
    return [held[:part] for held, part in zip(sums, parts)], notes, got


def reduce_done(totals, notes, got, *after):
    got = lax.optimization_barrier(tuple(got) + after)[: len(got)]
    joined = [[note] for note in notes]
    for block in got:
        start = 0
        for i, piece in enumerate(totals + notes):
            size = math.prod(piece.shape[:-1])
            part = block[start : start + size].reshape(piece.shape)
            start += size
            if i < len(totals):
                totals = totals[:i] + [totals[i] + part.astype(f32)] + totals[i + 1 :]
            else:
                joined[i - len(totals)].append(part)
    return totals, [jnp.concatenate(blocks, 0) for blocks in joined]


def hand_back_body(at, back_out, back_grad, _out, _grad, _after, out, grad, low, high, sems):
    @pl.when(at[0] > 0)
    def _():
        loads = [
            pltpu.make_async_copy(back_grad.at[0], low.at[0], sems.at[0]),
            pltpu.make_async_copy(back_out.at[0], low.at[1], sems.at[1]),
        ]
        for load in loads:
            load.start()
        loads[0].wait()
        high[...] = low[0].astype(f32)
        loads[1].wait()
        stores = [
            pltpu.make_async_copy(high, grad.at[at[1]], sems.at[2]),
            pltpu.make_async_copy(low.at[1], out.at[at[1]], sems.at[3]),
        ]
        for store in stores:
            store.start()
        for store in stores:
            store.wait()


def hand_back(at, back_out, back_grad, own_out, own_grad, after):
    return pl.pallas_call(
        hand_back_body,
        grid_spec=pltpu.PrefetchScalarGridSpec(
            num_scalar_prefetch=1,
            grid=(1,),
            in_specs=[anywhere] * 5,
            out_specs=[anywhere] * 2,
            scratch_shapes=[
                pltpu.VMEM((2,) + own_grad.shape[1:], bf16),
                pltpu.VMEM(own_grad.shape[1:], f32),
                pltpu.SemaphoreType.DMA((4,)),
            ],
        ),
        out_shape=[shape_of(own_out.shape, bf16), shape_of(own_grad.shape, f32)],
        input_output_aliases={3: 0, 4: 1},
        name="hand_back",
    )(at, back_out, back_grad, own_out, own_grad, after)


def result_body(
    sums1, sums2, cond1, cond2, mine1, other1, mine2, other2,
    ada, b_ada, qkv, out, b_out, up, b_up, down, b_down, ada_sum,
):
    rows, width = out.shape
    ratio = up.shape[1] // width
    me = lax.axis_index("dp").astype(jnp.int32)
    start = 0
    for cond, mine, other in ((cond1, mine1, other1), (cond2, mine2, other2)):
        half = mine.shape[0]
        parts = 2 if cond is cond1 else 4
        row = lax.broadcasted_iota(jnp.int32, (half, cond.shape[1]), 0)
        for part in range(parts):
            hit = lax.rem(row, parts) == part
            total = 0.0
            for i, ref in enumerate((mine, other)):
                left = jnp.where(hit, cond[i * half : (i + 1) * half].astype(f32), 0.0)
                total = total + dot(left.astype(bf16), ref[...], 0, 0)
            cols = slice((start + part) * width, (start + part + 1) * width)
            ada[:, cols] = total[:rows]
            ada_sum[:, cols] = total[rows : rows + 1]
        start += parts
    b_ada[...] = pltpu.roll(ada_sum[...], lax.rem(6 * width - me * 6 * rows, 6 * width), 1)[
        :, : 6 * rows
    ]
    for part in range(3):
        qkv[:, part * width : (part + 1) * width] = sums1[0, part * rows : (part + 1) * rows]
    out[...] = sums2[0, :rows]
    for part in range(ratio):
        up[:, part * width : (part + 1) * width] = sums2[
            0, (1 + part) * rows : (2 + part) * rows
        ]
    after = (1 + 2 * ratio) * rows
    down[...] = sums2[0, after - ratio * rows : after]
    for i, ref in enumerate((b_out, b_up, b_down)):
        size = ref.shape[1]
        line = sums2[0, after + i : after + i + 1]
        shift = lax.rem(width - lax.rem(me * size, width), width)
        ref[...] = pltpu.roll(line, shift, 1)[:, :size]


def results(sums1, sums2, cond1, cond2, mine1, other1, mine2, other2, rows, ratio):
    width = sums1.shape[2]
    shapes = [
        (rows, 6 * width), (1, 6 * rows), (rows, 3 * width), (rows, width), (1, rows),
        (rows, ratio * width), (1, ratio * rows), (ratio * rows, width), (1, rows),
    ]
    return pl.pallas_call(
        result_body,
        out_shape=[shape_of(s, f32) for s in shapes],
        scratch_shapes=[pltpu.VMEM((1, 6 * width), f32)],
        name="results",
    )(sums1, sums2, cond1, cond2, mine1, other1, mine2, other2)


def body(
    fields, conditions, step_counts, cotangent,
    w_ada, b_ada, w_qkv, w_out, b_out, w_up, b_up, w_down, b_down,
):
    devices = lax.axis_size("dp")
    chips = devices // 2
    me = lax.axis_index("dp").astype(jnp.int32)
    chip, core = me >> 1, me & 1
    steps, length, width = fields.shape[1:]
    hidden_units = w_up.shape[1]
    ratio = hidden_units // width
    rows = width // devices
    fields, conditions, cotangent = fields[0], conditions[0], cotangent[0]
    groups = chip_groups(chips)

    count = step_counts[0]
    biases = jnp.concatenate([b_ada, b_out, b_up, b_down])[None]
    first, second = pack_shards(w_ada, w_qkv, w_out, w_up, w_down, biases)
    head = jnp.concatenate([conditions, jnp.full((4, width), count, bf16)], 0)
    other_head = swap(tie(head, first), 1)
    other_count = other_head[steps, 0].astype(jnp.int32)
    give = count - other_count >= 2
    take = (other_count - count >= 2).astype(jnp.int32)
    keep = count - give.astype(jnp.int32)
    flags = jnp.stack([keep, take, chip_order(chip, chips), core])
    far_cond = lax.dynamic_index_in_dim(other_head, other_count - 1, 0)
    cond = jnp.concatenate([conditions, jnp.zeros((8 - steps, width), bf16)], 0)
    cond = jnp.where((jnp.arange(8) == keep)[:, None] & (take > 0), far_cond, cond)
    cond_act = jax.nn.silu(cond.astype(f32)).astype(bf16)

    cond_row = (1 + 2 * ratio) * rows
    mine_a = first[None]
    mine_b = lax.dynamic_update_slice_in_dim(second, cond_act[:steps], cond_row, 0)[None]
    for group in groups[:-1]:
        mine_a = jnp.concatenate(gather_group(mine_a, group), 0)
    far_x = swap(tie(lax.dynamic_index_in_dim(fields, count - 1, 0), mine_a), 1)
    far_g = swap(tie(lax.dynamic_index_in_dim(cotangent, count - 1, 0), mine_a), 1)
    for group in groups[:-1]:
        mine_b = jnp.concatenate(gather_group(tie(mine_b, far_x, far_g), group), 0)
    both_b = jnp.stack([mine_b, swap(tie(mine_b, mine_a), 1)])
    mine_a = gather_group(mine_a, groups[-1])
    other_a = [swap(piece, 1) for piece in mine_a]
    first_kernel = lax.optimization_barrier((flags, both_b, far_x, far_g, cond_act))
    qkv, expo, att, inv, mod, bias, full_qkv = attend_forward(
        first_kernel[0], fields, far_x, cond_act, mine_a, other_a, 8 + ratio
    )
    all_b = gather_group(first_kernel[1], groups[-1])
    all_b = lax.optimization_barrier((*all_b, mod))[:-1]
    own_out, far_out, grad_x1, grad_att, note2, keep2, send2 = feed_forward(
        flags, fields, far_x, cotangent, far_g, att, inv, mod, bias, all_b, hidden_units
    )

    up_groups = tuple(reversed(groups))
    late = up_groups[2:]
    masks = [[mask << 1 for mask in group_masks(group)] for group in up_groups]
    got2 = swap(send2.reshape(-1, width), 1)
    held2, note2, sends = stage(keep2, note2, [got2], len(masks[0]))
    gots = [swap(send, mask) for send, mask in zip(sends, masks[0])]
    back_out = swap(far_out, 1)
    g_first = first_pairs(tie(flags, held2), qkv, expo, att, grad_att)
    gots = lax.optimization_barrier((*gots, g_first))[:-1]
    held2, note2, sends = stage(held2, note2, gots, len(masks[1]))
    gots = [swap(send, mask) for send, mask in zip(sends, masks[1])]
    own_grad, far_grad, note1, keep1, send1 = finish(
        tie(flags, held2), fields, far_x, qkv, expo, att, grad_att, grad_x1, mod, full_qkv, g_first,
        chips,
    )
    got1 = swap(send1, 1)
    held1 = keep1 + got1.astype(f32)
    back_grad = swap(tie(far_grad, got1), 1)
    note1 = note1[None]

    all_b = lax.optimization_barrier((*all_b, got1))[:-1]
    cond = jnp.stack([piece[..., cond_row : cond_row + steps, :] for piece in all_b])
    cond = lax.dynamic_slice_in_dim(cond, me * rows, rows, 4)
    sizes = [1 << len(group) for group in up_groups]
    cond = cond.reshape([sizes[0], 2] + sizes[1:] + [steps, rows])
    last = len(sizes)
    cond = cond.transpose([1] + list(range(last, 1, -1)) + [0, last + 1, last + 2])
    cond = cond.reshape(-1, rows)
    cond = jnp.concatenate([cond, jnp.ones((cond.shape[0], 1), bf16)], 1)
    cond = jnp.concatenate([cond, jnp.zeros((cond.shape[0], -cond.shape[1] % 16), bf16)], 1)
    cond1, cond2 = jnp.repeat(cond, 2, 0), jnp.repeat(cond, 4, 0)

    going = reduce_start(up_groups[0], [held1], [note1])
    (held1,), (note1,) = reduce_done(*going, cond1, cond2)
    gots = lax.optimization_barrier((*gots, held1))[:-1]
    held2, note2, sends = stage(held2, note2, gots, len(masks[2]) if late else 0)
    own_out, own_grad = hand_back(
        jnp.stack([give.astype(jnp.int32), count - 1]), back_out, back_grad, own_out, own_grad, held1
    )
    for i, group in enumerate(up_groups[1:]):
        if i > 0:
            gots = [swap(send, mask) for send, mask in zip(sends, masks[i + 1])]
            held2, note2, sends = stage(
                held2, note2, gots, len(masks[i + 2]) if i + 2 < len(masks) else 0
            )
        (held1,), (note1,) = reduce_done(*reduce_start(group, [held1], [note1]))
    note1 = note1.reshape(-1, width)
    other1, other2 = swap(note1, 1), swap(note2, 1)
    grads = results(
        held1, held2, cond1, cond2, note1, other1, note2, other2, rows, ratio
    )
    grads = [g[0] if i in (1, 4, 6, 8) else g for i, g in enumerate(grads)]

    return (own_out[None], own_grad[None], *grads)


def solution(mesh):
    item, matrix, vector = P("dp", None, None, None), P("dp", None), P("dp")
    return jax.shard_map(
        body,
        mesh=mesh,
        in_specs=(
            item, P("dp", None, None), vector, item,
            matrix, vector, matrix, matrix, vector, matrix, vector, matrix, vector,
        ),
        out_specs=(
            item, item, matrix, vector, matrix, matrix, vector, matrix, vector, matrix, vector,
        ),
        check_vma=False,
    )
```

```python
import functools
import math

import jax
import jax.numpy as jnp
from jax import lax
from jax.experimental import pallas as pl
from jax.experimental.pallas import tpu as pltpu
from jax.sharding import PartitionSpec as P

HEAD = 64
PAIR = 2 * HEAD
EPS = 1e-6
LOG2E = 1.4426950408889634
VMEM_LIMIT = 60 * 2**20
bf16 = jnp.bfloat16
f32 = jnp.float32
shape_of = jax.ShapeDtypeStruct


def dot(left, right, left_dim=1, right_dim=0):
    return lax.dot_general(
        left, right, (((left_dim,), (right_dim,)), ((), ())), preferred_element_type=f32
    )


def norm(value):
    mean = jnp.mean(value, -1, keepdims=True)
    cent = value - mean
    var = jnp.mean(cent * cent, -1, keepdims=True)
    rstd = lax.rsqrt(var + EPS)
    return cent * rstd, rstd


def row_sum(value):
    return jnp.sum(value, 0, keepdims=True)


def up_to(value, unit):
    return -(-value // unit) * unit


def call(body, grid, in_specs, out_specs, out_shape, scratch, name, flops, args):
    return pl.pallas_call(
        body,
        grid_spec=pltpu.PrefetchScalarGridSpec(
            num_scalar_prefetch=1,
            grid=grid,
            in_specs=in_specs,
            out_specs=out_specs,
            scratch_shapes=scratch,
        ),
        out_shape=out_shape,
        compiler_params=pltpu.CompilerParams(vmem_limit_bytes=VMEM_LIMIT),
        cost_estimate=pl.CostEstimate(flops=flops, bytes_accessed=10**7, transcendentals=0),
        name=name,
    )(*args)


anywhere = pl.BlockSpec(memory_space=pl.ANY)


def fetch(pieces, dest, sems):
    copies = [pltpu.make_async_copy(p, dest.at[k], sems.at[k]) for k, p in enumerate(pieces)]
    for copy in copies:
        copy.start()
    for copy in copies:
        copy.wait()


def fixed(shape):
    return pl.BlockSpec(shape, lambda *at: (0,) * len(shape))


KEEP, TAKE, PLACE, CORE = range(4)


def own_slot(flags, slot):
    return jnp.minimum(slot, flags[KEEP] - 1)


def is_live(flags, slot):
    return slot < flags[KEEP] + flags[TAKE]


def live_at(flags, slot, block, blocks):
    live = flags[KEEP] + flags[TAKE]
    return jnp.minimum(slot, live - 1), jnp.where(slot < live, block, blocks - 1)


def result_slot(flags, slot, steps):
    after = jnp.clip(slot - flags[TAKE], flags[KEEP] - 1, steps - 1)
    return jnp.where(slot < flags[KEEP], slot, after)


def kinds(flags, slot, steps):
    own = slot < flags[KEEP]
    far = (slot == flags[KEEP]) & (flags[TAKE] > 0)
    return own, far, jnp.logical_not(own | far) & (slot - flags[TAKE] < steps)


def pack_body(ada, qkv, out, up, down, bias, first, second, first_s, second_s):
    rows, width = out.shape
    me = lax.axis_index("dp").astype(jnp.int32)
    first_s[...] = jnp.zeros_like(first_s)
    second_s[...] = jnp.zeros_like(second_s)

    def put(dest, start, ref):
        for part in range(ref.shape[1] // width):
            dest[start + part * rows : start + (part + 1) * rows] = ref[
                :, part * width : (part + 1) * width
            ].astype(f32)

    put(first_s, 0, ada)
    put(first_s, 6 * rows, qkv)
    put(second_s, 0, out)
    put(second_s, rows, up)
    after = rows + up.shape[1] * rows // width
    second_s[after : after + down.shape[0]] = down[...].astype(f32)
    source = lax.broadcasted_iota(jnp.int32, (bias.shape[1], width), 0)
    lane = lax.broadcasted_iota(jnp.int32, (bias.shape[1], width), 1)
    start = 0
    for i, count in enumerate((6 * rows, rows, up.shape[1] * rows // width, rows)):
        at = lax.rem(me * count, width) + source - start
        at = jnp.where(at >= width, at - width, at)
        hit = (source >= start) & (source < start + count) & (at == lane)
        first_s[9 * rows + i : 9 * rows + i + 1] = dot(bias[...], jnp.where(hit, 1.0, 0.0).astype(bf16))
        start += count
    first[...] = first_s[...].astype(bf16)
    second[...] = second_s[...].astype(bf16)


def pack_shards(*args):
    _, _, out, up, down, _ = args
    rows, width = out.shape
    sizes = (up_to(9 * rows + 4, 16), up_to(rows + up.shape[1] * rows // width + down.shape[0] + 4, 16))
    return pl.pallas_call(
        pack_body,
        out_shape=[shape_of((n, width), bf16) for n in sizes],
        scratch_shapes=[pltpu.VMEM((n, width), f32) for n in sizes],
        name="pack_shards",
    )(*args)


def each_shard(flags, chips, blocks_of):
    first = flags[CORE] == 0
    for chip in range(chips):
        mine, other = blocks_of(jnp.bitwise_xor(flags[PLACE], chip_order(chip, chips)))
        mine, other = mine.astype(f32), other.astype(f32)
        yield 2 * chip, jnp.where(first, mine, other)
        yield 2 * chip + 1, jnp.where(first, other, mine)


def place_columns(dest, device, block, start, rows, count, width):
    for part in range(count):
        dest[device * rows : (device + 1) * rows, part * width : (part + 1) * width] = block[
            start + part * rows : start + (part + 1) * rows
        ]


def attend_pair(qkv, pair, expo, att, inv):
    length = att.shape[-2]
    row_block = 256
    keys = qkv[0, 1, pair]
    values = qkv[0, 2, pair]
    values_ones = jnp.concatenate([values, jnp.ones_like(values)], 1)
    first = lax.broadcasted_iota(jnp.int32, (row_block, PAIR), 1) < HEAD
    for i in range(length // row_block):
        r = pl.ds(i * row_block, row_block)
        query = qkv[0, 0, pair, r, :]
        outs = []
        for head in range(2):
            sel = first if head == 0 else jnp.logical_not(first)
            scores = dot(jnp.where(sel, query, jnp.zeros_like(query)), keys, 1, 1)
            top = jnp.max(scores, -1, keepdims=True)
            e = jnp.exp2((scores - top) * (0.125 * LOG2E)).astype(bf16)
            expo[0, head, r, :] = e
            outs.append(dot(e, values_ones))
        out = jnp.where(first, outs[0][:, :PAIR], outs[1][:, :PAIR])
        inverse = 1.0 / jnp.where(first, outs[0][:, PAIR:], outs[1][:, PAIR:])
        att[0, 0, r, :] = (out * inverse).astype(bf16)
        inv[0, 0, r, :] = inverse


def attend_forward_body(flags, own_x, far_x, cond, *refs):
    pieces = refs[:-11]
    qkv, expo, att, inv, mod, bias, w_qkv, w_f32, bias_f32, shards, sems = refs[-11:]
    slot = pl.program_id(0)
    pair = pl.program_id(1)
    length, width = own_x.shape[1:]
    group, others = shards.shape[1:3]
    chips = group * others
    rows = width // (2 * chips)
    pairs = width // PAIR

    def blocks_of(place):
        at = lax.div(place, others), lax.rem(place, others)
        return shards[(0, *at)], shards[(1, *at)]

    @pl.when((slot == 0) & (pair == 0))
    def _():
        fetch(pieces[:group], shards.at[0], sems.at[0])
        fetch(pieces[group:], shards.at[1], sems.at[1])
        bias_f32[...] = jnp.zeros_like(bias_f32)
        lane = lax.broadcasted_iota(jnp.int32, (1, width), 1)
        for device, block in each_shard(flags, chips, blocks_of):
            place_columns(w_f32, device, block, 0, rows, 6, width)
            start = 0
            for i, count in enumerate((6 * rows, rows, bias_f32.shape[0] * rows - 8 * rows, rows)):
                low, high = device * count, (device + 1) * count
                for part in range(low // width, (high - 1) // width + 1):
                    at = lane + part * width
                    bias_f32[start + part : start + part + 1] += jnp.where(
                        (at >= low) & (at < high), block[9 * rows + i : 9 * rows + i + 1], 0.0
                    )
                start += 2 * chips * count // width
        for part in range(6):
            cols = slice(part * width, (part + 1) * width)
            mod[:, cols] = dot(cond[...], w_f32[:, cols].astype(bf16)) + bias_f32[part : part + 1]
        for part in range(bias_f32.shape[0] - 6):
            bias[:, part * width : (part + 1) * width] = bias_f32[6 + part : 7 + part]
        for device, block in each_shard(flags, chips, blocks_of):
            place_columns(w_f32, device, block, 6 * rows, rows, 3, width)
        w_qkv[...] = w_f32[:, : 3 * width].astype(bf16)

    @pl.when((pair == 0) & is_live(flags, slot))
    def _():
        shift = mod[pl.ds(slot, 1), :width]
        scale = 1.0 + mod[pl.ds(slot, 1), width : 2 * width]
        row_block = 256

        def project(ref):
            @pl.loop(0, length // row_block)
            def _(i):
                r = pl.ds(pl.multiple_of(i * row_block, row_block), row_block)
                normed, _ = norm(ref[0, r, :].astype(f32))
                h1 = (normed * scale + shift).astype(bf16)
                result = dot(h1, w_qkv[...]).astype(bf16)
                for kind in range(3):
                    for p in range(pairs):
                        at = kind * width + p * PAIR
                        qkv[0, kind, p, r, :] = result[:, at : at + PAIR]

        @pl.when(slot < flags[KEEP])
        def _():
            project(own_x)

        @pl.when(slot >= flags[KEEP])
        def _():
            project(far_x)

    @pl.when(is_live(flags, slot))
    def _():
        attend_pair(qkv, pair, expo, att, inv)


def attend_forward(flags, own_x, far_x, cond, mine, other, bias_rows):
    steps, length, width = own_x.shape
    pairs = width // PAIR
    shards_shape = (2, len(mine)) + mine[0].shape
    args = (flags, own_x, far_x, cond, *mine, *other)

    def at(s, p, flags):
        return live_at(flags, s, p, pairs) + (0, 0)

    whole = pl.BlockSpec((1, 3, pairs, length, PAIR), lambda s, p, flags: (at(s, p, flags)[0], 0, 0, 0, 0))
    part = pl.BlockSpec((1, 1, length, PAIR), at)
    return call(
        attend_forward_body,
        (steps, pairs),
        [
            pl.BlockSpec((1, length, width), lambda s, p, flags: (own_slot(flags, s), 0, 0)),
            fixed(far_x.shape), fixed(cond.shape),
        ] + [anywhere] * (2 * len(mine)),
        [
            whole,
            pl.BlockSpec((1, 2, length, length), at),
            part, part,
            fixed((8, 6 * width)), fixed((1, (bias_rows - 6) * width)), fixed((width, 3 * width)),
        ],
        [
            shape_of((steps, 3, pairs, length, PAIR), bf16),
            shape_of((steps, 2 * pairs, length, length), bf16),
            shape_of((steps, pairs, length, PAIR), bf16),
            shape_of((steps, pairs, length, PAIR), f32),
            shape_of((8, 6 * width), f32),
            shape_of((1, (bias_rows - 6) * width), f32),
            shape_of((width, 3 * width), bf16),
        ],
        [
            pltpu.VMEM((width, 6 * width), f32),
            pltpu.VMEM((bias_rows, width), f32),
            pltpu.VMEM(shards_shape, bf16),
            pltpu.SemaphoreType.DMA((2, len(mine))),
        ],
        "attend_forward", 30 * 10**9, args,
    )


def pack_chunk(flags, device, chunk, keep, send):
    place = jnp.bitwise_xor(flags[PLACE], chip_order(device >> 1, keep.shape[0]))

    @pl.when(flags[CORE] == (device & 1))
    def _():
        keep[place] = chunk[...].astype(keep.dtype)

    @pl.when(flags[CORE] != (device & 1))
    def _():
        send[place] = chunk[...].astype(bf16)


def feed_forward_body(
    steps, flags, own_x, far_x, own_g, far_g, att, inv, mod, bias, *refs
):
    (
        own_out, far_out, grad_x1, grad_att, note, keep, send,
        x_s, g_s, w_out, w_up, w_down, sum_out, sum_up, sum_down_t, down_f32, chunk, bias_sum,
        grad_mod, note_s, shards, sems,
    ) = refs[-22:]
    pieces = refs[:-22]
    slot = pl.program_id(0)
    step = pl.program_id(1)
    own, far, dead = kinds(flags, slot, steps)
    width = x_s.shape[1]
    hidden_units = w_up.shape[1]
    ratio = hidden_units // width
    group, _, others = shards.shape[:3]
    chips = group * others
    rows = width // (2 * chips)

    def blocks_of(place):
        part, place = lax.div(place, others), lax.rem(place, others)
        return shards[part, 0, place], shards[part, 1, place]

    @pl.when((slot == 0) & (step == 0))
    def _():
        fetch(pieces, shards, sems)
        for device, block in each_shard(flags, chips, blocks_of):
            place_columns(sum_out, device, block, 0, rows, 1, width)
            place_columns(sum_up, device, block, rows, rows, ratio, width)
            place_columns(
                down_f32, device, block, (1 + ratio) * rows, ratio * rows, 1, width
            )
        w_out[...] = sum_out[...].astype(bf16)
        w_up[...] = sum_up[...].astype(bf16)
        w_down[...] = down_f32[...].astype(bf16)
        for ref in (sum_out, sum_up, sum_down_t, bias_sum, chunk, grad_mod):
            ref[...] = jnp.zeros_like(ref)

    @pl.when(dead)
    def _():
        own_out[...] = jnp.zeros_like(own_out)

    @pl.when(own)
    def _():
        x_s[...] = own_x[0].astype(f32)
        g_s[...] = own_g[0].astype(f32)

    @pl.when(far)
    def _():
        x_s[...] = far_x[0].astype(f32)
        g_s[...] = far_g[0].astype(f32)

    @pl.when(is_live(flags, slot))
    def _():
        def vector(part):
            return mod[pl.ds(slot, 1), part * width : (part + 1) * width]

        gate1, shift2, scale2, gate2 = vector(2), vector(3), 1.0 + vector(4), vector(5)
        b_out = bias[:, :width]
        b_up = bias[:, width : width + hidden_units]
        b_down = bias[:, width + hidden_units :]

        def lanes(ref):
            return jnp.concatenate([ref[0, p] for p in range(ref.shape[1])], 1)

        attended = lanes(att)
        branch1 = dot(attended, w_out[...]) + b_out
        x1 = x_s[...] + gate1 * branch1
        normed2, rstd = norm(x1)
        h2 = (normed2 * scale2 + shift2).astype(bf16)
        pre = dot(h2, w_up[...]) + b_up
        cdf = 0.5 * (1.0 + lax.erf(pre * (1 / math.sqrt(2.0))))
        hidden = (pre * cdf).astype(bf16)
        slope = cdf + pre * jnp.exp2(pre * pre * (-0.5 * LOG2E)) * (1 / math.sqrt(2 * math.pi))
        branch2 = dot(hidden, w_down[...]) + b_down
        result = (x1 + gate2 * branch2).astype(bf16)

        @pl.when(own)
        def _():
            own_out[0] = result

        @pl.when(far)
        def _():
            far_out[0] = result

        grad = g_s[...]
        grad_b2 = (gate2 * grad).astype(bf16)
        grad_pre = (dot(grad_b2, w_down[...], 1, 1) * slope).astype(bf16)
        grad_h2 = dot(grad_pre, w_up[...], 1, 1)
        grad_n = grad_h2 * scale2
        g_x1 = grad + rstd * (
            grad_n
            - jnp.mean(grad_n, -1, keepdims=True)
            - normed2 * jnp.mean(grad_n * normed2, -1, keepdims=True)
        )
        grad_b1 = (gate1 * g_x1).astype(bf16)
        grad_x1[0] = g_x1
        g_att = (dot(grad_b1, w_out[...], 1, 1) * lanes(inv)).astype(bf16)
        for p in range(width // PAIR):
            grad_att[0, p] = g_att[:, p * PAIR : (p + 1) * PAIR]

        def add_mod(part, value):
            grad_mod[pl.ds(slot, 1), part * width : (part + 1) * width] += row_sum(value)

        add_mod(0, g_x1 * branch1)
        add_mod(1, grad_h2)
        add_mod(2, grad_h2 * normed2)
        add_mod(3, grad * branch2)
        sum_out[...] += dot(attended, grad_b1, 0, 0)
        sum_up[...] += dot(h2, grad_pre, 0, 0)
        sum_down_t[...] += dot(grad_b2, hidden, 0, 0)
        bias_sum[:, :width] += row_sum(grad_b1.astype(f32))
        bias_sum[:, width : width + hidden_units] += row_sum(grad_pre.astype(f32))
        bias_sum[:, width + hidden_units :] += row_sum(grad_b2.astype(f32))

    @pl.when((slot == pl.num_programs(0) - 1) & (step == pl.num_programs(1) - 1))
    def _():
        down_f32[...] = sum_down_t[...].T
        for device in range(2 * chips):
            span = slice(device * rows, (device + 1) * rows)
            chunk[:rows] = sum_out[span]
            for part in range(ratio):
                chunk[(1 + part) * rows : (2 + part) * rows] = sum_up[
                    span, part * width : (part + 1) * width
                ]
            chunk[(1 + ratio) * rows : (1 + 2 * ratio) * rows] = down_f32[
                device * ratio * rows : (device + 1) * ratio * rows
            ]
            up_row = 1 + device * ratio * rows // width
            for i, part in enumerate((0, up_row, 1 + ratio)):
                at = (1 + 2 * ratio) * rows + i
                chunk[at : at + 1] = bias_sum[:, part * width : (part + 1) * width]
            pack_chunk(flags, device, chunk, keep, send)
        note_s[...] = jnp.zeros_like(note_s)
        for row in range(4 * steps):
            part = row % 4
            note_s[row : row + 1] = grad_mod[
                row // 4 : row // 4 + 1, part * width : (part + 1) * width
            ]
        note[...] = note_s[...].astype(bf16)


def feed_forward(
    flags, own_x, far_x, own_g, far_g, att, inv, mod, bias, shards, hidden_units
):
    steps, length, width = own_x.shape
    row_block = 1024
    blocks = length // row_block
    group, others = len(shards), shards[0].shape[1]
    rows = width // (2 * group * others)
    ratio = hidden_units // width
    packed_rows = up_to((1 + 2 * ratio) * rows + 3, 16)
    sum_shape = (group * others, packed_rows, width)
    note_shape = (up_to(4 * steps, 16), width)

    def own(s, b, flags):
        return (own_slot(flags, s), jnp.where(s < flags[KEEP], b, blocks - 1), 0)

    def far(s, b, flags):
        keep = flags[KEEP]
        return (0, jnp.where(s < keep, 0, jnp.where(s == keep, b, blocks - 1)), 0)

    def live(s, b, flags):
        return live_at(flags, s, b, blocks) + (0,)

    def live_parts(s, b, flags):
        at, part = live_at(flags, s, b, blocks)
        return (at, 0, part, 0)

    def own_result(s, b, flags):
        own, _, dead = kinds(flags, s, steps)
        return (result_slot(flags, s, steps), jnp.where(own | dead, b, blocks - 1), 0)

    def block(where):
        return pl.BlockSpec((1, row_block, width), where)

    def parts(count):
        return pl.BlockSpec((1, count, row_block, PAIR), live_parts)

    pairs = width // PAIR
    args = (flags, own_x, far_x, own_g, far_g, att, inv, mod, bias, *shards)
    return call(
        functools.partial(feed_forward_body, steps),
        (steps + 1, blocks),
        [
            block(own), block(far), block(own), block(far), parts(pairs), parts(pairs),
            fixed(mod.shape), fixed(bias.shape),
        ] + [anywhere] * group,
        [
            block(own_result), block(far), block(live), parts(pairs),
            fixed(note_shape), fixed(sum_shape), fixed(sum_shape),
        ],
        [
            shape_of((steps, length, width), bf16),
            shape_of((1, length, width), bf16),
            shape_of((steps, length, width), f32),
            shape_of((steps, pairs, length, PAIR), bf16),
            shape_of(note_shape, bf16),
            shape_of(sum_shape, bf16),
            shape_of(sum_shape, bf16),
        ],
        [
            pltpu.VMEM((row_block, width), f32),
            pltpu.VMEM((row_block, width), f32),
            pltpu.VMEM((width, width), bf16),
            pltpu.VMEM((width, hidden_units), bf16),
            pltpu.VMEM((hidden_units, width), bf16),
            pltpu.VMEM((width, width), f32),
            pltpu.VMEM((width, hidden_units), f32),
            pltpu.VMEM((width, hidden_units), f32),
            pltpu.VMEM((hidden_units, width), f32),
            pltpu.VMEM((packed_rows, width), f32),
            pltpu.VMEM(bias.shape, f32),
            pltpu.VMEM((8, 4 * width), f32),
            pltpu.VMEM(note_shape, f32),
            pltpu.VMEM((group,) + shards[0].shape, bf16),
            pltpu.SemaphoreType.DMA((group,)),
        ],
        "feed_forward", 60 * 10**9, args,
    )


def attend_backward_pair(qkv, expo, att, grad_att, g_qkv, keys_t, values_t):
    length = att.shape[2]
    row_block = 512
    keys = qkv[0, 1, 0]
    values = qkv[0, 2, 0]
    values_ones = jnp.concatenate([values, jnp.ones_like(values)], 1)
    lane = lax.broadcasted_iota(jnp.int32, (row_block, PAIR), 1)
    first = lane < HEAD
    for i in range(length // row_block):
        r = pl.ds(i * row_block, row_block)
        query = qkv[0, 0, 0, r, :]
        g_att = grad_att[0, 0, r, :]
        product = g_att.astype(f32) * att[0, 0, r, :].astype(f32)
        query_t = query.T
        g_att_t = g_att.T
        grads_q = []
        for head in range(2):
            sel = first if head == 0 else jnp.logical_not(first)
            delta = jnp.sum(jnp.where(sel, product, 0.0), -1, keepdims=True)
            high = delta.astype(bf16).astype(f32)
            extra = jnp.where(
                lane == 0, -high, jnp.where(lane == 1, high - delta, 0.0)
            ).astype(bf16)
            left = jnp.concatenate([jnp.where(sel, g_att, jnp.zeros_like(g_att)), extra], 1)
            e = expo[0, head, r, :]
            grad_s = e * dot(left, values_ones, 1, 1).astype(bf16)
            grads_q.append(dot(grad_s, keys))
            span = slice(head * HEAD, (head + 1) * HEAD)
            add_k = dot(query_t[span], grad_s)
            add_v = dot(g_att_t[span], e)
            if i == 0:
                keys_t[span] = add_k
                values_t[span] = add_v
            else:
                keys_t[span] += add_k
                values_t[span] += add_v
        g_qkv[0, r, :] = (jnp.where(first, grads_q[0], grads_q[1]) * 0.125).astype(bf16)
    g_qkv[1] = (keys_t[...] * 0.125).astype(bf16).T
    g_qkv[2] = values_t[...].astype(bf16).T


def first_pairs_body(flags, qkv, expo, att, grad_att, g_qkv, keys_t, values_t):
    @pl.when(is_live(flags, pl.program_id(0)))
    def _():
        attend_backward_pair(qkv, expo, att, grad_att, g_qkv.at[0, 0], keys_t, values_t)


def first_pairs(flags, qkv, expo, att, grad_att):
    steps, _, pairs, length, _ = qkv.shape
    pairs -= 1

    def part(s, p, flags):
        return live_at(flags, s, p, pairs) + (0, 0)

    def qkv_at(s, p, flags):
        at, pair = live_at(flags, s, p, pairs)
        return (at, 0, pair, 0, 0)

    heads = pl.BlockSpec((1, 1, length, PAIR), part)
    return call(
        first_pairs_body,
        (steps, pairs),
        [
            pl.BlockSpec((1, 3, 1, length, PAIR), qkv_at),
            pl.BlockSpec((1, 2, length, length), part),
            heads, heads,
        ],
        pl.BlockSpec((1, 1, 3, length, PAIR), lambda s, p, flags: part(s, p, flags) + (0,)),
        shape_of((steps, pairs, 3, length, PAIR), bf16),
        [pltpu.VMEM((PAIR, length), f32), pltpu.VMEM((PAIR, length), f32)],
        "first_pairs", 40 * 10**9, (flags, qkv, expo, att, grad_att),
    )


def finish_body(
    steps, flags, own_x, far_x, qkv, expo, att, grad_att, grad_x1, mod, w_qkv, g_first,
    own_grad, far_grad, note, keep, send, g_last, keys_t, values_t, sum_qkv, chunk, grad_mod, note_s,
):
    slot = pl.program_id(0)
    own, far, dead = kinds(flags, slot, steps)
    length, width = own_x.shape[1:]
    chips = keep.shape[0]
    rows = width // (2 * chips)

    @pl.when(slot == 0)
    def _():
        for ref in (sum_qkv, chunk, grad_mod):
            ref[...] = jnp.zeros_like(ref)

    @pl.when(dead)
    def _():
        own_grad[...] = jnp.zeros_like(own_grad)

    @pl.when(is_live(flags, slot))
    def _():
        attend_backward_pair(qkv, expo, att, grad_att, g_last, keys_t, values_t)

    def finish(x_ref, out_ref):
        shift = mod[pl.ds(slot, 1), :width]
        scale = 1.0 + mod[pl.ds(slot, 1), width : 2 * width]
        row_block = 512
        for i in range(length // row_block):
            r = pl.ds(i * row_block, row_block)
            normed, rstd = norm(x_ref[0, r, :].astype(f32))
            h1 = (normed * scale + shift).astype(bf16)
            grad = []
            for kind in range(3):
                grad += [g_first[0, p, kind, r, :] for p in range(g_first.shape[1])]
                grad.append(g_last[kind, r, :])
            grad = jnp.concatenate(grad, 1)
            grad_h1 = dot(grad, w_qkv[...], 1, 1)
            sum_qkv[...] += dot(h1, grad, 0, 0)
            grad_mod[pl.ds(slot, 1), :width] += row_sum(grad_h1)
            grad_mod[pl.ds(slot, 1), width:] += row_sum(grad_h1 * normed)
            grad_n = grad_h1 * scale
            out_ref[0, r, :] = (
                grad_x1[0, r, :]
                + rstd
                * (
                    grad_n
                    - jnp.mean(grad_n, -1, keepdims=True)
                    - normed * jnp.mean(grad_n * normed, -1, keepdims=True)
                )
            ).astype(out_ref.dtype)

    @pl.when(own)
    def _():
        finish(own_x, own_grad)

    @pl.when(far)
    def _():
        finish(far_x, far_grad)

    @pl.when(slot == steps)
    def _():
        for device in range(2 * chips):
            for part in range(3):
                chunk[part * rows : (part + 1) * rows] = sum_qkv[
                    device * rows : (device + 1) * rows, part * width : (part + 1) * width
                ]
            pack_chunk(flags, device, chunk, keep, send)
        note_s[...] = jnp.zeros_like(note_s)
        for row in range(2 * steps):
            part = row % 2
            note_s[row : row + 1] = grad_mod[
                row // 2 : row // 2 + 1, part * width : (part + 1) * width
            ]
        note[...] = note_s[...].astype(bf16)


def finish(
    flags, own_x, far_x, qkv, expo, att, grad_att, grad_x1, mod, w_qkv, g_first, chips
):
    steps, length, width = own_x.shape
    last = width // PAIR - 1
    sum_shape = (chips, up_to(3 * width // (2 * chips), 8), width)
    note_shape = (up_to(2 * steps, 8), width)

    def at(*part):
        return lambda s, flags: (live_at(flags, s, 0, 1)[0],) + part

    def block(where):
        return pl.BlockSpec((1, length, width), where)

    heads = pl.BlockSpec((1, 1, length, PAIR), at(last, 0, 0))
    return call(
        functools.partial(finish_body, steps),
        (steps + 1,),
        [
            block(lambda s, flags: (own_slot(flags, s), 0, 0)),
            block(lambda s, flags: (0, 0, 0)),
            pl.BlockSpec((1, 3, 1, length, PAIR), at(0, last, 0, 0)),
            pl.BlockSpec((1, 2, length, length), at(last, 0, 0)),
            heads, heads, block(at(0, 0)), fixed(mod.shape), fixed(w_qkv.shape),
            pl.BlockSpec((1, last, 3, length, PAIR), at(0, 0, 0, 0)),
        ],
        [
            block(lambda s, flags: (result_slot(flags, s, steps), 0, 0)),
            block(lambda s, flags: (0, 0, 0)),
            fixed(note_shape), fixed(sum_shape), fixed(sum_shape),
        ],
        [
            shape_of((steps, length, width), f32),
            shape_of((1, length, width), bf16),
            shape_of(note_shape, bf16),
            shape_of(sum_shape, f32),
            shape_of(sum_shape, bf16),
        ],
        [
            pltpu.VMEM((3, length, PAIR), bf16),
            pltpu.VMEM((PAIR, length), f32),
            pltpu.VMEM((PAIR, length), f32),
            pltpu.VMEM((width, 3 * width), f32),
            pltpu.VMEM(sum_shape[1:], f32),
            pltpu.VMEM((8, 2 * width), f32),
            pltpu.VMEM(note_shape, f32),
        ],
        "finish", 40 * 10**9,
        (flags, own_x, far_x, qkv, expo, att, grad_att, grad_x1, mod, w_qkv, g_first),
    )


def swap(array, mask):
    count = lax.axis_size("dp")
    return lax.ppermute(array, "dp", [(i, i ^ mask) for i in range(count)])


def tie(value, *others):
    return lax.optimization_barrier((value,) + others)[0]


def chip_groups(chips):
    bits = chips.bit_length() - 1
    return tuple(tuple(range(max(top - 2, 0), top)) for top in range(bits, 0, -2))


def chip_order(chip, chips):
    place, low = 0, 0
    for group in chip_groups(chips):
        place = place | ((chip >> group[0]) & ((1 << len(group)) - 1)) << low
        low += len(group)
    return place


def group_masks(group):
    return [sum(((k >> i) & 1) << b for i, b in enumerate(group)) for k in range(1, 1 << len(group))]


def gather_group(held, group):
    return [held] + [swap(held, mask << 1) for mask in group_masks(group)]


def stage_body(adds, sends, with_notes, held, notes, *refs):
    adds, outs = refs[:adds], refs[adds:]
    parts, rows, _ = held.shape
    size = parts * rows
    keep, joined, outs = outs[0], outs[1], outs[2:]
    own = notes.shape[0]
    joined[:own] = notes[...]
    if adds[0].shape[0] > size:
        for k, add in enumerate(adds):
            joined[(k + 1) * own : (k + 2) * own] = add[size:]
    count = parts // (sends + 1)
    for part in range(parts):
        total = held[part].astype(f32)
        for add in adds:
            total = total + add[part * rows : (part + 1) * rows].astype(f32)
        if part < count:
            keep[part] = total
        else:
            at = part % count * rows
            outs[part // count - 1][at : at + rows] = total.astype(bf16)
    if with_notes:
        for out in outs:
            out[count * rows :] = joined[...]


def stage(held, notes, adds, sends=0, with_notes=True):
    parts, rows, width = held.shape
    extra = adds[0].shape[0] - parts * rows
    count = parts // (sends + 1)
    joined = notes.shape[0] + len(adds) * extra
    size = count * rows + (joined if with_notes else 0)
    keep, joined, *outs = pl.pallas_call(
        functools.partial(stage_body, len(adds), sends, with_notes),
        out_shape=[shape_of((count, rows, width), f32), shape_of((joined, width), bf16)]
        + [shape_of((size, width), bf16)] * sends,
        name="stage",
    )(held, notes, *adds)
    return keep, joined, outs


def reduce_start(group, sums, notes):
    masks = group_masks(group)
    parts = [held.shape[0] // (len(masks) + 1) for held in sums]
    got = []
    for k, mask in enumerate(masks):
        pieces = [held[(k + 1) * n : (k + 2) * n].astype(bf16) for held, n in zip(sums, parts)]
        pieces += notes
        width = pieces[0].shape[-1]
        got.append(swap(jnp.concatenate([p.reshape(-1, width) for p in pieces], 0), mask << 1))
    return [held[:part] for held, part in zip(sums, parts)], notes, got


def reduce_done(totals, notes, got, *after):
    got = lax.optimization_barrier(tuple(got) + after)[: len(got)]
    joined = [[note] for note in notes]
    for block in got:
        start = 0
        for i, piece in enumerate(totals + notes):
            size = math.prod(piece.shape[:-1])
            part = block[start : start + size].reshape(piece.shape)
            start += size
            if i < len(totals):
                totals = totals[:i] + [totals[i] + part.astype(f32)] + totals[i + 1 :]
            else:
                joined[i - len(totals)].append(part)
    return totals, [jnp.concatenate(blocks, 0) for blocks in joined]


def hand_back_body(at, back_out, back_grad, _out, _grad, _after, out, grad, low, high, sems):
    @pl.when(at[0] > 0)
    def _():
        loads = [
            pltpu.make_async_copy(back_grad.at[0], low.at[0], sems.at[0]),
            pltpu.make_async_copy(back_out.at[0], low.at[1], sems.at[1]),
        ]
        for load in loads:
            load.start()
        loads[0].wait()
        high[...] = low[0].astype(f32)
        loads[1].wait()
        stores = [
            pltpu.make_async_copy(high, grad.at[at[1]], sems.at[2]),
            pltpu.make_async_copy(low.at[1], out.at[at[1]], sems.at[3]),
        ]
        for store in stores:
            store.start()
        for store in stores:
            store.wait()


def hand_back(at, back_out, back_grad, own_out, own_grad, after):
    return pl.pallas_call(
        hand_back_body,
        grid_spec=pltpu.PrefetchScalarGridSpec(
            num_scalar_prefetch=1,
            grid=(1,),
            in_specs=[anywhere] * 5,
            out_specs=[anywhere] * 2,
            scratch_shapes=[
                pltpu.VMEM((2,) + own_grad.shape[1:], bf16),
                pltpu.VMEM(own_grad.shape[1:], f32),
                pltpu.SemaphoreType.DMA((4,)),
            ],
        ),
        out_shape=[shape_of(own_out.shape, bf16), shape_of(own_grad.shape, f32)],
        input_output_aliases={3: 0, 4: 1},
        name="hand_back",
    )(at, back_out, back_grad, own_out, own_grad, after)


def condition_body(at, steps, order, *refs):
    pieces, (left, blocks, cond, sems) = refs[:-4], refs[-4:]
    width = cond.shape[1]
    rows = width * steps // cond.shape[0]
    me = lax.axis_index("dp").astype(jnp.int32)
    base = at // 16 * 16
    fetch([piece.at[:, :, pl.ds(base, 16), :] for piece in pieces], blocks, sems)
    at -= base
    for core in range(2):
        for place, (part, other) in enumerate(order):
            start = (core * len(order) + place) * steps
            cond[start : start + steps] = blocks[part, core, other, at : at + steps].astype(f32)
    turned = pltpu.roll(cond[...], lax.rem(width - me * rows, width), 1)[:, :PAIR]
    lane = lax.broadcasted_iota(jnp.int32, turned.shape, 1)
    left[...] = jnp.where(lane < rows, turned, jnp.where(lane == rows, 1.0, 0.0)).astype(bf16)


def condition_columns(pieces, sizes, cond_row, steps):
    _, others, _, width = pieces[0].shape
    chips = len(pieces) * others
    order = []
    for place in range(chips):
        digits, rest = [], place
        for size in sizes:
            digits.append(rest % size)
            rest //= size
        other, low = 0, 1
        for digit, size in zip(reversed(digits[1:]), reversed(sizes[1:])):
            other += digit * low
            low *= size
        order.append((digits[0], other))
    return pl.pallas_call(
        functools.partial(condition_body, cond_row, steps, order),
        in_specs=[anywhere] * len(pieces),
        out_shape=shape_of((2 * chips * steps, PAIR), bf16),
        scratch_shapes=[
            pltpu.VMEM((len(pieces), 2, others, 16, width), bf16),
            pltpu.VMEM((2 * chips * steps, width), f32),
            pltpu.SemaphoreType.DMA((len(pieces),)),
        ],
        name="condition_columns",
    )(*pieces)


def result_body(
    sums1, sums2, left, mine1, other1, mine2, other2,
    ada, b_ada, qkv, out, b_out, up, b_up, down, b_down, ada_sum,
):
    rows, width = out.shape
    ratio = up.shape[1] // width
    me = lax.axis_index("dp").astype(jnp.int32)
    for part in range(3):
        qkv[:, part * width : (part + 1) * width] = sums1[0, part * rows : (part + 1) * rows]
    out[...] = sums2[0, :rows]
    for part in range(ratio):
        up[:, part * width : (part + 1) * width] = sums2[
            0, (1 + part) * rows : (2 + part) * rows
        ]
    after = (1 + 2 * ratio) * rows
    down[...] = sums2[0, after - ratio * rows : after]
    for i, ref in enumerate((b_out, b_up, b_down)):
        size = ref.shape[1]
        line = sums2[0, after + i : after + i + 1]
        shift = lax.rem(width - lax.rem(me * size, width), width)
        ref[...] = pltpu.roll(line, shift, 1)[:, :size]
    half = left.shape[0] // 2
    start = 0
    for count, refs in ((2, (mine1, other1)), (4, (mine2, other2))):
        source = lax.broadcasted_iota(jnp.int32, (half, count * half), 1)
        target = lax.broadcasted_iota(jnp.int32, (half, count * half), 0)
        for part in range(count):
            pick = jnp.where(source == target * count + part, 1.0, 0.0).astype(bf16)
            total = 0.0
            for i, ref in enumerate(refs):
                picked = dot(pick, ref[...]).astype(bf16)
                total = total + dot(left[i * half : (i + 1) * half], picked, 0, 0)
            cols = slice((start + part) * width, (start + part + 1) * width)
            ada[:, cols] = total[:rows]
            ada_sum[:, cols] = total[rows : rows + 1]
        start += count
    b_ada[...] = pltpu.roll(ada_sum[...], lax.rem(6 * width - me * 6 * rows, 6 * width), 1)[
        :, : 6 * rows
    ]


def results(sums1, sums2, left, mine1, other1, mine2, other2, rows, ratio):
    width = sums1.shape[2]
    shapes = [
        (rows, 6 * width), (1, 6 * rows), (rows, 3 * width), (rows, width), (1, rows),
        (rows, ratio * width), (1, ratio * rows), (ratio * rows, width), (1, rows),
    ]
    return pl.pallas_call(
        result_body,
        out_shape=[shape_of(s, f32) for s in shapes],
        scratch_shapes=[pltpu.VMEM((1, 6 * width), f32)],
        name="results",
    )(sums1, sums2, left, mine1, other1, mine2, other2)


def body(
    fields, conditions, step_counts, cotangent,
    w_ada, b_ada, w_qkv, w_out, b_out, w_up, b_up, w_down, b_down,
):
    devices = lax.axis_size("dp")
    chips = devices // 2
    me = lax.axis_index("dp").astype(jnp.int32)
    chip, core = me >> 1, me & 1
    steps, length, width = fields.shape[1:]
    hidden_units = w_up.shape[1]
    ratio = hidden_units // width
    rows = width // devices
    fields, conditions, cotangent = fields[0], conditions[0], cotangent[0]
    groups = chip_groups(chips)

    count = step_counts[0]
    biases = jnp.concatenate([b_ada, b_out, b_up, b_down])[None]
    first, second = pack_shards(w_ada, w_qkv, w_out, w_up, w_down, biases)
    head = jnp.concatenate([conditions, jnp.full((4, width), count, bf16)], 0)
    other_head = swap(tie(head, first), 1)
    other_count = other_head[steps, 0].astype(jnp.int32)
    give = count - other_count >= 2
    take = (other_count - count >= 2).astype(jnp.int32)
    keep = count - give.astype(jnp.int32)
    flags = jnp.stack([keep, take, chip_order(chip, chips), core])
    far_cond = lax.dynamic_index_in_dim(other_head, other_count - 1, 0)
    cond = jnp.concatenate([conditions, jnp.zeros((8 - steps, width), bf16)], 0)
    cond = jnp.where((jnp.arange(8) == keep)[:, None] & (take > 0), far_cond, cond)
    cond_act = jax.nn.silu(cond.astype(f32)).astype(bf16)

    cond_row = (1 + 2 * ratio) * rows
    mine_a = first[None]
    mine_b = lax.dynamic_update_slice_in_dim(second, cond_act[:steps], cond_row, 0)[None]
    for group in groups[:-1]:
        mine_a = jnp.concatenate(gather_group(mine_a, group), 0)
    far_x = swap(tie(lax.dynamic_index_in_dim(fields, count - 1, 0), mine_a), 1)
    far_g = swap(tie(lax.dynamic_index_in_dim(cotangent, count - 1, 0), mine_a), 1)
    for group in groups[:-1]:
        mine_b = jnp.concatenate(gather_group(tie(mine_b, far_x, far_g), group), 0)
    both_b = jnp.stack([mine_b, swap(tie(mine_b, mine_a), 1)])
    mine_a = gather_group(mine_a, groups[-1])
    other_a = [swap(piece, 1) for piece in mine_a]
    back_at = jnp.stack([give.astype(jnp.int32), count - 1])
    first_kernel = lax.optimization_barrier(
        (flags, both_b, far_x, far_g, cond_act, back_at)
    )
    back_at = first_kernel[5]
    qkv, expo, att, inv, mod, bias, full_qkv = attend_forward(
        first_kernel[0], fields, far_x, cond_act, mine_a, other_a, 8 + ratio
    )
    all_b = gather_group(first_kernel[1], groups[-1])
    all_b = lax.optimization_barrier((*all_b, mod))[:-1]
    own_out, far_out, grad_x1, grad_att, note2, keep2, send2 = feed_forward(
        flags, fields, far_x, cotangent, far_g, att, inv, mod, bias, all_b, hidden_units
    )

    up_groups = tuple(reversed(groups))
    late = up_groups[2:]
    masks = [[mask << 1 for mask in group_masks(group)] for group in up_groups]
    left = condition_columns(all_b, [len(m) + 1 for m in masks], cond_row, steps)
    got2 = tie(swap(send2.reshape(-1, width), 1), left)
    held2, note2, sends = stage(keep2, note2, [got2], len(masks[0]))
    gots = [swap(send, mask) for send, mask in zip(sends, masks[0])]
    back_out = swap(far_out, 1)
    g_first = first_pairs(tie(flags, held2), qkv, expo, att, grad_att)
    gots = lax.optimization_barrier((*gots, g_first))[:-1]
    held2, note2, sends = stage(held2, note2, gots, len(masks[1]))
    gots = [swap(send, mask) for send, mask in zip(sends, masks[1])]
    own_grad, far_grad, note1, keep1, send1 = finish(
        tie(flags, held2), fields, far_x, qkv, expo, att, grad_att, grad_x1, mod, full_qkv, g_first,
        chips,
    )
    got1 = swap(send1, 1)
    held1 = keep1 + got1.astype(f32)
    back_grad = swap(tie(far_grad, got1), 1)
    note1 = note1[None]

    going = reduce_start(up_groups[0], [held1], [note1])
    (held1,), (note1,) = reduce_done(*going)
    gots = lax.optimization_barrier((*gots, held1))[:-1]
    held2, note2, sends = stage(held2, note2, gots, len(masks[2]) if late else 0)
    own_out, own_grad = hand_back(
        back_at, back_out, back_grad, own_out, own_grad, held1
    )
    for i, group in enumerate(up_groups[1:]):
        if i > 0:
            gots = [swap(send, mask) for send, mask in zip(sends, masks[i + 1])]
            held2, note2, sends = stage(
                held2, note2, gots, len(masks[i + 2]) if i + 2 < len(masks) else 0
            )
        (held1,), (note1,) = reduce_done(*reduce_start(group, [held1], [note1]))
    note1 = note1.reshape(-1, width)
    other1, other2 = swap(note1, 1), swap(note2, 1)
    grads = results(held1, held2, left, note1, other1, note2, other2, rows, ratio)
    grads = [g[0] if i in (1, 4, 6, 8) else g for i, g in enumerate(grads)]

    return (own_out[None], own_grad[None], *grads)


def solution(mesh):
    item, matrix, vector = P("dp", None, None, None), P("dp", None), P("dp")
    return jax.shard_map(
        body,
        mesh=mesh,
        in_specs=(
            item, P("dp", None, None), vector, item,
            matrix, vector, matrix, matrix, vector, matrix, vector, matrix, vector,
        ),
        out_specs=(
            item, item, matrix, vector, matrix, matrix, vector, matrix, vector, matrix, vector,
        ),
        check_vma=False,
    )
```

```python
import functools
import math

import jax
import jax.numpy as jnp
from jax import lax
from jax.experimental import pallas as pl
from jax.experimental.pallas import tpu as pltpu
from jax.sharding import PartitionSpec as P

HEAD = 64
PAIR = 2 * HEAD
EPS = 1e-6
LOG2E = 1.4426950408889634
VMEM_LIMIT = 60 * 2**20
bf16 = jnp.bfloat16
f32 = jnp.float32
shape_of = jax.ShapeDtypeStruct


def dot(left, right, left_dim=1, right_dim=0):
    return lax.dot_general(
        left, right, (((left_dim,), (right_dim,)), ((), ())), preferred_element_type=f32
    )


def norm(value):
    mean = jnp.mean(value, -1, keepdims=True)
    cent = value - mean
    var = jnp.mean(cent * cent, -1, keepdims=True)
    rstd = lax.rsqrt(var + EPS)
    return cent * rstd, rstd


def row_sum(value):
    return jnp.sum(value, 0, keepdims=True)


def up_to(value, unit):
    return -(-value // unit) * unit


def call(body, grid, in_specs, out_specs, out_shape, scratch, name, flops, args):
    return pl.pallas_call(
        body,
        grid_spec=pltpu.PrefetchScalarGridSpec(
            num_scalar_prefetch=1,
            grid=grid,
            in_specs=in_specs,
            out_specs=out_specs,
            scratch_shapes=scratch,
        ),
        out_shape=out_shape,
        compiler_params=pltpu.CompilerParams(vmem_limit_bytes=VMEM_LIMIT),
        cost_estimate=pl.CostEstimate(flops=flops, bytes_accessed=10**7, transcendentals=0),
        name=name,
    )(*args)


anywhere = pl.BlockSpec(memory_space=pl.ANY)


def fetch(pieces, dest, sems):
    copies = [pltpu.make_async_copy(p, dest.at[k], sems.at[k]) for k, p in enumerate(pieces)]
    for copy in copies:
        copy.start()
    for copy in copies:
        copy.wait()


def fixed(shape):
    return pl.BlockSpec(shape, lambda *at: (0,) * len(shape))


KEEP, TAKE, PLACE, CORE = range(4)


def own_slot(flags, slot):
    return jnp.minimum(slot, flags[KEEP] - 1)


def is_live(flags, slot):
    return slot < flags[KEEP] + flags[TAKE]


def live_at(flags, slot, block, blocks):
    live = flags[KEEP] + flags[TAKE]
    return jnp.minimum(slot, live - 1), jnp.where(slot < live, block, blocks - 1)


def result_slot(flags, slot, steps):
    after = jnp.clip(slot - flags[TAKE], flags[KEEP] - 1, steps - 1)
    return jnp.where(slot < flags[KEEP], slot, after)


def kinds(flags, slot, steps):
    own = slot < flags[KEEP]
    far = (slot == flags[KEEP]) & (flags[TAKE] > 0)
    return own, far, jnp.logical_not(own | far) & (slot - flags[TAKE] < steps)


def pack_body(ada, qkv, out, up, down, bias, first, second, first_s, second_s):
    rows, width = out.shape
    me = lax.axis_index("dp").astype(jnp.int32)
    first_s[...] = jnp.zeros_like(first_s)
    second_s[...] = jnp.zeros_like(second_s)

    def put(dest, start, ref):
        for part in range(ref.shape[1] // width):
            dest[start + part * rows : start + (part + 1) * rows] = ref[
                :, part * width : (part + 1) * width
            ].astype(f32)

    put(first_s, 0, ada)
    put(first_s, 6 * rows, qkv)
    put(second_s, 0, out)
    put(second_s, rows, up)
    after = rows + up.shape[1] * rows // width
    second_s[after : after + down.shape[0]] = down[...].astype(f32)
    source = lax.broadcasted_iota(jnp.int32, (bias.shape[1], width), 0)
    lane = lax.broadcasted_iota(jnp.int32, (bias.shape[1], width), 1)
    start = 0
    for i, count in enumerate((6 * rows, rows, up.shape[1] * rows // width, rows)):
        at = lax.rem(me * count, width) + source - start
        at = jnp.where(at >= width, at - width, at)
        hit = (source >= start) & (source < start + count) & (at == lane)
        first_s[9 * rows + i : 9 * rows + i + 1] = dot(bias[...], jnp.where(hit, 1.0, 0.0).astype(bf16))
        start += count
    first[...] = first_s[...].astype(bf16)
    second[...] = second_s[...].astype(bf16)


def pack_shards(*args):
    _, _, out, up, down, _ = args
    rows, width = out.shape
    sizes = (up_to(9 * rows + 4, 16), up_to(rows + up.shape[1] * rows // width + down.shape[0] + 4, 16))
    return pl.pallas_call(
        pack_body,
        out_shape=[shape_of((n, width), bf16) for n in sizes],
        scratch_shapes=[pltpu.VMEM((n, width), f32) for n in sizes],
        name="pack_shards",
    )(*args)


def each_shard(flags, chips, blocks_of):
    first = flags[CORE] == 0
    for chip in range(chips):
        mine, other = blocks_of(jnp.bitwise_xor(flags[PLACE], chip_order(chip, chips)))
        mine, other = mine.astype(f32), other.astype(f32)
        yield 2 * chip, jnp.where(first, mine, other)
        yield 2 * chip + 1, jnp.where(first, other, mine)


def place_columns(dest, device, block, start, rows, count, width):
    for part in range(count):
        dest[device * rows : (device + 1) * rows, part * width : (part + 1) * width] = block[
            start + part * rows : start + (part + 1) * rows
        ]


def attend_pair(qkv, pair, expo, att, inv):
    length = att.shape[-2]
    row_block = 256
    keys = qkv[0, 1, pair]
    values = qkv[0, 2, pair]
    values_ones = jnp.concatenate([values, jnp.ones_like(values)], 1)
    first = lax.broadcasted_iota(jnp.int32, (row_block, PAIR), 1) < HEAD
    for i in range(length // row_block):
        r = pl.ds(i * row_block, row_block)
        query = qkv[0, 0, pair, r, :]
        outs = []
        for head in range(2):
            sel = first if head == 0 else jnp.logical_not(first)
            scores = dot(jnp.where(sel, query, jnp.zeros_like(query)), keys, 1, 1)
            top = jnp.max(scores, -1, keepdims=True)
            e = jnp.exp2((scores - top) * (0.125 * LOG2E)).astype(bf16)
            expo[0, head, r, :] = e
            outs.append(dot(e, values_ones))
        out = jnp.where(first, outs[0][:, :PAIR], outs[1][:, :PAIR])
        inverse = 1.0 / jnp.where(first, outs[0][:, PAIR:], outs[1][:, PAIR:])
        att[0, 0, r, :] = (out * inverse).astype(bf16)
        inv[0, 0, r, :] = inverse


def attend_forward_body(flags, own_x, far_x, cond, *refs):
    pieces = refs[:-11]
    qkv, expo, att, inv, mod, bias, w_qkv, w_f32, bias_f32, shards, sems = refs[-11:]
    slot = pl.program_id(0)
    pair = pl.program_id(1)
    length, width = own_x.shape[1:]
    group, others = shards.shape[1:3]
    chips = group * others
    rows = width // (2 * chips)
    pairs = width // PAIR

    def blocks_of(place):
        at = lax.div(place, others), lax.rem(place, others)
        return shards[(0, *at)], shards[(1, *at)]

    @pl.when((slot == 0) & (pair == 0))
    def _():
        fetch(pieces[:group], shards.at[0], sems.at[0])
        fetch(pieces[group:], shards.at[1], sems.at[1])
        bias_f32[...] = jnp.zeros_like(bias_f32)
        lane = lax.broadcasted_iota(jnp.int32, (1, width), 1)
        for device, block in each_shard(flags, chips, blocks_of):
            place_columns(w_f32, device, block, 0, rows, 6, width)
            start = 0
            for i, count in enumerate((6 * rows, rows, bias_f32.shape[0] * rows - 8 * rows, rows)):
                low, high = device * count, (device + 1) * count
                for part in range(low // width, (high - 1) // width + 1):
                    at = lane + part * width
                    bias_f32[start + part : start + part + 1] += jnp.where(
                        (at >= low) & (at < high), block[9 * rows + i : 9 * rows + i + 1], 0.0
                    )
                start += 2 * chips * count // width
        for part in range(6):
            cols = slice(part * width, (part + 1) * width)
            mod[:, cols] = dot(cond[...], w_f32[:, cols].astype(bf16)) + bias_f32[part : part + 1]
        for part in range(bias_f32.shape[0] - 6):
            bias[:, part * width : (part + 1) * width] = bias_f32[6 + part : 7 + part]
        for device, block in each_shard(flags, chips, blocks_of):
            place_columns(w_f32, device, block, 6 * rows, rows, 3, width)
        w_qkv[...] = w_f32[:, : 3 * width].astype(bf16)

    @pl.when((pair == 0) & is_live(flags, slot))
    def _():
        shift = mod[pl.ds(slot, 1), :width]
        scale = 1.0 + mod[pl.ds(slot, 1), width : 2 * width]
        row_block = 256

        def project(ref):
            @pl.loop(0, length // row_block)
            def _(i):
                r = pl.ds(pl.multiple_of(i * row_block, row_block), row_block)
                normed, _ = norm(ref[0, r, :].astype(f32))
                h1 = (normed * scale + shift).astype(bf16)
                result = dot(h1, w_qkv[...]).astype(bf16)
                for kind in range(3):
                    for p in range(pairs):
                        at = kind * width + p * PAIR
                        qkv[0, kind, p, r, :] = result[:, at : at + PAIR]

        @pl.when(slot < flags[KEEP])
        def _():
            project(own_x)

        @pl.when(slot >= flags[KEEP])
        def _():
            project(far_x)

    @pl.when(is_live(flags, slot))
    def _():
        attend_pair(qkv, pair, expo, att, inv)


def attend_forward(flags, own_x, far_x, cond, mine, other, bias_rows):
    steps, length, width = own_x.shape
    pairs = width // PAIR
    shards_shape = (2, len(mine)) + mine[0].shape
    args = (flags, own_x, far_x, cond, *mine, *other)

    def at(s, p, flags):
        return live_at(flags, s, p, pairs) + (0, 0)

    whole = pl.BlockSpec((1, 3, pairs, length, PAIR), lambda s, p, flags: (at(s, p, flags)[0], 0, 0, 0, 0))
    part = pl.BlockSpec((1, 1, length, PAIR), at)
    return call(
        attend_forward_body,
        (steps, pairs),
        [
            pl.BlockSpec((1, length, width), lambda s, p, flags: (own_slot(flags, s), 0, 0)),
            fixed(far_x.shape), fixed(cond.shape),
        ] + [anywhere] * (2 * len(mine)),
        [
            whole,
            pl.BlockSpec((1, 2, length, length), at),
            part, part,
            fixed((8, 6 * width)), fixed((1, (bias_rows - 6) * width)), fixed((width, 3 * width)),
        ],
        [
            shape_of((steps, 3, pairs, length, PAIR), bf16),
            shape_of((steps, 2 * pairs, length, length), bf16),
            shape_of((steps, pairs, length, PAIR), bf16),
            shape_of((steps, pairs, length, PAIR), f32),
            shape_of((8, 6 * width), f32),
            shape_of((1, (bias_rows - 6) * width), f32),
            shape_of((width, 3 * width), bf16),
        ],
        [
            pltpu.VMEM((width, 6 * width), f32),
            pltpu.VMEM((bias_rows, width), f32),
            pltpu.VMEM(shards_shape, bf16),
            pltpu.SemaphoreType.DMA((2, len(mine))),
        ],
        "attend_forward", 30 * 10**9, args,
    )


def pack_chunk(flags, device, chunk, keep, send):
    place = jnp.bitwise_xor(flags[PLACE], chip_order(device >> 1, keep.shape[0]))

    @pl.when(flags[CORE] == (device & 1))
    def _():
        keep[place] = chunk[...].astype(keep.dtype)

    @pl.when(flags[CORE] != (device & 1))
    def _():
        send[place] = chunk[...].astype(bf16)


def feed_forward_body(
    steps, flags, own_x, far_x, own_g, far_g, att, inv, mod, bias, *refs
):
    (
        own_out, far_out, grad_x1, grad_att, note, keep, send,
        x_s, g_s, w_out, w_up, w_down, sum_out, sum_up, sum_down_t, down_f32, chunk, bias_sum,
        grad_mod, note_s, shards, sems,
    ) = refs[-22:]
    pieces = refs[:-22]
    slot = pl.program_id(0)
    step = pl.program_id(1)
    own, far, dead = kinds(flags, slot, steps)
    width = x_s.shape[1]
    hidden_units = w_up.shape[1]
    ratio = hidden_units // width
    group, _, others = shards.shape[:3]
    chips = group * others
    rows = width // (2 * chips)

    def blocks_of(place):
        part, place = lax.div(place, others), lax.rem(place, others)
        return shards[part, 0, place], shards[part, 1, place]

    @pl.when((slot == 0) & (step == 0))
    def _():
        fetch(pieces, shards, sems)
        for device, block in each_shard(flags, chips, blocks_of):
            place_columns(sum_out, device, block, 0, rows, 1, width)
            place_columns(sum_up, device, block, rows, rows, ratio, width)
            place_columns(
                down_f32, device, block, (1 + ratio) * rows, ratio * rows, 1, width
            )
        w_out[...] = sum_out[...].astype(bf16)
        w_up[...] = sum_up[...].astype(bf16)
        w_down[...] = down_f32[...].astype(bf16)
        for ref in (sum_out, sum_up, sum_down_t, bias_sum, chunk, grad_mod):
            ref[...] = jnp.zeros_like(ref)

    @pl.when(dead)
    def _():
        own_out[...] = jnp.zeros_like(own_out)

    @pl.when(own)
    def _():
        x_s[...] = own_x[0].astype(f32)
        g_s[...] = own_g[0].astype(f32)

    @pl.when(far)
    def _():
        x_s[...] = far_x[0].astype(f32)
        g_s[...] = far_g[0].astype(f32)

    @pl.when(is_live(flags, slot))
    def _():
        def vector(part):
            return mod[pl.ds(slot, 1), part * width : (part + 1) * width]

        gate1, shift2, scale2, gate2 = vector(2), vector(3), 1.0 + vector(4), vector(5)
        b_out = bias[:, :width]
        b_up = bias[:, width : width + hidden_units]
        b_down = bias[:, width + hidden_units :]

        def lanes(ref):
            return jnp.concatenate([ref[0, p] for p in range(ref.shape[1])], 1)

        attended = lanes(att)
        branch1 = dot(attended, w_out[...]) + b_out
        x1 = x_s[...] + gate1 * branch1
        normed2, rstd = norm(x1)
        h2 = (normed2 * scale2 + shift2).astype(bf16)
        pre = dot(h2, w_up[...]) + b_up
        cdf = 0.5 * (1.0 + lax.erf(pre * (1 / math.sqrt(2.0))))
        hidden = (pre * cdf).astype(bf16)
        slope = cdf + pre * jnp.exp2(pre * pre * (-0.5 * LOG2E)) * (1 / math.sqrt(2 * math.pi))
        branch2 = dot(hidden, w_down[...]) + b_down
        result = (x1 + gate2 * branch2).astype(bf16)

        @pl.when(own)
        def _():
            own_out[0] = result

        @pl.when(far)
        def _():
            far_out[0] = result

        grad = g_s[...]
        grad_b2 = (gate2 * grad).astype(bf16)
        grad_pre = (dot(grad_b2, w_down[...], 1, 1) * slope).astype(bf16)
        grad_h2 = dot(grad_pre, w_up[...], 1, 1)
        grad_n = grad_h2 * scale2
        g_x1 = grad + rstd * (
            grad_n
            - jnp.mean(grad_n, -1, keepdims=True)
            - normed2 * jnp.mean(grad_n * normed2, -1, keepdims=True)
        )
        grad_b1 = (gate1 * g_x1).astype(bf16)
        grad_x1[0] = g_x1
        g_att = (dot(grad_b1, w_out[...], 1, 1) * lanes(inv)).astype(bf16)
        for p in range(width // PAIR):
            grad_att[0, p] = g_att[:, p * PAIR : (p + 1) * PAIR]

        def add_mod(part, value):
            grad_mod[pl.ds(slot, 1), part * width : (part + 1) * width] += row_sum(value)

        add_mod(0, g_x1 * branch1)
        add_mod(1, grad_h2)
        add_mod(2, grad_h2 * normed2)
        add_mod(3, grad * branch2)
        sum_out[...] += dot(attended, grad_b1, 0, 0)
        sum_up[...] += dot(h2, grad_pre, 0, 0)
        sum_down_t[...] += dot(grad_b2, hidden, 0, 0)
        bias_sum[:, :width] += row_sum(grad_b1.astype(f32))
        bias_sum[:, width : width + hidden_units] += row_sum(grad_pre.astype(f32))
        bias_sum[:, width + hidden_units :] += row_sum(grad_b2.astype(f32))

    @pl.when((slot == pl.num_programs(0) - 1) & (step == pl.num_programs(1) - 1))
    def _():
        down_f32[...] = sum_down_t[...].T
        for device in range(2 * chips):
            span = slice(device * rows, (device + 1) * rows)
            chunk[:rows] = sum_out[span]
            for part in range(ratio):
                chunk[(1 + part) * rows : (2 + part) * rows] = sum_up[
                    span, part * width : (part + 1) * width
                ]
            chunk[(1 + ratio) * rows : (1 + 2 * ratio) * rows] = down_f32[
                device * ratio * rows : (device + 1) * ratio * rows
            ]
            up_row = 1 + device * ratio * rows // width
            for i, part in enumerate((0, up_row, 1 + ratio)):
                at = (1 + 2 * ratio) * rows + i
                chunk[at : at + 1] = bias_sum[:, part * width : (part + 1) * width]
            pack_chunk(flags, device, chunk, keep, send)
        note_s[...] = jnp.zeros_like(note_s)
        for row in range(4 * steps):
            part = row % 4
            note_s[row : row + 1] = grad_mod[
                row // 4 : row // 4 + 1, part * width : (part + 1) * width
            ]
        note[...] = note_s[...].astype(bf16)


def feed_forward(
    flags, own_x, far_x, own_g, far_g, att, inv, mod, bias, shards, hidden_units
):
    steps, length, width = own_x.shape
    row_block = 1024
    blocks = length // row_block
    group, others = len(shards), shards[0].shape[1]
    rows = width // (2 * group * others)
    ratio = hidden_units // width
    packed_rows = up_to((1 + 2 * ratio) * rows + 3, 16)
    sum_shape = (group * others, packed_rows, width)
    note_shape = (up_to(4 * steps, 16), width)

    def own(s, b, flags):
        return (own_slot(flags, s), jnp.where(s < flags[KEEP], b, blocks - 1), 0)

    def far(s, b, flags):
        keep = flags[KEEP]
        return (0, jnp.where(s < keep, 0, jnp.where(s == keep, b, blocks - 1)), 0)

    def live(s, b, flags):
        return live_at(flags, s, b, blocks) + (0,)

    def live_parts(s, b, flags):
        at, part = live_at(flags, s, b, blocks)
        return (at, 0, part, 0)

    def own_result(s, b, flags):
        own, _, dead = kinds(flags, s, steps)
        return (result_slot(flags, s, steps), jnp.where(own | dead, b, blocks - 1), 0)

    def block(where):
        return pl.BlockSpec((1, row_block, width), where)

    def parts(count):
        return pl.BlockSpec((1, count, row_block, PAIR), live_parts)

    pairs = width // PAIR
    args = (flags, own_x, far_x, own_g, far_g, att, inv, mod, bias, *shards)
    return call(
        functools.partial(feed_forward_body, steps),
        (steps + 1, blocks),
        [
            block(own), block(far), block(own), block(far), parts(pairs), parts(pairs),
            fixed(mod.shape), fixed(bias.shape),
        ] + [anywhere] * group,
        [
            block(own_result), block(far), block(live), parts(pairs),
            fixed(note_shape), fixed(sum_shape), fixed(sum_shape),
        ],
        [
            shape_of((steps, length, width), bf16),
            shape_of((1, length, width), bf16),
            shape_of((steps, length, width), f32),
            shape_of((steps, pairs, length, PAIR), bf16),
            shape_of(note_shape, bf16),
            shape_of(sum_shape, bf16),
            shape_of(sum_shape, bf16),
        ],
        [
            pltpu.VMEM((row_block, width), f32),
            pltpu.VMEM((row_block, width), f32),
            pltpu.VMEM((width, width), bf16),
            pltpu.VMEM((width, hidden_units), bf16),
            pltpu.VMEM((hidden_units, width), bf16),
            pltpu.VMEM((width, width), f32),
            pltpu.VMEM((width, hidden_units), f32),
            pltpu.VMEM((width, hidden_units), f32),
            pltpu.VMEM((hidden_units, width), f32),
            pltpu.VMEM((packed_rows, width), f32),
            pltpu.VMEM(bias.shape, f32),
            pltpu.VMEM((8, 4 * width), f32),
            pltpu.VMEM(note_shape, f32),
            pltpu.VMEM((group,) + shards[0].shape, bf16),
            pltpu.SemaphoreType.DMA((group,)),
        ],
        "feed_forward", 60 * 10**9, args,
    )


def attend_backward_pair(qkv, expo, att, grad_att, g_qkv, keys_t, values_t):
    length = att.shape[2]
    row_block = 512
    keys = qkv[0, 1, 0]
    values = qkv[0, 2, 0]
    values_ones = jnp.concatenate([values, jnp.ones_like(values)], 1)
    lane = lax.broadcasted_iota(jnp.int32, (row_block, PAIR), 1)
    first = lane < HEAD
    for i in range(length // row_block):
        r = pl.ds(i * row_block, row_block)
        query = qkv[0, 0, 0, r, :]
        g_att = grad_att[0, 0, r, :]
        product = g_att.astype(f32) * att[0, 0, r, :].astype(f32)
        query_t = query.T
        g_att_t = g_att.T
        grads_q = []
        for head in range(2):
            sel = first if head == 0 else jnp.logical_not(first)
            delta = jnp.sum(jnp.where(sel, product, 0.0), -1, keepdims=True)
            high = delta.astype(bf16).astype(f32)
            extra = jnp.where(
                lane == 0, -high, jnp.where(lane == 1, high - delta, 0.0)
            ).astype(bf16)
            left = jnp.concatenate([jnp.where(sel, g_att, jnp.zeros_like(g_att)), extra], 1)
            e = expo[0, head, r, :]
            grad_s = e * dot(left, values_ones, 1, 1).astype(bf16)
            grads_q.append(dot(grad_s, keys))
            span = slice(head * HEAD, (head + 1) * HEAD)
            add_k = dot(query_t[span], grad_s)
            add_v = dot(g_att_t[span], e)
            if i == 0:
                keys_t[span] = add_k
                values_t[span] = add_v
            else:
                keys_t[span] += add_k
                values_t[span] += add_v
        g_qkv[0, r, :] = (jnp.where(first, grads_q[0], grads_q[1]) * 0.125).astype(bf16)
    g_qkv[1] = (keys_t[...] * 0.125).astype(bf16).T
    g_qkv[2] = values_t[...].astype(bf16).T


def first_pairs_body(flags, qkv, expo, att, grad_att, g_qkv, keys_t, values_t):
    @pl.when(is_live(flags, pl.program_id(0)))
    def _():
        attend_backward_pair(qkv, expo, att, grad_att, g_qkv.at[0, 0], keys_t, values_t)


def first_pairs(flags, qkv, expo, att, grad_att):
    steps, _, pairs, length, _ = qkv.shape
    pairs -= 1

    def part(s, p, flags):
        return live_at(flags, s, p, pairs) + (0, 0)

    def qkv_at(s, p, flags):
        at, pair = live_at(flags, s, p, pairs)
        return (at, 0, pair, 0, 0)

    heads = pl.BlockSpec((1, 1, length, PAIR), part)
    return call(
        first_pairs_body,
        (steps, pairs),
        [
            pl.BlockSpec((1, 3, 1, length, PAIR), qkv_at),
            pl.BlockSpec((1, 2, length, length), part),
            heads, heads,
        ],
        pl.BlockSpec((1, 1, 3, length, PAIR), lambda s, p, flags: part(s, p, flags) + (0,)),
        shape_of((steps, pairs, 3, length, PAIR), bf16),
        [pltpu.VMEM((PAIR, length), f32), pltpu.VMEM((PAIR, length), f32)],
        "first_pairs", 40 * 10**9, (flags, qkv, expo, att, grad_att),
    )


def finish_body(
    steps, flags, own_x, far_x, qkv, expo, att, grad_att, grad_x1, mod, w_qkv, g_first,
    own_grad, far_grad, note, keep, send, g_last, keys_t, values_t, sum_qkv, chunk, grad_mod, note_s,
):
    slot = pl.program_id(0)
    own, far, dead = kinds(flags, slot, steps)
    length, width = own_x.shape[1:]
    chips = keep.shape[0]
    rows = width // (2 * chips)

    @pl.when(slot == 0)
    def _():
        for ref in (sum_qkv, chunk, grad_mod):
            ref[...] = jnp.zeros_like(ref)

    @pl.when(dead)
    def _():
        own_grad[...] = jnp.zeros_like(own_grad)

    @pl.when(is_live(flags, slot))
    def _():
        attend_backward_pair(qkv, expo, att, grad_att, g_last, keys_t, values_t)

    def finish(x_ref, out_ref):
        shift = mod[pl.ds(slot, 1), :width]
        scale = 1.0 + mod[pl.ds(slot, 1), width : 2 * width]
        row_block = 512
        for i in range(length // row_block):
            r = pl.ds(i * row_block, row_block)
            normed, rstd = norm(x_ref[0, r, :].astype(f32))
            h1 = (normed * scale + shift).astype(bf16)
            grad = []
            for kind in range(3):
                grad += [g_first[0, p, kind, r, :] for p in range(g_first.shape[1])]
                grad.append(g_last[kind, r, :])
            grad = jnp.concatenate(grad, 1)
            grad_h1 = dot(grad, w_qkv[...], 1, 1)
            sum_qkv[...] += dot(h1, grad, 0, 0)
            grad_mod[pl.ds(slot, 1), :width] += row_sum(grad_h1)
            grad_mod[pl.ds(slot, 1), width:] += row_sum(grad_h1 * normed)
            grad_n = grad_h1 * scale
            out_ref[0, r, :] = (
                grad_x1[0, r, :]
                + rstd
                * (
                    grad_n
                    - jnp.mean(grad_n, -1, keepdims=True)
                    - normed * jnp.mean(grad_n * normed, -1, keepdims=True)
                )
            ).astype(out_ref.dtype)

    @pl.when(own)
    def _():
        finish(own_x, own_grad)

    @pl.when(far)
    def _():
        finish(far_x, far_grad)

    @pl.when(slot == steps)
    def _():
        for device in range(2 * chips):
            for part in range(3):
                chunk[part * rows : (part + 1) * rows] = sum_qkv[
                    device * rows : (device + 1) * rows, part * width : (part + 1) * width
                ]
            pack_chunk(flags, device, chunk, keep, send)
        note_s[...] = jnp.zeros_like(note_s)
        for row in range(2 * steps):
            part = row % 2
            note_s[row : row + 1] = grad_mod[
                row // 2 : row // 2 + 1, part * width : (part + 1) * width
            ]
        note[...] = note_s[...].astype(bf16)


def finish(
    flags, own_x, far_x, qkv, expo, att, grad_att, grad_x1, mod, w_qkv, g_first, chips
):
    steps, length, width = own_x.shape
    last = width // PAIR - 1
    sum_shape = (chips, up_to(3 * width // (2 * chips), 8), width)
    note_shape = (up_to(2 * steps, 8), width)

    def at(*part):
        return lambda s, flags: (live_at(flags, s, 0, 1)[0],) + part

    def block(where):
        return pl.BlockSpec((1, length, width), where)

    heads = pl.BlockSpec((1, 1, length, PAIR), at(last, 0, 0))
    return call(
        functools.partial(finish_body, steps),
        (steps + 1,),
        [
            block(lambda s, flags: (own_slot(flags, s), 0, 0)),
            block(lambda s, flags: (0, 0, 0)),
            pl.BlockSpec((1, 3, 1, length, PAIR), at(0, last, 0, 0)),
            pl.BlockSpec((1, 2, length, length), at(last, 0, 0)),
            heads, heads, block(at(0, 0)), fixed(mod.shape), fixed(w_qkv.shape),
            pl.BlockSpec((1, last, 3, length, PAIR), at(0, 0, 0, 0)),
        ],
        [
            block(lambda s, flags: (result_slot(flags, s, steps), 0, 0)),
            block(lambda s, flags: (0, 0, 0)),
            fixed(note_shape), fixed(sum_shape), fixed(sum_shape),
        ],
        [
            shape_of((steps, length, width), f32),
            shape_of((1, length, width), bf16),
            shape_of(note_shape, bf16),
            shape_of(sum_shape, f32),
            shape_of(sum_shape, bf16),
        ],
        [
            pltpu.VMEM((3, length, PAIR), bf16),
            pltpu.VMEM((PAIR, length), f32),
            pltpu.VMEM((PAIR, length), f32),
            pltpu.VMEM((width, 3 * width), f32),
            pltpu.VMEM(sum_shape[1:], f32),
            pltpu.VMEM((8, 2 * width), f32),
            pltpu.VMEM(note_shape, f32),
        ],
        "finish", 40 * 10**9,
        (flags, own_x, far_x, qkv, expo, att, grad_att, grad_x1, mod, w_qkv, g_first),
    )


def swap(array, mask):
    count = lax.axis_size("dp")
    return lax.ppermute(array, "dp", [(i, i ^ mask) for i in range(count)])


def tie(value, *others):
    return lax.optimization_barrier((value,) + others)[0]


def chip_groups(chips):
    bits = chips.bit_length() - 1
    return tuple(tuple(range(max(top - 2, 0), top)) for top in range(bits, 0, -2))


def chip_order(chip, chips):
    place, low = 0, 0
    for group in chip_groups(chips):
        place = place | ((chip >> group[0]) & ((1 << len(group)) - 1)) << low
        low += len(group)
    return place


def group_masks(group):
    return [sum(((k >> i) & 1) << b for i, b in enumerate(group)) for k in range(1, 1 << len(group))]


def gather_group(held, group):
    return [held] + [swap(held, mask << 1) for mask in group_masks(group)]


def stage_body(adds, sends, with_notes, held, notes, *refs):
    adds, outs = refs[:adds], refs[adds:]
    parts, rows, _ = held.shape
    size = parts * rows
    keep, joined, outs = outs[0], outs[1], outs[2:]
    own = notes.shape[0]
    joined[:own] = notes[...]
    if adds[0].shape[0] > size:
        for k, add in enumerate(adds):
            joined[(k + 1) * own : (k + 2) * own] = add[size:]
    count = parts // (sends + 1)
    for part in range(parts):
        total = held[part].astype(f32)
        for add in adds:
            total = total + add[part * rows : (part + 1) * rows].astype(f32)
        if part < count:
            keep[part] = total
        else:
            at = part % count * rows
            outs[part // count - 1][at : at + rows] = total.astype(bf16)
    if with_notes:
        for out in outs:
            out[count * rows :] = joined[...]


def stage(held, notes, adds, sends=0, with_notes=True):
    parts, rows, width = held.shape
    extra = adds[0].shape[0] - parts * rows
    count = parts // (sends + 1)
    joined = notes.shape[0] + len(adds) * extra
    size = count * rows + (joined if with_notes else 0)
    keep, joined, *outs = pl.pallas_call(
        functools.partial(stage_body, len(adds), sends, with_notes),
        out_shape=[shape_of((count, rows, width), f32), shape_of((joined, width), bf16)]
        + [shape_of((size, width), bf16)] * sends,
        name="stage",
    )(held, notes, *adds)
    return keep, joined, outs


def reduce_start(group, sums, notes):
    masks = group_masks(group)
    parts = [held.shape[0] // (len(masks) + 1) for held in sums]
    got = []
    for k, mask in enumerate(masks):
        pieces = [held[(k + 1) * n : (k + 2) * n].astype(bf16) for held, n in zip(sums, parts)]
        pieces += notes
        width = pieces[0].shape[-1]
        got.append(swap(jnp.concatenate([p.reshape(-1, width) for p in pieces], 0), mask << 1))
    return [held[:part] for held, part in zip(sums, parts)], notes, got


def reduce_done(totals, notes, got, *after):
    got = lax.optimization_barrier(tuple(got) + after)[: len(got)]
    joined = [[note] for note in notes]
    for block in got:
        start = 0
        for i, piece in enumerate(totals + notes):
            size = math.prod(piece.shape[:-1])
            part = block[start : start + size].reshape(piece.shape)
            start += size
            if i < len(totals):
                totals = totals[:i] + [totals[i] + part.astype(f32)] + totals[i + 1 :]
            else:
                joined[i - len(totals)].append(part)
    return totals, [jnp.concatenate(blocks, 0) for blocks in joined]


def hand_back_body(at, back_out, back_grad, _out, _grad, _after, out, grad, done, low, high, sems):
    done[...] = jnp.zeros_like(done)

    @pl.when(at[0] > 0)
    def _():
        loads = [
            pltpu.make_async_copy(back_grad.at[0], low.at[0], sems.at[0]),
            pltpu.make_async_copy(back_out.at[0], low.at[1], sems.at[1]),
        ]
        for load in loads:
            load.start()
        loads[0].wait()
        high[...] = low[0].astype(f32)
        loads[1].wait()
        stores = [
            pltpu.make_async_copy(high, grad.at[at[1]], sems.at[2]),
            pltpu.make_async_copy(low.at[1], out.at[at[1]], sems.at[3]),
        ]
        for store in stores:
            store.start()
        for store in stores:
            store.wait()


def hand_back(at, back_out, back_grad, own_out, own_grad, after):
    return pl.pallas_call(
        hand_back_body,
        grid_spec=pltpu.PrefetchScalarGridSpec(
            num_scalar_prefetch=1,
            grid=(1,),
            in_specs=[anywhere] * 5,
            out_specs=[anywhere] * 2 + [fixed((8, 128))],
            scratch_shapes=[
                pltpu.VMEM((2,) + own_grad.shape[1:], bf16),
                pltpu.VMEM(own_grad.shape[1:], f32),
                pltpu.SemaphoreType.DMA((4,)),
            ],
        ),
        out_shape=[
            shape_of(own_out.shape, bf16), shape_of(own_grad.shape, f32), shape_of((8, 128), f32),
        ],
        input_output_aliases={3: 0, 4: 1},
        name="hand_back",
    )(at, back_out, back_grad, own_out, own_grad, after)


def condition_body(at, steps, order, *refs):
    pieces, (left, blocks, cond, sems) = refs[:-4], refs[-4:]
    width = cond.shape[1]
    rows = width * steps // cond.shape[0]
    me = lax.axis_index("dp").astype(jnp.int32)
    base = at // 16 * 16
    fetch([piece.at[:, :, pl.ds(base, 16), :] for piece in pieces], blocks, sems)
    at -= base
    for core in range(2):
        for place, (part, other) in enumerate(order):
            start = (core * len(order) + place) * steps
            cond[start : start + steps] = blocks[part, core, other, at : at + steps].astype(f32)
    turned = pltpu.roll(cond[...], lax.rem(width - me * rows, width), 1)[:, :PAIR]
    lane = lax.broadcasted_iota(jnp.int32, turned.shape, 1)
    left[...] = jnp.where(lane < rows, turned, jnp.where(lane == rows, 1.0, 0.0)).astype(bf16)


def condition_columns(pieces, sizes, cond_row, steps):
    _, others, _, width = pieces[0].shape
    chips = len(pieces) * others
    order = []
    for place in range(chips):
        digits, rest = [], place
        for size in sizes:
            digits.append(rest % size)
            rest //= size
        other, low = 0, 1
        for digit, size in zip(reversed(digits[1:]), reversed(sizes[1:])):
            other += digit * low
            low *= size
        order.append((digits[0], other))
    return pl.pallas_call(
        functools.partial(condition_body, cond_row, steps, order),
        in_specs=[anywhere] * len(pieces),
        out_shape=shape_of((2 * chips * steps, PAIR), bf16),
        scratch_shapes=[
            pltpu.VMEM((len(pieces), 2, others, 16, width), bf16),
            pltpu.VMEM((2 * chips * steps, width), f32),
            pltpu.SemaphoreType.DMA((len(pieces),)),
        ],
        name="condition_columns",
    )(*pieces)


def result_body(
    sums1, sums2, left, mine1, other1, mine2, other2, _done,
    ada, b_ada, qkv, out, b_out, up, b_up, down, b_down, ada_sum,
):
    rows, width = out.shape
    ratio = up.shape[1] // width
    me = lax.axis_index("dp").astype(jnp.int32)
    for part in range(3):
        qkv[:, part * width : (part + 1) * width] = sums1[0, part * rows : (part + 1) * rows]
    out[...] = sums2[0, :rows]
    for part in range(ratio):
        up[:, part * width : (part + 1) * width] = sums2[
            0, (1 + part) * rows : (2 + part) * rows
        ]
    after = (1 + 2 * ratio) * rows
    down[...] = sums2[0, after - ratio * rows : after]
    for i, ref in enumerate((b_out, b_up, b_down)):
        size = ref.shape[1]
        line = sums2[0, after + i : after + i + 1]
        shift = lax.rem(width - lax.rem(me * size, width), width)
        ref[...] = pltpu.roll(line, shift, 1)[:, :size]
    half = left.shape[0] // 2
    start = 0
    for count, refs in ((2, (mine1, other1)), (4, (mine2, other2))):
        source = lax.broadcasted_iota(jnp.int32, (half, count * half), 1)
        target = lax.broadcasted_iota(jnp.int32, (half, count * half), 0)
        for part in range(count):
            pick = jnp.where(source == target * count + part, 1.0, 0.0).astype(bf16)
            total = 0.0
            for i, ref in enumerate(refs):
                picked = dot(pick, ref[...]).astype(bf16)
                total = total + dot(left[i * half : (i + 1) * half], picked, 0, 0)
            cols = slice((start + part) * width, (start + part + 1) * width)
            ada[:, cols] = total[:rows]
            ada_sum[:, cols] = total[rows : rows + 1]
        start += count
    b_ada[...] = pltpu.roll(ada_sum[...], lax.rem(6 * width - me * 6 * rows, 6 * width), 1)[
        :, : 6 * rows
    ]


def results(sums1, sums2, left, mine1, other1, mine2, other2, done, rows, ratio):
    width = sums1.shape[2]
    shapes = [
        (rows, 6 * width), (1, 6 * rows), (rows, 3 * width), (rows, width), (1, rows),
        (rows, ratio * width), (1, ratio * rows), (ratio * rows, width), (1, rows),
    ]
    return pl.pallas_call(
        result_body,
        out_shape=[shape_of(s, f32) for s in shapes],
        scratch_shapes=[pltpu.VMEM((1, 6 * width), f32)],
        name="results",
    )(sums1, sums2, left, mine1, other1, mine2, other2, done)


def body(
    fields, conditions, step_counts, cotangent,
    w_ada, b_ada, w_qkv, w_out, b_out, w_up, b_up, w_down, b_down,
):
    devices = lax.axis_size("dp")
    chips = devices // 2
    me = lax.axis_index("dp").astype(jnp.int32)
    chip, core = me >> 1, me & 1
    steps, length, width = fields.shape[1:]
    hidden_units = w_up.shape[1]
    ratio = hidden_units // width
    rows = width // devices
    fields, conditions, cotangent = fields[0], conditions[0], cotangent[0]
    groups = chip_groups(chips)

    count = step_counts[0]
    biases = jnp.concatenate([b_ada, b_out, b_up, b_down])[None]
    first, second = pack_shards(w_ada, w_qkv, w_out, w_up, w_down, biases)
    head = jnp.concatenate([conditions, jnp.full((4, width), count, bf16)], 0)
    other_head = swap(tie(head, first), 1)
    other_count = other_head[steps, 0].astype(jnp.int32)
    give = count - other_count >= 2
    take = (other_count - count >= 2).astype(jnp.int32)
    keep = count - give.astype(jnp.int32)
    flags = jnp.stack([keep, take, chip_order(chip, chips), core])
    far_cond = lax.dynamic_index_in_dim(other_head, other_count - 1, 0)
    cond = jnp.concatenate([conditions, jnp.zeros((8 - steps, width), bf16)], 0)
    cond = jnp.where((jnp.arange(8) == keep)[:, None] & (take > 0), far_cond, cond)
    cond_act = jax.nn.silu(cond.astype(f32)).astype(bf16)

    cond_row = (1 + 2 * ratio) * rows
    mine_a = first[None]
    mine_b = lax.dynamic_update_slice_in_dim(second, cond_act[:steps], cond_row, 0)[None]
    for group in groups[:-1]:
        pieces = lax.optimization_barrier((*gather_group(mine_a, group), cond_act, flags))[:-2]
        mine_a = jnp.concatenate(pieces, 0)
    far_x = swap(tie(lax.dynamic_index_in_dim(fields, count - 1, 0), mine_a), 1)
    far_g = swap(tie(lax.dynamic_index_in_dim(cotangent, count - 1, 0), mine_a), 1)
    for group in groups[:-1]:
        mine_b = jnp.concatenate(gather_group(tie(mine_b, far_x, far_g), group), 0)
    both_b = jnp.stack([mine_b, swap(tie(mine_b, mine_a), 1)])
    mine_a = gather_group(mine_a, groups[-1])
    other_a = [swap(piece, 1) for piece in mine_a]
    back_at = jnp.stack([give.astype(jnp.int32), count - 1])
    first_kernel = lax.optimization_barrier(
        (flags, both_b, far_x, far_g, cond_act, back_at)
    )
    back_at = first_kernel[5]
    qkv, expo, att, inv, mod, bias, full_qkv = attend_forward(
        first_kernel[0], fields, far_x, cond_act, mine_a, other_a, 8 + ratio
    )
    all_b = gather_group(first_kernel[1], groups[-1])
    all_b = lax.optimization_barrier((*all_b, mod))[:-1]
    own_out, far_out, grad_x1, grad_att, note2, keep2, send2 = feed_forward(
        flags, fields, far_x, cotangent, far_g, att, inv, mod, bias, all_b, hidden_units
    )

    up_groups = tuple(reversed(groups))
    late = up_groups[2:]
    masks = [[mask << 1 for mask in group_masks(group)] for group in up_groups]
    left = condition_columns(all_b, [len(m) + 1 for m in masks], cond_row, steps)
    got2 = tie(swap(send2.reshape(-1, width), 1), left)
    held2, note2, sends = stage(keep2, note2, [got2], len(masks[0]))
    gots = [swap(send, mask) for send, mask in zip(sends, masks[0])]
    back_out = swap(far_out, 1)
    g_first = first_pairs(tie(flags, held2), qkv, expo, att, grad_att)
    gots = lax.optimization_barrier((*gots, g_first))[:-1]
    held2, note2, sends = stage(held2, note2, gots, len(masks[1]))
    gots = [swap(send, mask) for send, mask in zip(sends, masks[1])]
    own_grad, far_grad, note1, keep1, send1 = finish(
        tie(flags, held2, back_out), fields, far_x, qkv, expo, att, grad_att, grad_x1, mod, full_qkv, g_first,
        chips,
    )
    got1 = swap(send1, 1)
    gots = lax.optimization_barrier((*gots, keep1))[:-1]
    held2, note2, sends = stage(held2, note2, gots, len(masks[2]) if late else 0)
    held1 = keep1 + got1.astype(f32)
    back_grad = swap(far_grad, 1)
    note1 = note1[None]

    going = reduce_start(up_groups[0], [held1], [note1])
    (held1,), (note1,) = reduce_done(*going, back_grad)
    own_out, own_grad, done = hand_back(
        back_at, back_out, back_grad, own_out, own_grad, held1
    )
    for i, group in enumerate(up_groups[1:]):
        if i > 0:
            gots = [swap(send, mask) for send, mask in zip(sends, masks[i + 1])]
            held2, note2, sends = stage(
                held2, note2, gots, len(masks[i + 2]) if i + 2 < len(masks) else 0
            )
        (held1,), (note1,) = reduce_done(*reduce_start(group, [held1], [note1]))
    note1 = note1.reshape(-1, width)
    other1, other2 = swap(note1, 1), swap(note2, 1)
    grads = results(held1, held2, left, note1, other1, note2, other2, done, rows, ratio)
    grads = [g[0] if i in (1, 4, 6, 8) else g for i, g in enumerate(grads)]

    return (own_out[None], own_grad[None], *grads)


def solution(mesh):
    item, matrix, vector = P("dp", None, None, None), P("dp", None), P("dp")
    return jax.shard_map(
        body,
        mesh=mesh,
        in_specs=(
            item, P("dp", None, None), vector, item,
            matrix, vector, matrix, matrix, vector, matrix, vector, matrix, vector,
        ),
        out_specs=(
            item, item, matrix, vector, matrix, matrix, vector, matrix, vector, matrix, vector,
        ),
        check_vma=False,
    )
```

```python
import functools
import math

import jax
import jax.numpy as jnp
from jax import lax
from jax.experimental import pallas as pl
from jax.experimental.pallas import tpu as pltpu
from jax.sharding import PartitionSpec as P

HEAD = 64
PAIR = 2 * HEAD
EPS = 1e-6
LOG2E = 1.4426950408889634
VMEM_LIMIT = 63 * 2**20
bf16 = jnp.bfloat16
f32 = jnp.float32
shape_of = jax.ShapeDtypeStruct


def dot(left, right, left_dim=1, right_dim=0):
    return lax.dot_general(
        left, right, (((left_dim,), (right_dim,)), ((), ())), preferred_element_type=f32
    )


def norm(value):
    mean = jnp.mean(value, -1, keepdims=True)
    cent = value - mean
    var = jnp.mean(cent * cent, -1, keepdims=True)
    rstd = lax.rsqrt(var + EPS)
    return cent * rstd, rstd


def row_sum(value):
    return jnp.sum(value, 0, keepdims=True)


def up_to(value, unit):
    return -(-value // unit) * unit


def call(body, grid, in_specs, out_specs, out_shape, scratch, name, flops, args):
    return pl.pallas_call(
        body,
        grid_spec=pltpu.PrefetchScalarGridSpec(
            num_scalar_prefetch=1,
            grid=grid,
            in_specs=in_specs,
            out_specs=out_specs,
            scratch_shapes=scratch,
        ),
        out_shape=out_shape,
        compiler_params=pltpu.CompilerParams(vmem_limit_bytes=VMEM_LIMIT),
        cost_estimate=pl.CostEstimate(flops=flops, bytes_accessed=10**7, transcendentals=0),
        name=name,
    )(*args)


anywhere = pl.BlockSpec(memory_space=pl.ANY)


def fetch(pieces, dest, sems):
    copies = [pltpu.make_async_copy(p, dest.at[k], sems.at[k]) for k, p in enumerate(pieces)]
    for copy in copies:
        copy.start()
    for copy in copies:
        copy.wait()


def fixed(shape):
    return pl.BlockSpec(shape, lambda *at: (0,) * len(shape))


KEEP, TAKE, PLACE, CORE = range(4)


def own_slot(flags, slot):
    return jnp.minimum(slot, flags[KEEP] - 1)


def is_live(flags, slot):
    return slot < flags[KEEP] + flags[TAKE]


def live_at(flags, slot, block, blocks):
    live = flags[KEEP] + flags[TAKE]
    return jnp.minimum(slot, live - 1), jnp.where(slot < live, block, blocks - 1)


def result_slot(flags, slot, steps):
    after = jnp.clip(slot - flags[TAKE], flags[KEEP] - 1, steps - 1)
    return jnp.where(slot < flags[KEEP], slot, after)


def kinds(flags, slot, steps):
    own = slot < flags[KEEP]
    far = (slot == flags[KEEP]) & (flags[TAKE] > 0)
    return own, far, jnp.logical_not(own | far) & (slot - flags[TAKE] < steps)


def pack_body(ada, qkv, out, up, down, b_ada, b_out, b_up, b_down, first, second, first_s, second_s):
    rows, width = out.shape
    me = lax.axis_index("dp").astype(jnp.int32)
    first_s[...] = jnp.zeros_like(first_s)
    second_s[...] = jnp.zeros_like(second_s)

    def put(dest, start, ref):
        for part in range(ref.shape[1] // width):
            dest[start + part * rows : start + (part + 1) * rows] = ref[
                :, part * width : (part + 1) * width
            ].astype(f32)

    put(first_s, 0, ada)
    put(first_s, 6 * rows, qkv)
    put(second_s, 0, out)
    put(second_s, rows, up)
    after = rows + up.shape[1] * rows // width
    second_s[after : after + down.shape[0]] = down[...].astype(f32)
    for i, bias in enumerate((b_ada, b_out, b_up, b_down)):
        count = bias.shape[0]
        source = lax.broadcasted_iota(jnp.int32, (count, width), 0)
        lane = lax.broadcasted_iota(jnp.int32, (count, width), 1)
        at = lax.rem(me * count, width) + source
        hit = jnp.where(at >= width, at - width, at) == lane
        line = jnp.broadcast_to(bias[...].astype(f32)[None], (8, count)).astype(bf16)
        first_s[9 * rows + i : 9 * rows + i + 1] = dot(line, jnp.where(hit, 1.0, 0.0).astype(bf16))[:1]
    first[...] = first_s[...].astype(bf16)
    second[...] = second_s[...].astype(bf16)


def pack_shards(*args):
    _, _, out, up, down = args[:5]
    rows, width = out.shape
    sizes = (up_to(9 * rows + 4, 16), up_to(rows + up.shape[1] * rows // width + down.shape[0] + 4, 16))
    return pl.pallas_call(
        pack_body,
        out_shape=[shape_of((n, width), bf16) for n in sizes],
        scratch_shapes=[pltpu.VMEM((n, width), f32) for n in sizes],
        name="pack_shards",
    )(*args)


def each_shard(flags, chips, blocks_of):
    first = flags[CORE] == 0
    for chip in range(chips):
        mine, other = blocks_of(jnp.bitwise_xor(flags[PLACE], chip_order(chip, chips)))
        mine, other = mine.astype(f32), other.astype(f32)
        yield 2 * chip, jnp.where(first, mine, other)
        yield 2 * chip + 1, jnp.where(first, other, mine)


def place_columns(dest, device, block, start, rows, count, width):
    for part in range(count):
        dest[device * rows : (device + 1) * rows, part * width : (part + 1) * width] = block[
            start + part * rows : start + (part + 1) * rows
        ]


def attend_pair(qkv, pair, expo, att, inv):
    length = att.shape[-2]
    row_block = 128
    keys = qkv[0, 1, pair]
    values = qkv[0, 2, pair]
    values_ones = jnp.concatenate([values, jnp.ones_like(values)], 1)
    first = lax.broadcasted_iota(jnp.int32, (row_block, PAIR), 1) < HEAD
    for i in range(length // row_block):
        r = pl.ds(i * row_block, row_block)
        query = qkv[0, 0, pair, r, :]
        outs = []
        for head in range(2):
            sel = first if head == 0 else jnp.logical_not(first)
            scores = dot(jnp.where(sel, query, jnp.zeros_like(query)), keys, 1, 1)
            top = jnp.max(scores, -1, keepdims=True)
            e = jnp.exp2((scores - top) * (0.125 * LOG2E)).astype(bf16)
            expo[0, head, r, :] = e
            outs.append(dot(e, values_ones))
        out = jnp.where(first, outs[0][:, :PAIR], outs[1][:, :PAIR])
        inverse = 1.0 / jnp.where(first, outs[0][:, PAIR:], outs[1][:, PAIR:])
        att[0, 0, r, :] = (out * inverse).astype(bf16)
        inv[0, 0, r, :] = inverse


def attend_forward_body(flags, own_x, far_x, cond, *refs):
    pieces = refs[:-11]
    qkv, expo, att, inv, mod, bias, w_qkv, w_f32, bias_f32, shards, sems = refs[-11:]
    slot = pl.program_id(0)
    pair = pl.program_id(1)
    length, width = own_x.shape[1:]
    group, others = shards.shape[1:3]
    chips = group * others
    rows = width // (2 * chips)
    pairs = width // PAIR

    def blocks_of(place):
        at = lax.div(place, others), lax.rem(place, others)
        return shards[(0, *at)], shards[(1, *at)]

    @pl.when((slot == 0) & (pair == 0))
    def _():
        fetch(pieces[:group], shards.at[0], sems.at[0])
        fetch(pieces[group:], shards.at[1], sems.at[1])
        bias_f32[...] = jnp.zeros_like(bias_f32)
        lane = lax.broadcasted_iota(jnp.int32, (1, width), 1)
        for device, block in each_shard(flags, chips, blocks_of):
            place_columns(w_f32, device, block, 0, rows, 6, width)
            start = 0
            for i, count in enumerate((6 * rows, rows, bias_f32.shape[0] * rows - 8 * rows, rows)):
                low, high = device * count, (device + 1) * count
                for part in range(low // width, (high - 1) // width + 1):
                    at = lane + part * width
                    bias_f32[start + part : start + part + 1] += jnp.where(
                        (at >= low) & (at < high), block[9 * rows + i : 9 * rows + i + 1], 0.0
                    )
                start += 2 * chips * count // width
        for part in range(6):
            cols = slice(part * width, (part + 1) * width)
            mod[:, cols] = dot(cond[...], w_f32[:, cols].astype(bf16)) + bias_f32[part : part + 1]
        for part in range(bias_f32.shape[0] - 6):
            bias[:, part * width : (part + 1) * width] = bias_f32[6 + part : 7 + part]
        for device, block in each_shard(flags, chips, blocks_of):
            place_columns(w_f32, device, block, 6 * rows, rows, 3, width)
        w_qkv[...] = w_f32[:, : 3 * width].astype(bf16)

    @pl.when((pair == 0) & is_live(flags, slot))
    def _():
        shift = mod[pl.ds(slot, 1), :width]
        scale = 1.0 + mod[pl.ds(slot, 1), width : 2 * width]
        row_block = 256

        def project(ref):
            @pl.loop(0, length // row_block)
            def _(i):
                r = pl.ds(pl.multiple_of(i * row_block, row_block), row_block)
                normed, _ = norm(ref[0, r, :].astype(f32))
                h1 = (normed * scale + shift).astype(bf16)
                result = dot(h1, w_qkv[...]).astype(bf16)
                for kind in range(3):
                    for p in range(pairs):
                        at = kind * width + p * PAIR
                        qkv[0, kind, p, r, :] = result[:, at : at + PAIR]

        @pl.when(slot < flags[KEEP])
        def _():
            project(own_x)

        @pl.when(slot >= flags[KEEP])
        def _():
            project(far_x)

    @pl.when(is_live(flags, slot))
    def _():
        attend_pair(qkv, pair, expo, att, inv)


def attend_forward(flags, own_x, far_x, cond, mine, other, bias_rows):
    steps, length, width = own_x.shape
    pairs = width // PAIR
    shards_shape = (2, len(mine)) + mine[0].shape
    args = (flags, own_x, far_x, cond, *mine, *other)

    def at(s, p, flags):
        return live_at(flags, s, p, pairs) + (0, 0)

    whole = pl.BlockSpec((1, 3, pairs, length, PAIR), lambda s, p, flags: (at(s, p, flags)[0], 0, 0, 0, 0))
    part = pl.BlockSpec((1, 1, length, PAIR), at)
    return call(
        attend_forward_body,
        (steps, pairs),
        [
            pl.BlockSpec((1, length, width), lambda s, p, flags: (own_slot(flags, s), 0, 0)),
            fixed(far_x.shape), fixed(cond.shape),
        ] + [anywhere] * (2 * len(mine)),
        [
            whole,
            pl.BlockSpec((1, 2, length, length), at),
            part, part,
            fixed((8, 6 * width)), fixed((1, (bias_rows - 6) * width)), fixed((width, 3 * width)),
        ],
        [
            shape_of((steps, 3, pairs, length, PAIR), bf16),
            shape_of((steps, 2 * pairs, length, length), bf16),
            shape_of((steps, pairs, length, PAIR), bf16),
            shape_of((steps, pairs, length, PAIR), f32),
            shape_of((8, 6 * width), f32),
            shape_of((1, (bias_rows - 6) * width), f32),
            shape_of((width, 3 * width), bf16),
        ],
        [
            pltpu.VMEM((width, 6 * width), f32),
            pltpu.VMEM((bias_rows, width), f32),
            pltpu.VMEM(shards_shape, bf16),
            pltpu.SemaphoreType.DMA((2, len(mine))),
        ],
        "attend_forward", 30 * 10**9, args,
    )


def pack_chunk(flags, device, chunk, keep, send):
    place = jnp.bitwise_xor(flags[PLACE], chip_order(device >> 1, keep.shape[0]))

    @pl.when(flags[CORE] == (device & 1))
    def _():
        keep[place] = chunk[...].astype(keep.dtype)

    @pl.when(flags[CORE] != (device & 1))
    def _():
        send[place] = chunk[...].astype(bf16)


def feed_forward_body(
    steps, flags, own_x, far_x, own_g, far_g, att, inv, mod, bias, *refs
):
    (
        own_out, far_out, grad_x1, grad_att, note, keep, send,
        x_s, g_s, w_out, w_up, w_down, sum_out, sum_up, sum_down_t, down_f32, chunk, bias_sum,
        grad_mod, note_s, shards, sems,
    ) = refs[-22:]
    pieces = refs[:-22]
    slot = pl.program_id(0)
    step = pl.program_id(1)
    own, far, dead = kinds(flags, slot, steps)
    width = x_s.shape[1]
    hidden_units = w_up.shape[1]
    ratio = hidden_units // width
    group, _, others = shards.shape[:3]
    chips = group * others
    rows = width // (2 * chips)

    def blocks_of(place):
        part, place = lax.div(place, others), lax.rem(place, others)
        return shards[part, 0, place], shards[part, 1, place]

    @pl.when((slot == 0) & (step == 0))
    def _():
        fetch(pieces, shards, sems)
        for device, block in each_shard(flags, chips, blocks_of):
            place_columns(sum_out, device, block, 0, rows, 1, width)
            place_columns(sum_up, device, block, rows, rows, ratio, width)
            place_columns(
                down_f32, device, block, (1 + ratio) * rows, ratio * rows, 1, width
            )
        w_out[...] = sum_out[...].astype(bf16)
        w_up[...] = sum_up[...].astype(bf16)
        w_down[...] = down_f32[...].astype(bf16)
        for ref in (sum_out, sum_up, sum_down_t, bias_sum, chunk, grad_mod):
            ref[...] = jnp.zeros_like(ref)

    @pl.when(dead)
    def _():
        own_out[...] = jnp.zeros_like(own_out)

    @pl.when(own)
    def _():
        x_s[...] = own_x[0].astype(f32)
        g_s[...] = own_g[0].astype(f32)

    @pl.when(far)
    def _():
        x_s[...] = far_x[0].astype(f32)
        g_s[...] = far_g[0].astype(f32)

    @pl.when(is_live(flags, slot))
    def _():
        def vector(part):
            return mod[pl.ds(slot, 1), part * width : (part + 1) * width]

        gate1, shift2, scale2, gate2 = vector(2), vector(3), 1.0 + vector(4), vector(5)
        b_out = bias[:, :width]
        b_up = bias[:, width : width + hidden_units]
        b_down = bias[:, width + hidden_units :]

        def lanes(ref):
            return jnp.concatenate([ref[0, p] for p in range(ref.shape[1])], 1)

        attended = lanes(att)
        branch1 = dot(attended, w_out[...]) + b_out
        x1 = x_s[...] + gate1 * branch1
        normed2, rstd = norm(x1)
        h2 = (normed2 * scale2 + shift2).astype(bf16)
        pre = dot(h2, w_up[...]) + b_up
        cdf = 0.5 * (1.0 + lax.erf(pre * (1 / math.sqrt(2.0))))
        hidden = (pre * cdf).astype(bf16)
        slope = cdf + pre * jnp.exp2(pre * pre * (-0.5 * LOG2E)) * (1 / math.sqrt(2 * math.pi))
        branch2 = dot(hidden, w_down[...]) + b_down
        result = (x1 + gate2 * branch2).astype(bf16)

        @pl.when(own)
        def _():
            own_out[0] = result

        @pl.when(far)
        def _():
            far_out[0] = result

        grad = g_s[...]
        grad_b2 = (gate2 * grad).astype(bf16)
        grad_pre = (dot(grad_b2, w_down[...], 1, 1) * slope).astype(bf16)
        grad_h2 = dot(grad_pre, w_up[...], 1, 1)
        grad_n = grad_h2 * scale2
        g_x1 = grad + rstd * (
            grad_n
            - jnp.mean(grad_n, -1, keepdims=True)
            - normed2 * jnp.mean(grad_n * normed2, -1, keepdims=True)
        )
        grad_b1 = (gate1 * g_x1).astype(bf16)
        grad_x1[0] = g_x1
        g_att = (dot(grad_b1, w_out[...], 1, 1) * lanes(inv)).astype(bf16)
        for p in range(width // PAIR):
            grad_att[0, p] = g_att[:, p * PAIR : (p + 1) * PAIR]

        def add_mod(part, value):
            grad_mod[pl.ds(slot, 1), part * width : (part + 1) * width] += row_sum(value)

        add_mod(0, g_x1 * branch1)
        add_mod(1, grad_h2)
        add_mod(2, grad_h2 * normed2)
        add_mod(3, grad * branch2)
        sum_out[...] += dot(attended, grad_b1, 0, 0)
        sum_up[...] += dot(h2, grad_pre, 0, 0)
        sum_down_t[...] += dot(grad_b2, hidden, 0, 0)
        bias_sum[:, :width] += row_sum(grad_b1.astype(f32))
        bias_sum[:, width : width + hidden_units] += row_sum(grad_pre.astype(f32))
        bias_sum[:, width + hidden_units :] += row_sum(grad_b2.astype(f32))

    @pl.when((slot == pl.num_programs(0) - 1) & (step == pl.num_programs(1) - 1))
    def _():
        down_f32[...] = sum_down_t[...].T
        for device in range(2 * chips):
            span = slice(device * rows, (device + 1) * rows)
            chunk[:rows] = sum_out[span]
            for part in range(ratio):
                chunk[(1 + part) * rows : (2 + part) * rows] = sum_up[
                    span, part * width : (part + 1) * width
                ]
            chunk[(1 + ratio) * rows : (1 + 2 * ratio) * rows] = down_f32[
                device * ratio * rows : (device + 1) * ratio * rows
            ]
            up_row = 1 + device * ratio * rows // width
            for i, part in enumerate((0, up_row, 1 + ratio)):
                at = (1 + 2 * ratio) * rows + i
                chunk[at : at + 1] = bias_sum[:, part * width : (part + 1) * width]
            pack_chunk(flags, device, chunk, keep, send)
        note_s[...] = jnp.zeros_like(note_s)
        for row in range(4 * steps):
            part = row % 4
            note_s[row : row + 1] = grad_mod[
                row // 4 : row // 4 + 1, part * width : (part + 1) * width
            ]
        note[...] = note_s[...].astype(bf16)


def feed_forward(
    flags, own_x, far_x, own_g, far_g, att, inv, mod, bias, shards, hidden_units
):
    steps, length, width = own_x.shape
    row_block = 1024
    blocks = length // row_block
    group, others = len(shards), shards[0].shape[1]
    rows = width // (2 * group * others)
    ratio = hidden_units // width
    packed_rows = up_to((1 + 2 * ratio) * rows + 3, 16)
    sum_shape = (group * others, packed_rows, width)
    note_shape = (up_to(4 * steps, 16), width)

    def own(s, b, flags):
        return (own_slot(flags, s), jnp.where(s < flags[KEEP], b, blocks - 1), 0)

    def far(s, b, flags):
        keep = flags[KEEP]
        return (0, jnp.where(s < keep, 0, jnp.where(s == keep, b, blocks - 1)), 0)

    def live(s, b, flags):
        return live_at(flags, s, b, blocks) + (0,)

    def live_parts(s, b, flags):
        at, part = live_at(flags, s, b, blocks)
        return (at, 0, part, 0)

    def own_result(s, b, flags):
        own, _, dead = kinds(flags, s, steps)
        return (result_slot(flags, s, steps), jnp.where(own | dead, b, blocks - 1), 0)

    def block(where):
        return pl.BlockSpec((1, row_block, width), where)

    def parts(count):
        return pl.BlockSpec((1, count, row_block, PAIR), live_parts)

    pairs = width // PAIR
    args = (flags, own_x, far_x, own_g, far_g, att, inv, mod, bias, *shards)
    return call(
        functools.partial(feed_forward_body, steps),
        (steps + 1, blocks),
        [
            block(own), block(far), block(own), block(far), parts(pairs), parts(pairs),
            fixed(mod.shape), fixed(bias.shape),
        ] + [anywhere] * group,
        [
            block(own_result), block(far), block(live), parts(pairs),
            fixed(note_shape), fixed(sum_shape), fixed(sum_shape),
        ],
        [
            shape_of((steps, length, width), bf16),
            shape_of((1, length, width), bf16),
            shape_of((steps, length, width), f32),
            shape_of((steps, pairs, length, PAIR), bf16),
            shape_of(note_shape, bf16),
            shape_of(sum_shape, bf16),
            shape_of(sum_shape, bf16),
        ],
        [
            pltpu.VMEM((row_block, width), f32),
            pltpu.VMEM((row_block, width), f32),
            pltpu.VMEM((width, width), bf16),
            pltpu.VMEM((width, hidden_units), bf16),
            pltpu.VMEM((hidden_units, width), bf16),
            pltpu.VMEM((width, width), f32),
            pltpu.VMEM((width, hidden_units), f32),
            pltpu.VMEM((width, hidden_units), f32),
            pltpu.VMEM((hidden_units, width), f32),
            pltpu.VMEM((packed_rows, width), f32),
            pltpu.VMEM(bias.shape, f32),
            pltpu.VMEM((8, 4 * width), f32),
            pltpu.VMEM(note_shape, f32),
            pltpu.VMEM((group,) + shards[0].shape, bf16),
            pltpu.SemaphoreType.DMA((group,)),
        ],
        "feed_forward", 60 * 10**9, args,
    )


def attend_backward_pair(qkv, expo, att, grad_att, g_qkv, keys_t, values_t):
    length = att.shape[2]
    row_block = 512
    keys = qkv[0, 1, 0]
    values = qkv[0, 2, 0]
    values_ones = jnp.concatenate([values, jnp.ones_like(values)], 1)
    lane = lax.broadcasted_iota(jnp.int32, (row_block, PAIR), 1)
    first = lane < HEAD
    for i in range(length // row_block):
        r = pl.ds(i * row_block, row_block)
        query = qkv[0, 0, 0, r, :]
        g_att = grad_att[0, 0, r, :]
        product = g_att.astype(f32) * att[0, 0, r, :].astype(f32)
        query_t = query.T
        g_att_t = g_att.T
        grads_q = []
        for head in range(2):
            sel = first if head == 0 else jnp.logical_not(first)
            delta = jnp.sum(jnp.where(sel, product, 0.0), -1, keepdims=True)
            high = delta.astype(bf16).astype(f32)
            extra = jnp.where(
                lane == 0, -high, jnp.where(lane == 1, high - delta, 0.0)
            ).astype(bf16)
            left = jnp.concatenate([jnp.where(sel, g_att, jnp.zeros_like(g_att)), extra], 1)
            e = expo[0, head, r, :]
            grad_s = e * dot(left, values_ones, 1, 1).astype(bf16)
            grads_q.append(dot(grad_s, keys))
            span = slice(head * HEAD, (head + 1) * HEAD)
            add_k = dot(query_t[span], grad_s)
            add_v = dot(g_att_t[span], e)
            if i == 0:
                keys_t[span] = add_k
                values_t[span] = add_v
            else:
                keys_t[span] += add_k
                values_t[span] += add_v
        g_qkv[0, r, :] = (jnp.where(first, grads_q[0], grads_q[1]) * 0.125).astype(bf16)
    g_qkv[1] = (keys_t[...] * 0.125).astype(bf16).T
    g_qkv[2] = values_t[...].astype(bf16).T


def first_pairs_body(flags, qkv, expo, att, grad_att, g_qkv, keys_t, values_t):
    @pl.when(is_live(flags, pl.program_id(0)))
    def _():
        attend_backward_pair(qkv, expo, att, grad_att, g_qkv.at[0, 0], keys_t, values_t)


def first_pairs(flags, qkv, expo, att, grad_att):
    steps, _, pairs, length, _ = qkv.shape
    pairs -= 1

    def part(s, p, flags):
        return live_at(flags, s, p, pairs) + (0, 0)

    def qkv_at(s, p, flags):
        at, pair = live_at(flags, s, p, pairs)
        return (at, 0, pair, 0, 0)

    heads = pl.BlockSpec((1, 1, length, PAIR), part)
    return call(
        first_pairs_body,
        (steps, pairs),
        [
            pl.BlockSpec((1, 3, 1, length, PAIR), qkv_at),
            pl.BlockSpec((1, 2, length, length), part),
            heads, heads,
        ],
        pl.BlockSpec((1, 1, 3, length, PAIR), lambda s, p, flags: part(s, p, flags) + (0,)),
        shape_of((steps, pairs, 3, length, PAIR), bf16),
        [pltpu.VMEM((PAIR, length), f32), pltpu.VMEM((PAIR, length), f32)],
        "first_pairs", 40 * 10**9, (flags, qkv, expo, att, grad_att),
    )


def finish_body(
    steps, flags, own_x, far_x, qkv, expo, att, grad_att, grad_x1, mod, w_qkv, g_first,
    own_grad, far_grad, note, keep, send, g_last, keys_t, values_t, sum_qkv, chunk, grad_mod, note_s,
):
    slot = pl.program_id(0)
    own, far, dead = kinds(flags, slot, steps)
    length, width = own_x.shape[1:]
    chips = keep.shape[0]
    rows = width // (2 * chips)

    @pl.when(slot == 0)
    def _():
        for ref in (sum_qkv, chunk, grad_mod):
            ref[...] = jnp.zeros_like(ref)

    @pl.when(dead)
    def _():
        own_grad[...] = jnp.zeros_like(own_grad)

    @pl.when(is_live(flags, slot))
    def _():
        attend_backward_pair(qkv, expo, att, grad_att, g_last, keys_t, values_t)

    def finish(x_ref, out_ref):
        shift = mod[pl.ds(slot, 1), :width]
        scale = 1.0 + mod[pl.ds(slot, 1), width : 2 * width]
        row_block = 512
        for i in range(length // row_block):
            r = pl.ds(i * row_block, row_block)
            normed, rstd = norm(x_ref[0, r, :].astype(f32))
            h1 = (normed * scale + shift).astype(bf16)
            grad = []
            for kind in range(3):
                grad += [g_first[0, p, kind, r, :] for p in range(g_first.shape[1])]
                grad.append(g_last[kind, r, :])
            grad = jnp.concatenate(grad, 1)
            grad_h1 = dot(grad, w_qkv[...], 1, 1)
            sum_qkv[...] += dot(h1, grad, 0, 0)
            grad_mod[pl.ds(slot, 1), :width] += row_sum(grad_h1)
            grad_mod[pl.ds(slot, 1), width:] += row_sum(grad_h1 * normed)
            grad_n = grad_h1 * scale
            out_ref[0, r, :] = (
                grad_x1[0, r, :]
                + rstd
                * (
                    grad_n
                    - jnp.mean(grad_n, -1, keepdims=True)
                    - normed * jnp.mean(grad_n * normed, -1, keepdims=True)
                )
            ).astype(out_ref.dtype)

    @pl.when(own)
    def _():
        finish(own_x, own_grad)

    @pl.when(far)
    def _():
        finish(far_x, far_grad)

    @pl.when(slot == steps)
    def _():
        for device in range(2 * chips):
            for part in range(3):
                chunk[part * rows : (part + 1) * rows] = sum_qkv[
                    device * rows : (device + 1) * rows, part * width : (part + 1) * width
                ]
            pack_chunk(flags, device, chunk, keep, send)
        note_s[...] = jnp.zeros_like(note_s)
        for row in range(2 * steps):
            part = row % 2
            note_s[row : row + 1] = grad_mod[
                row // 2 : row // 2 + 1, part * width : (part + 1) * width
            ]
        note[...] = note_s[...].astype(bf16)


def finish(
    flags, own_x, far_x, qkv, expo, att, grad_att, grad_x1, mod, w_qkv, g_first, chips
):
    steps, length, width = own_x.shape
    last = width // PAIR - 1
    sum_shape = (chips, up_to(3 * width // (2 * chips), 8), width)
    note_shape = (up_to(2 * steps, 8), width)

    def at(*part):
        return lambda s, flags: (live_at(flags, s, 0, 1)[0],) + part

    def block(where):
        return pl.BlockSpec((1, length, width), where)

    heads = pl.BlockSpec((1, 1, length, PAIR), at(last, 0, 0))
    return call(
        functools.partial(finish_body, steps),
        (steps + 1,),
        [
            block(lambda s, flags: (own_slot(flags, s), 0, 0)),
            block(lambda s, flags: (0, 0, 0)),
            pl.BlockSpec((1, 3, 1, length, PAIR), at(0, last, 0, 0)),
            pl.BlockSpec((1, 2, length, length), at(last, 0, 0)),
            heads, heads, block(at(0, 0)), fixed(mod.shape), fixed(w_qkv.shape),
            pl.BlockSpec((1, last, 3, length, PAIR), at(0, 0, 0, 0)),
        ],
        [
            block(lambda s, flags: (result_slot(flags, s, steps), 0, 0)),
            block(lambda s, flags: (0, 0, 0)),
            fixed(note_shape), fixed(sum_shape), fixed(sum_shape),
        ],
        [
            shape_of((steps, length, width), f32),
            shape_of((1, length, width), bf16),
            shape_of(note_shape, bf16),
            shape_of(sum_shape, f32),
            shape_of(sum_shape, bf16),
        ],
        [
            pltpu.VMEM((3, length, PAIR), bf16),
            pltpu.VMEM((PAIR, length), f32),
            pltpu.VMEM((PAIR, length), f32),
            pltpu.VMEM((width, 3 * width), f32),
            pltpu.VMEM(sum_shape[1:], f32),
            pltpu.VMEM((8, 2 * width), f32),
            pltpu.VMEM(note_shape, f32),
        ],
        "finish", 40 * 10**9,
        (flags, own_x, far_x, qkv, expo, att, grad_att, grad_x1, mod, w_qkv, g_first),
    )


def swap(array, mask):
    count = lax.axis_size("dp")
    return lax.ppermute(array, "dp", [(i, i ^ mask) for i in range(count)])


def tie(value, *others):
    return lax.optimization_barrier((value,) + others)[0]


def chip_groups(chips):
    bits = chips.bit_length() - 1
    return tuple(tuple(range(max(top - 2, 0), top)) for top in range(bits, 0, -2))


def chip_order(chip, chips):
    place, low = 0, 0
    for group in chip_groups(chips):
        place = place | ((chip >> group[0]) & ((1 << len(group)) - 1)) << low
        low += len(group)
    return place


def group_masks(group):
    return [sum(((k >> i) & 1) << b for i, b in enumerate(group)) for k in range(1, 1 << len(group))]


def gather_group(held, group):
    return [held] + [swap(held, mask << 1) for mask in group_masks(group)]


def stage_body(adds, sends, with_notes, held, notes, *refs):
    adds, outs = refs[:adds], refs[adds:]
    parts, rows, _ = held.shape
    size = parts * rows
    keep, joined, outs = outs[0], outs[1], outs[2:]
    own = notes.shape[0]
    joined[:own] = notes[...]
    if adds[0].shape[0] > size:
        for k, add in enumerate(adds):
            joined[(k + 1) * own : (k + 2) * own] = add[size:]
    count = parts // (sends + 1)
    for part in range(parts):
        total = held[part].astype(f32)
        for add in adds:
            total = total + add[part * rows : (part + 1) * rows].astype(f32)
        if part < count:
            keep[part] = total
        else:
            at = part % count * rows
            outs[part // count - 1][at : at + rows] = total.astype(bf16)
    if with_notes:
        for out in outs:
            out[count * rows :] = joined[...]


def stage(held, notes, adds, sends=0, with_notes=True):
    parts, rows, width = held.shape
    extra = adds[0].shape[0] - parts * rows
    count = parts // (sends + 1)
    joined = notes.shape[0] + len(adds) * extra
    size = count * rows + (joined if with_notes else 0)
    keep, joined, *outs = pl.pallas_call(
        functools.partial(stage_body, len(adds), sends, with_notes),
        out_shape=[shape_of((count, rows, width), f32), shape_of((joined, width), bf16)]
        + [shape_of((size, width), bf16)] * sends,
        name="stage",
    )(held, notes, *adds)
    return keep, joined, outs


def reduce_start(group, sums, notes):
    masks = group_masks(group)
    parts = [held.shape[0] // (len(masks) + 1) for held in sums]
    got = []
    for k, mask in enumerate(masks):
        pieces = [held[(k + 1) * n : (k + 2) * n].astype(bf16) for held, n in zip(sums, parts)]
        pieces += notes
        width = pieces[0].shape[-1]
        got.append(swap(jnp.concatenate([p.reshape(-1, width) for p in pieces], 0), mask << 1))
    return [held[:part] for held, part in zip(sums, parts)], notes, got


def reduce_done(totals, notes, got, *after):
    got = lax.optimization_barrier(tuple(got) + after)[: len(got)]
    joined = [[note] for note in notes]
    for block in got:
        start = 0
        for i, piece in enumerate(totals + notes):
            size = math.prod(piece.shape[:-1])
            part = block[start : start + size].reshape(piece.shape)
            start += size
            if i < len(totals):
                totals = totals[:i] + [totals[i] + part.astype(f32)] + totals[i + 1 :]
            else:
                joined[i - len(totals)].append(part)
    return totals, [jnp.concatenate(blocks, 0) for blocks in joined]


def hand_back_body(at, back_out, back_grad, _out, _grad, _after, out, grad, done, low, high, sems):
    done[...] = jnp.zeros_like(done)

    @pl.when(at[0] > 0)
    def _():
        loads = [
            pltpu.make_async_copy(back_grad.at[0], low.at[0], sems.at[0]),
            pltpu.make_async_copy(back_out.at[0], low.at[1], sems.at[1]),
        ]
        for load in loads:
            load.start()
        loads[0].wait()
        high[...] = low[0].astype(f32)
        loads[1].wait()
        stores = [
            pltpu.make_async_copy(high, grad.at[at[1]], sems.at[2]),
            pltpu.make_async_copy(low.at[1], out.at[at[1]], sems.at[3]),
        ]
        for store in stores:
            store.start()
        for store in stores:
            store.wait()


def hand_back(at, back_out, back_grad, own_out, own_grad, after):
    return pl.pallas_call(
        hand_back_body,
        grid_spec=pltpu.PrefetchScalarGridSpec(
            num_scalar_prefetch=1,
            grid=(1,),
            in_specs=[anywhere] * 5,
            out_specs=[anywhere] * 2 + [fixed((8, 128))],
            scratch_shapes=[
                pltpu.VMEM((2,) + own_grad.shape[1:], bf16),
                pltpu.VMEM(own_grad.shape[1:], f32),
                pltpu.SemaphoreType.DMA((4,)),
            ],
        ),
        out_shape=[
            shape_of(own_out.shape, bf16), shape_of(own_grad.shape, f32), shape_of((8, 128), f32),
        ],
        input_output_aliases={3: 0, 4: 1},
        name="hand_back",
    )(at, back_out, back_grad, own_out, own_grad, after)


def condition_body(at, steps, order, *refs):
    pieces, (left, blocks, cond, sems) = refs[:-4], refs[-4:]
    width = cond.shape[1]
    rows = width * steps // cond.shape[0]
    me = lax.axis_index("dp").astype(jnp.int32)
    base = at // 16 * 16
    fetch([piece.at[:, :, pl.ds(base, 16), :] for piece in pieces], blocks, sems)
    at -= base
    for core in range(2):
        for place, (part, other) in enumerate(order):
            start = (core * len(order) + place) * steps
            cond[start : start + steps] = blocks[part, core, other, at : at + steps].astype(f32)
    turned = pltpu.roll(cond[...], lax.rem(width - me * rows, width), 1)[:, :PAIR]
    lane = lax.broadcasted_iota(jnp.int32, turned.shape, 1)
    left[...] = jnp.where(lane < rows, turned, jnp.where(lane == rows, 1.0, 0.0)).astype(bf16)


def condition_columns(pieces, sizes, cond_row, steps):
    _, others, _, width = pieces[0].shape
    chips = len(pieces) * others
    order = []
    for place in range(chips):
        digits, rest = [], place
        for size in sizes:
            digits.append(rest % size)
            rest //= size
        other, low = 0, 1
        for digit, size in zip(reversed(digits[1:]), reversed(sizes[1:])):
            other += digit * low
            low *= size
        order.append((digits[0], other))
    return pl.pallas_call(
        functools.partial(condition_body, cond_row, steps, order),
        in_specs=[anywhere] * len(pieces),
        out_shape=shape_of((2 * chips * steps, PAIR), bf16),
        scratch_shapes=[
            pltpu.VMEM((len(pieces), 2, others, 16, width), bf16),
            pltpu.VMEM((2 * chips * steps, width), f32),
            pltpu.SemaphoreType.DMA((len(pieces),)),
        ],
        name="condition_columns",
    )(*pieces)


def result_body(
    sums1, sums2, left, mine1, other1, mine2, other2, _done,
    ada, b_ada, qkv, out, b_out, up, b_up, down, b_down, ada_sum,
):
    rows, width = out.shape
    ratio = up.shape[1] // width
    me = lax.axis_index("dp").astype(jnp.int32)
    for part in range(3):
        qkv[:, part * width : (part + 1) * width] = sums1[0, part * rows : (part + 1) * rows]
    out[...] = sums2[0, :rows]
    for part in range(ratio):
        up[:, part * width : (part + 1) * width] = sums2[
            0, (1 + part) * rows : (2 + part) * rows
        ]
    after = (1 + 2 * ratio) * rows
    down[...] = sums2[0, after - ratio * rows : after]
    for i, ref in enumerate((b_out, b_up, b_down)):
        size = ref.shape[1]
        line = sums2[0, after + i : after + i + 1]
        shift = lax.rem(width - lax.rem(me * size, width), width)
        ref[...] = pltpu.roll(line, shift, 1)[:, :size]
    half = left.shape[0] // 2
    start = 0
    for count, refs in ((2, (mine1, other1)), (4, (mine2, other2))):
        source = lax.broadcasted_iota(jnp.int32, (half, count * half), 1)
        target = lax.broadcasted_iota(jnp.int32, (half, count * half), 0)
        for part in range(count):
            pick = jnp.where(source == target * count + part, 1.0, 0.0).astype(bf16)
            total = 0.0
            for i, ref in enumerate(refs):
                picked = dot(pick, ref[...]).astype(bf16)
                total = total + dot(left[i * half : (i + 1) * half], picked, 0, 0)
            cols = slice((start + part) * width, (start + part + 1) * width)
            ada[:, cols] = total[:rows]
            ada_sum[:, cols] = total[rows : rows + 1]
        start += count
    b_ada[...] = pltpu.roll(ada_sum[...], lax.rem(6 * width - me * 6 * rows, 6 * width), 1)[
        :, : 6 * rows
    ]


def results(sums1, sums2, left, mine1, other1, mine2, other2, done, rows, ratio):
    width = sums1.shape[2]
    shapes = [
        (rows, 6 * width), (1, 6 * rows), (rows, 3 * width), (rows, width), (1, rows),
        (rows, ratio * width), (1, ratio * rows), (ratio * rows, width), (1, rows),
    ]
    return pl.pallas_call(
        result_body,
        out_shape=[shape_of(s, f32) for s in shapes],
        scratch_shapes=[pltpu.VMEM((1, 6 * width), f32)],
        name="results",
    )(sums1, sums2, left, mine1, other1, mine2, other2, done)


def body(
    fields, conditions, step_counts, cotangent,
    w_ada, b_ada, w_qkv, w_out, b_out, w_up, b_up, w_down, b_down,
):
    devices = lax.axis_size("dp")
    chips = devices // 2
    me = lax.axis_index("dp").astype(jnp.int32)
    chip, core = me >> 1, me & 1
    steps, length, width = fields.shape[1:]
    hidden_units = w_up.shape[1]
    ratio = hidden_units // width
    rows = width // devices
    fields, conditions, cotangent = fields[0], conditions[0], cotangent[0]
    groups = chip_groups(chips)

    count = step_counts[0]
    first, second = pack_shards(
        w_ada, w_qkv, w_out, w_up, w_down, b_ada, b_out, b_up, b_down
    )
    head = jnp.concatenate([conditions, jnp.full((4, width), count, bf16)], 0)
    other_head = swap(tie(head, first), 1)
    other_count = other_head[steps, 0].astype(jnp.int32)
    give = count - other_count >= 2
    take = (other_count - count >= 2).astype(jnp.int32)
    keep = count - give.astype(jnp.int32)
    flags = jnp.stack([keep, take, chip_order(chip, chips), core])
    far_cond = lax.dynamic_index_in_dim(other_head, other_count - 1, 0)
    cond = jnp.concatenate([conditions, jnp.zeros((8 - steps, width), bf16)], 0)
    cond = jnp.where((jnp.arange(8) == keep)[:, None] & (take > 0), far_cond, cond)
    cond_act = jax.nn.silu(cond.astype(f32)).astype(bf16)

    cond_row = (1 + 2 * ratio) * rows
    mine_a = first[None]
    mine_b = lax.dynamic_update_slice_in_dim(second, cond_act[:steps], cond_row, 0)[None]
    for group in groups[:-1]:
        pieces = lax.optimization_barrier((*gather_group(mine_a, group), cond_act, flags))[:-2]
        mine_a = jnp.concatenate(pieces, 0)
    far_x = swap(tie(lax.dynamic_index_in_dim(fields, count - 1, 0), mine_a), 1)
    far_g = swap(tie(lax.dynamic_index_in_dim(cotangent, count - 1, 0), mine_a), 1)
    for group in groups[:-1]:
        mine_b = jnp.concatenate(gather_group(tie(mine_b, far_x, far_g), group), 0)
    both_b = jnp.stack([mine_b, swap(tie(mine_b, mine_a), 1)])
    mine_a = gather_group(mine_a, groups[-1])
    other_a = [swap(piece, 1) for piece in mine_a]
    back_at = jnp.stack([give.astype(jnp.int32), count - 1])
    first_kernel = lax.optimization_barrier(
        (flags, both_b, far_x, far_g, cond_act, back_at)
    )
    back_at = first_kernel[5]
    qkv, expo, att, inv, mod, bias, full_qkv = attend_forward(
        first_kernel[0], fields, far_x, cond_act, mine_a, other_a, 8 + ratio
    )
    all_b = gather_group(first_kernel[1], groups[-1])
    all_b = lax.optimization_barrier((*all_b, mod))[:-1]
    own_out, far_out, grad_x1, grad_att, note2, keep2, send2 = feed_forward(
        flags, fields, far_x, cotangent, far_g, att, inv, mod, bias, all_b, hidden_units
    )

    up_groups = tuple(reversed(groups))
    late = up_groups[2:]
    masks = [[mask << 1 for mask in group_masks(group)] for group in up_groups]
    left = condition_columns(all_b, [len(m) + 1 for m in masks], cond_row, steps)
    got2 = tie(swap(send2.reshape(-1, width), 1), left)
    held2, note2, sends = stage(keep2, note2, [got2], len(masks[0]))
    gots = [swap(send, mask) for send, mask in zip(sends, masks[0])]
    back_out = swap(far_out, 1)
    g_first = first_pairs(tie(flags, held2), qkv, expo, att, grad_att)
    gots = lax.optimization_barrier((*gots, g_first))[:-1]
    held2, note2, sends = stage(held2, note2, gots, len(masks[1]))
    gots = [swap(send, mask) for send, mask in zip(sends, masks[1])]
    own_grad, far_grad, note1, keep1, send1 = finish(
        tie(flags, held2, back_out), fields, far_x, qkv, expo, att, grad_att, grad_x1, mod, full_qkv, g_first,
        chips,
    )
    got1 = swap(send1, 1)
    gots = lax.optimization_barrier((*gots, keep1))[:-1]
    held2, note2, sends = stage(held2, note2, gots, len(masks[2]) if late else 0)
    held1 = keep1 + got1.astype(f32)
    back_grad = swap(far_grad, 1)
    note1 = note1[None]

    going = reduce_start(up_groups[0], [held1], [note1])
    (held1,), (note1,) = reduce_done(*going, back_grad)
    own_out, own_grad, done = hand_back(
        back_at, back_out, back_grad, own_out, own_grad, held1
    )
    for i, group in enumerate(up_groups[1:]):
        if i > 0:
            gots = [swap(send, mask) for send, mask in zip(sends, masks[i + 1])]
            held2, note2, sends = stage(
                held2, note2, gots, len(masks[i + 2]) if i + 2 < len(masks) else 0
            )
        (held1,), (note1,) = reduce_done(*reduce_start(group, [held1], [note1]))
    note1 = note1.reshape(-1, width)
    other1, other2 = swap(note1, 1), swap(note2, 1)
    grads = results(held1, held2, left, note1, other1, note2, other2, done, rows, ratio)
    grads = [g[0] if i in (1, 4, 6, 8) else g for i, g in enumerate(grads)]

    return (own_out[None], own_grad[None], *grads)


def solution(mesh):
    item, matrix, vector = P("dp", None, None, None), P("dp", None), P("dp")
    return jax.shard_map(
        body,
        mesh=mesh,
        in_specs=(
            item, P("dp", None, None), vector, item,
            matrix, vector, matrix, matrix, vector, matrix, vector, matrix, vector,
        ),
        out_specs=(
            item, item, matrix, vector, matrix, matrix, vector, matrix, vector, matrix, vector,
        ),
        check_vma=False,
    )
```

```python
import functools
import math

import jax
import jax.numpy as jnp
from jax import lax
from jax.experimental import pallas as pl
from jax.experimental.pallas import tpu as pltpu
from jax.sharding import PartitionSpec as P

HEAD = 64
PAIR = 2 * HEAD
EPS = 1e-6
LOG2E = 1.4426950408889634
VMEM_LIMIT = 63 * 2**20
bf16 = jnp.bfloat16
f32 = jnp.float32
shape_of = jax.ShapeDtypeStruct


def dot(left, right, left_dim=1, right_dim=0):
    return lax.dot_general(
        left, right, (((left_dim,), (right_dim,)), ((), ())), preferred_element_type=f32
    )


def norm(value):
    mean = jnp.mean(value, -1, keepdims=True)
    cent = value - mean
    var = jnp.mean(cent * cent, -1, keepdims=True)
    rstd = lax.rsqrt(var + EPS)
    return cent * rstd, rstd


def row_sum(value):
    return jnp.sum(value, 0, keepdims=True)


def up_to(value, unit):
    return -(-value // unit) * unit


def call(body, grid, in_specs, out_specs, out_shape, scratch, name, flops, args):
    return pl.pallas_call(
        body,
        grid_spec=pltpu.PrefetchScalarGridSpec(
            num_scalar_prefetch=1,
            grid=grid,
            in_specs=in_specs,
            out_specs=out_specs,
            scratch_shapes=scratch,
        ),
        out_shape=out_shape,
        compiler_params=pltpu.CompilerParams(vmem_limit_bytes=VMEM_LIMIT),
        cost_estimate=pl.CostEstimate(flops=flops, bytes_accessed=10**7, transcendentals=0),
        name=name,
    )(*args)


anywhere = pl.BlockSpec(memory_space=pl.ANY)


def fetch(pieces, dest, sems):
    copies = [pltpu.make_async_copy(p, dest.at[k], sems.at[k]) for k, p in enumerate(pieces)]
    for copy in copies:
        copy.start()
    for copy in copies:
        copy.wait()


def fixed(shape):
    return pl.BlockSpec(shape, lambda *at: (0,) * len(shape))


KEEP, TAKE, PLACE, CORE = range(4)


def own_slot(flags, slot):
    return jnp.minimum(slot, flags[KEEP] - 1)


def is_live(flags, slot):
    return slot < flags[KEEP] + flags[TAKE]


def live_at(flags, slot, block, blocks):
    live = flags[KEEP] + flags[TAKE]
    return jnp.minimum(slot, live - 1), jnp.where(slot < live, block, blocks - 1)


def result_slot(flags, slot, steps):
    after = jnp.clip(slot - flags[TAKE], flags[KEEP] - 1, steps - 1)
    return jnp.where(slot < flags[KEEP], slot, after)


def kinds(flags, slot, steps):
    own = slot < flags[KEEP]
    far = (slot == flags[KEEP]) & (flags[TAKE] > 0)
    return own, far, jnp.logical_not(own | far) & (slot - flags[TAKE] < steps)


def pack_body(ada, qkv, out, up, down, b_ada, b_out, b_up, b_down, first, second, first_s, second_s):
    rows, width = out.shape
    me = lax.axis_index("dp").astype(jnp.int32)
    first_s[...] = jnp.zeros_like(first_s)
    second_s[...] = jnp.zeros_like(second_s)

    def put(dest, start, ref):
        for part in range(ref.shape[1] // width):
            dest[start + part * rows : start + (part + 1) * rows] = ref[
                :, part * width : (part + 1) * width
            ].astype(f32)

    put(first_s, 0, ada)
    put(first_s, 6 * rows, qkv)
    put(second_s, 0, out)
    put(second_s, rows, up)
    after = rows + up.shape[1] * rows // width
    second_s[after : after + down.shape[0]] = down[...].astype(f32)
    for i, bias in enumerate((b_ada, b_out, b_up, b_down)):
        count = bias.shape[0]
        source = lax.broadcasted_iota(jnp.int32, (count, width), 0)
        lane = lax.broadcasted_iota(jnp.int32, (count, width), 1)
        at = lax.rem(me * count, width) + source
        hit = jnp.where(at >= width, at - width, at) == lane
        line = jnp.broadcast_to(bias[...].astype(f32)[None], (8, count)).astype(bf16)
        first_s[9 * rows + i : 9 * rows + i + 1] = dot(line, jnp.where(hit, 1.0, 0.0).astype(bf16))[:1]
    first[...] = first_s[...].astype(bf16)
    second[...] = second_s[...].astype(bf16)


def pack_shards(*args):
    _, _, out, up, down = args[:5]
    rows, width = out.shape
    sizes = (up_to(9 * rows + 4, 16), up_to(rows + up.shape[1] * rows // width + down.shape[0] + 4, 16))
    return pl.pallas_call(
        pack_body,
        out_shape=[shape_of((n, width), bf16) for n in sizes],
        scratch_shapes=[pltpu.VMEM((n, width), f32) for n in sizes],
        name="pack_shards",
    )(*args)


def each_shard(flags, chips, blocks_of):
    first = flags[CORE] == 0
    for chip in range(chips):
        mine, other = blocks_of(jnp.bitwise_xor(flags[PLACE], chip_order(chip, chips)))
        mine, other = mine.astype(f32), other.astype(f32)
        yield 2 * chip, jnp.where(first, mine, other)
        yield 2 * chip + 1, jnp.where(first, other, mine)


def place_columns(dest, device, block, start, rows, count, width):
    for part in range(count):
        dest[device * rows : (device + 1) * rows, part * width : (part + 1) * width] = block[
            start + part * rows : start + (part + 1) * rows
        ]


def attend_pair(qkv, pair, expo, att, inv):
    length = att.shape[-2]
    row_block = 128
    keys = qkv[0, 1, pair]
    values = qkv[0, 2, pair]
    values_ones = jnp.concatenate([values, jnp.ones_like(values)], 1)
    first = lax.broadcasted_iota(jnp.int32, (row_block, PAIR), 1) < HEAD
    for i in range(length // row_block):
        r = pl.ds(i * row_block, row_block)
        query = qkv[0, 0, pair, r, :]
        outs = []
        for head in range(2):
            sel = first if head == 0 else jnp.logical_not(first)
            scores = dot(jnp.where(sel, query, jnp.zeros_like(query)), keys, 1, 1)
            top = jnp.max(scores, -1, keepdims=True)
            e = jnp.exp2((scores - top) * (0.125 * LOG2E)).astype(bf16)
            expo[0, head, r, :] = e
            outs.append(dot(e, values_ones))
        out = jnp.where(first, outs[0][:, :PAIR], outs[1][:, :PAIR])
        inverse = 1.0 / jnp.where(first, outs[0][:, PAIR:], outs[1][:, PAIR:])
        att[0, 0, r, :] = (out * inverse).astype(bf16)
        inv[0, 0, r, :] = inverse


def attend_forward_body(flags, own_x, far_x, cond, *refs):
    pieces = refs[:-11]
    qkv, expo, att, inv, mod, bias, w_qkv, w_f32, bias_f32, shards, sems = refs[-11:]
    slot = pl.program_id(0)
    pair = pl.program_id(1)
    length, width = own_x.shape[1:]
    group, others = shards.shape[1:3]
    chips = group * others
    rows = width // (2 * chips)
    pairs = width // PAIR

    def blocks_of(place):
        at = lax.div(place, others), lax.rem(place, others)
        return shards[(0, *at)], shards[(1, *at)]

    @pl.when((slot == 0) & (pair == 0))
    def _():
        fetch(pieces[:group], shards.at[0], sems.at[0])
        fetch(pieces[group:], shards.at[1], sems.at[1])
        bias_f32[...] = jnp.zeros_like(bias_f32)
        lane = lax.broadcasted_iota(jnp.int32, (1, width), 1)
        for device, block in each_shard(flags, chips, blocks_of):
            place_columns(w_f32, device, block, 0, rows, 6, width)
            start = 0
            for i, count in enumerate((6 * rows, rows, bias_f32.shape[0] * rows - 8 * rows, rows)):
                low, high = device * count, (device + 1) * count
                for part in range(low // width, (high - 1) // width + 1):
                    at = lane + part * width
                    bias_f32[start + part : start + part + 1] += jnp.where(
                        (at >= low) & (at < high), block[9 * rows + i : 9 * rows + i + 1], 0.0
                    )
                start += 2 * chips * count // width
        for part in range(6):
            cols = slice(part * width, (part + 1) * width)
            mod[:, cols] = dot(cond[...], w_f32[:, cols].astype(bf16)) + bias_f32[part : part + 1]
        for part in range(bias_f32.shape[0] - 6):
            bias[:, part * width : (part + 1) * width] = bias_f32[6 + part : 7 + part]
        for device, block in each_shard(flags, chips, blocks_of):
            place_columns(w_f32, device, block, 6 * rows, rows, 3, width)
        w_qkv[...] = w_f32[:, : 3 * width].astype(bf16)

    @pl.when((pair == 0) & is_live(flags, slot))
    def _():
        shift = mod[pl.ds(slot, 1), :width]
        scale = 1.0 + mod[pl.ds(slot, 1), width : 2 * width]
        row_block = 256

        def project(ref):
            @pl.loop(0, length // row_block)
            def _(i):
                r = pl.ds(pl.multiple_of(i * row_block, row_block), row_block)
                normed, _ = norm(ref[0, r, :].astype(f32))
                h1 = (normed * scale + shift).astype(bf16)
                result = dot(h1, w_qkv[...]).astype(bf16)
                for kind in range(3):
                    for p in range(pairs):
                        at = kind * width + p * PAIR
                        qkv[0, kind, p, r, :] = result[:, at : at + PAIR]

        @pl.when(slot < flags[KEEP])
        def _():
            project(own_x)

        @pl.when(slot >= flags[KEEP])
        def _():
            project(far_x)

    @pl.when(is_live(flags, slot))
    def _():
        attend_pair(qkv, pair, expo, att, inv)


def attend_forward(flags, own_x, far_x, cond, mine, other, bias_rows):
    steps, length, width = own_x.shape
    pairs = width // PAIR
    shards_shape = (2, len(mine)) + mine[0].shape
    args = (flags, own_x, far_x, cond, *mine, *other)

    def at(s, p, flags):
        return live_at(flags, s, p, pairs) + (0, 0)

    whole = pl.BlockSpec((1, 3, pairs, length, PAIR), lambda s, p, flags: (at(s, p, flags)[0], 0, 0, 0, 0))
    part = pl.BlockSpec((1, 1, length, PAIR), at)
    return call(
        attend_forward_body,
        (steps, pairs),
        [
            pl.BlockSpec((1, length, width), lambda s, p, flags: (own_slot(flags, s), 0, 0)),
            fixed(far_x.shape), fixed(cond.shape),
        ] + [anywhere] * (2 * len(mine)),
        [
            whole,
            pl.BlockSpec((1, 2, length, length), at),
            part, part,
            fixed((8, 6 * width)), fixed((1, (bias_rows - 6) * width)), fixed((width, 3 * width)),
        ],
        [
            shape_of((steps, 3, pairs, length, PAIR), bf16),
            shape_of((steps, 2 * pairs, length, length), bf16),
            shape_of((steps, pairs, length, PAIR), bf16),
            shape_of((steps, pairs, length, PAIR), f32),
            shape_of((8, 6 * width), f32),
            shape_of((1, (bias_rows - 6) * width), f32),
            shape_of((width, 3 * width), bf16),
        ],
        [
            pltpu.VMEM((width, 6 * width), f32),
            pltpu.VMEM((bias_rows, width), f32),
            pltpu.VMEM(shards_shape, bf16),
            pltpu.SemaphoreType.DMA((2, len(mine))),
        ],
        "attend_forward", 30 * 10**9, args,
    )


def pack_chunk(flags, device, chunk, keep, send):
    place = jnp.bitwise_xor(flags[PLACE], chip_order(device >> 1, keep.shape[0]))

    @pl.when(flags[CORE] == (device & 1))
    def _():
        keep[place] = chunk[...].astype(keep.dtype)

    @pl.when(flags[CORE] != (device & 1))
    def _():
        send[place] = chunk[...].astype(bf16)


def feed_forward_body(
    steps, flags, own_x, far_x, own_g, far_g, att, inv, mod, bias, *refs
):
    (
        own_out, far_out, grad_x1, grad_att, note, keep, send,
        x_s, g_s, w_out, w_up, w_down, sum_out, sum_up, sum_down_t, down_f32, chunk, bias_sum,
        grad_mod, note_s, shards, sems,
    ) = refs[-22:]
    pieces = refs[:-22]
    slot = pl.program_id(0)
    step = pl.program_id(1)
    own, far, dead = kinds(flags, slot, steps)
    width = x_s.shape[1]
    hidden_units = w_up.shape[1]
    ratio = hidden_units // width
    group, _, others = shards.shape[:3]
    chips = group * others
    rows = width // (2 * chips)

    def blocks_of(place):
        part, place = lax.div(place, others), lax.rem(place, others)
        return shards[part, 0, place], shards[part, 1, place]

    @pl.when((slot == 0) & (step == 0))
    def _():
        fetch(pieces, shards, sems)
        for device, block in each_shard(flags, chips, blocks_of):
            place_columns(sum_out, device, block, 0, rows, 1, width)
            place_columns(sum_up, device, block, rows, rows, ratio, width)
            place_columns(
                down_f32, device, block, (1 + ratio) * rows, ratio * rows, 1, width
            )
        w_out[...] = sum_out[...].astype(bf16)
        w_up[...] = sum_up[...].astype(bf16)
        w_down[...] = down_f32[...].astype(bf16)
        for ref in (sum_out, sum_up, sum_down_t, bias_sum, chunk, grad_mod):
            ref[...] = jnp.zeros_like(ref)

    @pl.when(dead)
    def _():
        own_out[...] = jnp.zeros_like(own_out)

    @pl.when(own)
    def _():
        x_s[...] = own_x[0].astype(f32)
        g_s[...] = own_g[0].astype(f32)

    @pl.when(far)
    def _():
        x_s[...] = far_x[0].astype(f32)
        g_s[...] = far_g[0].astype(f32)

    @pl.when(is_live(flags, slot))
    def _():
        def vector(part):
            return mod[pl.ds(slot, 1), part * width : (part + 1) * width]

        gate1, shift2, scale2, gate2 = vector(2), vector(3), 1.0 + vector(4), vector(5)
        b_out = bias[:, :width]
        b_up = bias[:, width : width + hidden_units]
        b_down = bias[:, width + hidden_units :]

        def lanes(ref):
            return jnp.concatenate([ref[0, p] for p in range(ref.shape[1])], 1)

        attended = lanes(att)
        branch1 = dot(attended, w_out[...]) + b_out
        x1 = x_s[...] + gate1 * branch1
        normed2, rstd = norm(x1)
        h2 = (normed2 * scale2 + shift2).astype(bf16)
        pre = dot(h2, w_up[...]) + b_up
        cdf = 0.5 * (1.0 + lax.erf(pre * (1 / math.sqrt(2.0))))
        hidden = (pre * cdf).astype(bf16)
        slope = cdf + pre * jnp.exp2(pre * pre * (-0.5 * LOG2E)) * (1 / math.sqrt(2 * math.pi))
        branch2 = dot(hidden, w_down[...]) + b_down
        result = (x1 + gate2 * branch2).astype(bf16)

        @pl.when(own)
        def _():
            own_out[0] = result

        @pl.when(far)
        def _():
            far_out[0] = result

        grad = g_s[...]
        grad_b2 = (gate2 * grad).astype(bf16)
        grad_pre = (dot(grad_b2, w_down[...], 1, 1) * slope).astype(bf16)
        grad_h2 = dot(grad_pre, w_up[...], 1, 1)
        grad_n = grad_h2 * scale2
        g_x1 = grad + rstd * (
            grad_n
            - jnp.mean(grad_n, -1, keepdims=True)
            - normed2 * jnp.mean(grad_n * normed2, -1, keepdims=True)
        )
        grad_b1 = (gate1 * g_x1).astype(bf16)
        grad_x1[0] = g_x1
        g_att = (dot(grad_b1, w_out[...], 1, 1) * lanes(inv)).astype(bf16)
        for p in range(width // PAIR):
            grad_att[0, p] = g_att[:, p * PAIR : (p + 1) * PAIR]

        def add_mod(part, value):
            grad_mod[pl.ds(slot, 1), part * width : (part + 1) * width] += row_sum(value)

        add_mod(0, g_x1 * branch1)
        add_mod(1, grad_h2)
        add_mod(2, grad_h2 * normed2)
        add_mod(3, grad * branch2)
        sum_out[...] += dot(attended, grad_b1, 0, 0)
        sum_up[...] += dot(h2, grad_pre, 0, 0)
        sum_down_t[...] += dot(grad_b2, hidden, 0, 0)
        bias_sum[:, :width] += row_sum(grad_b1.astype(f32))
        bias_sum[:, width : width + hidden_units] += row_sum(grad_pre.astype(f32))
        bias_sum[:, width + hidden_units :] += row_sum(grad_b2.astype(f32))

    @pl.when((slot == pl.num_programs(0) - 1) & (step == pl.num_programs(1) - 1))
    def _():
        down_f32[...] = sum_down_t[...].T
        for device in range(2 * chips):
            span = slice(device * rows, (device + 1) * rows)
            chunk[:rows] = sum_out[span]
            for part in range(ratio):
                chunk[(1 + part) * rows : (2 + part) * rows] = sum_up[
                    span, part * width : (part + 1) * width
                ]
            chunk[(1 + ratio) * rows : (1 + 2 * ratio) * rows] = down_f32[
                device * ratio * rows : (device + 1) * ratio * rows
            ]
            up_row = 1 + device * ratio * rows // width
            for i, part in enumerate((0, up_row, 1 + ratio)):
                at = (1 + 2 * ratio) * rows + i
                chunk[at : at + 1] = bias_sum[:, part * width : (part + 1) * width]
            pack_chunk(flags, device, chunk, keep, send)
        note_s[...] = jnp.zeros_like(note_s)
        for row in range(4 * steps):
            part = row % 4
            note_s[row : row + 1] = grad_mod[
                row // 4 : row // 4 + 1, part * width : (part + 1) * width
            ]
        note[...] = note_s[...].astype(bf16)


def feed_forward(
    flags, own_x, far_x, own_g, far_g, att, inv, mod, bias, shards, hidden_units
):
    steps, length, width = own_x.shape
    row_block = 1024
    blocks = length // row_block
    group, others = len(shards), shards[0].shape[1]
    rows = width // (2 * group * others)
    ratio = hidden_units // width
    packed_rows = up_to((1 + 2 * ratio) * rows + 3, 16)
    sum_shape = (group * others, packed_rows, width)
    note_shape = (up_to(4 * steps, 16), width)

    def own(s, b, flags):
        return (own_slot(flags, s), jnp.where(s < flags[KEEP], b, blocks - 1), 0)

    def far(s, b, flags):
        keep = flags[KEEP]
        return (0, jnp.where(s < keep, 0, jnp.where(s == keep, b, blocks - 1)), 0)

    def live(s, b, flags):
        return live_at(flags, s, b, blocks) + (0,)

    def live_parts(s, b, flags):
        at, part = live_at(flags, s, b, blocks)
        return (at, 0, part, 0)

    def own_result(s, b, flags):
        own, _, dead = kinds(flags, s, steps)
        return (result_slot(flags, s, steps), jnp.where(own | dead, b, blocks - 1), 0)

    def block(where):
        return pl.BlockSpec((1, row_block, width), where)

    def parts(count):
        return pl.BlockSpec((1, count, row_block, PAIR), live_parts)

    pairs = width // PAIR
    args = (flags, own_x, far_x, own_g, far_g, att, inv, mod, bias, *shards)
    return call(
        functools.partial(feed_forward_body, steps),
        (steps + 1, blocks),
        [
            block(own), block(far), block(own), block(far), parts(pairs), parts(pairs),
            fixed(mod.shape), fixed(bias.shape),
        ] + [anywhere] * group,
        [
            block(own_result), block(far), block(live), parts(pairs),
            fixed(note_shape), fixed(sum_shape), fixed(sum_shape),
        ],
        [
            shape_of((steps, length, width), bf16),
            shape_of((1, length, width), bf16),
            shape_of((steps, length, width), f32),
            shape_of((steps, pairs, length, PAIR), bf16),
            shape_of(note_shape, bf16),
            shape_of(sum_shape, bf16),
            shape_of(sum_shape, bf16),
        ],
        [
            pltpu.VMEM((row_block, width), f32),
            pltpu.VMEM((row_block, width), f32),
            pltpu.VMEM((width, width), bf16),
            pltpu.VMEM((width, hidden_units), bf16),
            pltpu.VMEM((hidden_units, width), bf16),
            pltpu.VMEM((width, width), f32),
            pltpu.VMEM((width, hidden_units), f32),
            pltpu.VMEM((width, hidden_units), f32),
            pltpu.VMEM((hidden_units, width), f32),
            pltpu.VMEM((packed_rows, width), f32),
            pltpu.VMEM(bias.shape, f32),
            pltpu.VMEM((8, 4 * width), f32),
            pltpu.VMEM(note_shape, f32),
            pltpu.VMEM((group,) + shards[0].shape, bf16),
            pltpu.SemaphoreType.DMA((group,)),
        ],
        "feed_forward", 60 * 10**9, args,
    )


def attend_backward_pair(qkv, expo, att, grad_att, g_qkv, keys_t, values_t):
    length = att.shape[2]
    row_block = 1024
    keys = qkv[0, 1, 0]
    values = qkv[0, 2, 0]
    values_ones = jnp.concatenate([values, jnp.ones_like(values)], 1)
    lane = lax.broadcasted_iota(jnp.int32, (row_block, PAIR), 1)
    first = lane < HEAD
    for i in range(length // row_block):
        r = pl.ds(i * row_block, row_block)
        query = qkv[0, 0, 0, r, :]
        g_att = grad_att[0, 0, r, :]
        product = g_att.astype(f32) * att[0, 0, r, :].astype(f32)
        query_t = query.T
        g_att_t = g_att.T
        grads_q = []
        for head in range(2):
            sel = first if head == 0 else jnp.logical_not(first)
            delta = jnp.sum(jnp.where(sel, product, 0.0), -1, keepdims=True)
            high = delta.astype(bf16).astype(f32)
            extra = jnp.where(
                lane == 0, -high, jnp.where(lane == 1, high - delta, 0.0)
            ).astype(bf16)
            left = jnp.concatenate([jnp.where(sel, g_att, jnp.zeros_like(g_att)), extra], 1)
            e = expo[0, head, r, :]
            grad_s = e * dot(left, values_ones, 1, 1).astype(bf16)
            grads_q.append(dot(grad_s, keys))
            span = slice(head * HEAD, (head + 1) * HEAD)
            add_k = dot(query_t[span], grad_s)
            add_v = dot(g_att_t[span], e)
            if i == 0:
                keys_t[span] = add_k
                values_t[span] = add_v
            else:
                keys_t[span] += add_k
                values_t[span] += add_v
        g_qkv[0, r, :] = (jnp.where(first, grads_q[0], grads_q[1]) * 0.125).astype(bf16)
    g_qkv[1] = (keys_t[...] * 0.125).astype(bf16).T
    g_qkv[2] = values_t[...].astype(bf16).T


def first_pairs_body(flags, qkv, expo, att, grad_att, g_qkv, keys_t, values_t):
    @pl.when(is_live(flags, pl.program_id(0)))
    def _():
        attend_backward_pair(qkv, expo, att, grad_att, g_qkv.at[0, 0], keys_t, values_t)


def first_pairs(flags, qkv, expo, att, grad_att):
    steps, _, pairs, length, _ = qkv.shape
    pairs -= 1

    def part(s, p, flags):
        return live_at(flags, s, p, pairs) + (0, 0)

    def qkv_at(s, p, flags):
        at, pair = live_at(flags, s, p, pairs)
        return (at, 0, pair, 0, 0)

    heads = pl.BlockSpec((1, 1, length, PAIR), part)
    return call(
        first_pairs_body,
        (steps, pairs),
        [
            pl.BlockSpec((1, 3, 1, length, PAIR), qkv_at),
            pl.BlockSpec((1, 2, length, length), part),
            heads, heads,
        ],
        pl.BlockSpec((1, 1, 3, length, PAIR), lambda s, p, flags: part(s, p, flags) + (0,)),
        shape_of((steps, pairs, 3, length, PAIR), bf16),
        [pltpu.VMEM((PAIR, length), f32), pltpu.VMEM((PAIR, length), f32)],
        "first_pairs", 40 * 10**9, (flags, qkv, expo, att, grad_att),
    )


def finish_body(
    steps, flags, own_x, far_x, qkv, expo, att, grad_att, grad_x1, mod, w_qkv, g_first,
    own_grad, far_grad, note, keep, send, g_last, keys_t, values_t, sum_qkv, chunk, grad_mod, note_s,
):
    slot = pl.program_id(0)
    own, far, dead = kinds(flags, slot, steps)
    length, width = own_x.shape[1:]
    chips = keep.shape[0]
    rows = width // (2 * chips)

    @pl.when(slot == 0)
    def _():
        for ref in (sum_qkv, chunk, grad_mod):
            ref[...] = jnp.zeros_like(ref)

    @pl.when(dead)
    def _():
        own_grad[...] = jnp.zeros_like(own_grad)

    @pl.when(is_live(flags, slot))
    def _():
        attend_backward_pair(qkv, expo, att, grad_att, g_last, keys_t, values_t)

    def finish(x_ref, out_ref):
        shift = mod[pl.ds(slot, 1), :width]
        scale = 1.0 + mod[pl.ds(slot, 1), width : 2 * width]
        row_block = 1024
        for i in range(length // row_block):
            r = pl.ds(i * row_block, row_block)
            normed, rstd = norm(x_ref[0, r, :].astype(f32))
            h1 = (normed * scale + shift).astype(bf16)
            grad = []
            for kind in range(3):
                grad += [g_first[0, p, kind, r, :] for p in range(g_first.shape[1])]
                grad.append(g_last[kind, r, :])
            grad = jnp.concatenate(grad, 1)
            grad_h1 = dot(grad, w_qkv[...], 1, 1)
            sum_qkv[...] += dot(h1, grad, 0, 0)
            grad_mod[pl.ds(slot, 1), :width] += row_sum(grad_h1)
            grad_mod[pl.ds(slot, 1), width:] += row_sum(grad_h1 * normed)
            grad_n = grad_h1 * scale
            out_ref[0, r, :] = (
                grad_x1[0, r, :]
                + rstd
                * (
                    grad_n
                    - jnp.mean(grad_n, -1, keepdims=True)
                    - normed * jnp.mean(grad_n * normed, -1, keepdims=True)
                )
            ).astype(out_ref.dtype)

    @pl.when(own)
    def _():
        finish(own_x, own_grad)

    @pl.when(far)
    def _():
        finish(far_x, far_grad)

    @pl.when(slot == steps)
    def _():
        for device in range(2 * chips):
            for part in range(3):
                chunk[part * rows : (part + 1) * rows] = sum_qkv[
                    device * rows : (device + 1) * rows, part * width : (part + 1) * width
                ]
            pack_chunk(flags, device, chunk, keep, send)
        note_s[...] = jnp.zeros_like(note_s)
        for row in range(2 * steps):
            part = row % 2
            note_s[row : row + 1] = grad_mod[
                row // 2 : row // 2 + 1, part * width : (part + 1) * width
            ]
        note[...] = note_s[...].astype(bf16)


def finish(
    flags, own_x, far_x, qkv, expo, att, grad_att, grad_x1, mod, w_qkv, g_first, chips
):
    steps, length, width = own_x.shape
    last = width // PAIR - 1
    sum_shape = (chips, up_to(3 * width // (2 * chips), 8), width)
    note_shape = (up_to(2 * steps, 8), width)

    def at(*part):
        return lambda s, flags: (live_at(flags, s, 0, 1)[0],) + part

    def block(where):
        return pl.BlockSpec((1, length, width), where)

    heads = pl.BlockSpec((1, 1, length, PAIR), at(last, 0, 0))
    return call(
        functools.partial(finish_body, steps),
        (steps + 1,),
        [
            block(lambda s, flags: (own_slot(flags, s), 0, 0)),
            block(lambda s, flags: (0, 0, 0)),
            pl.BlockSpec((1, 3, 1, length, PAIR), at(0, last, 0, 0)),
            pl.BlockSpec((1, 2, length, length), at(last, 0, 0)),
            heads, heads, block(at(0, 0)), fixed(mod.shape), fixed(w_qkv.shape),
            pl.BlockSpec((1, last, 3, length, PAIR), at(0, 0, 0, 0)),
        ],
        [
            block(lambda s, flags: (result_slot(flags, s, steps), 0, 0)),
            block(lambda s, flags: (0, 0, 0)),
            fixed(note_shape), fixed(sum_shape), fixed(sum_shape),
        ],
        [
            shape_of((steps, length, width), f32),
            shape_of((1, length, width), bf16),
            shape_of(note_shape, bf16),
            shape_of(sum_shape, f32),
            shape_of(sum_shape, bf16),
        ],
        [
            pltpu.VMEM((3, length, PAIR), bf16),
            pltpu.VMEM((PAIR, length), f32),
            pltpu.VMEM((PAIR, length), f32),
            pltpu.VMEM((width, 3 * width), f32),
            pltpu.VMEM(sum_shape[1:], f32),
            pltpu.VMEM((8, 2 * width), f32),
            pltpu.VMEM(note_shape, f32),
        ],
        "finish", 40 * 10**9,
        (flags, own_x, far_x, qkv, expo, att, grad_att, grad_x1, mod, w_qkv, g_first),
    )


def swap(array, mask):
    count = lax.axis_size("dp")
    return lax.ppermute(array, "dp", [(i, i ^ mask) for i in range(count)])


def tie(value, *others):
    return lax.optimization_barrier((value,) + others)[0]


def chip_groups(chips):
    bits = chips.bit_length() - 1
    return tuple(tuple(range(max(top - 2, 0), top)) for top in range(bits, 0, -2))


def chip_order(chip, chips):
    place, low = 0, 0
    for group in chip_groups(chips):
        place = place | ((chip >> group[0]) & ((1 << len(group)) - 1)) << low
        low += len(group)
    return place


def group_masks(group):
    return [sum(((k >> i) & 1) << b for i, b in enumerate(group)) for k in range(1, 1 << len(group))]


def gather_group(held, group):
    return [held] + [swap(held, mask << 1) for mask in group_masks(group)]


def stage_body(adds, sends, with_notes, held, notes, *refs):
    adds, outs = refs[:adds], refs[adds:]
    parts, rows, _ = held.shape
    size = parts * rows
    keep, joined, outs = outs[0], outs[1], outs[2:]
    own = notes.shape[0]
    joined[:own] = notes[...]
    if adds[0].shape[0] > size:
        for k, add in enumerate(adds):
            joined[(k + 1) * own : (k + 2) * own] = add[size:]
    count = parts // (sends + 1)
    for part in range(parts):
        total = held[part].astype(f32)
        for add in adds:
            total = total + add[part * rows : (part + 1) * rows].astype(f32)
        if part < count:
            keep[part] = total
        else:
            at = part % count * rows
            outs[part // count - 1][at : at + rows] = total.astype(bf16)
    if with_notes:
        for out in outs:
            out[count * rows :] = joined[...]


def stage(held, notes, adds, sends=0, with_notes=True):
    parts, rows, width = held.shape
    extra = adds[0].shape[0] - parts * rows
    count = parts // (sends + 1)
    joined = notes.shape[0] + len(adds) * extra
    size = count * rows + (joined if with_notes else 0)
    keep, joined, *outs = pl.pallas_call(
        functools.partial(stage_body, len(adds), sends, with_notes),
        out_shape=[shape_of((count, rows, width), f32), shape_of((joined, width), bf16)]
        + [shape_of((size, width), bf16)] * sends,
        name="stage",
    )(held, notes, *adds)
    return keep, joined, outs


def reduce_start(group, sums, notes):
    masks = group_masks(group)
    parts = [held.shape[0] // (len(masks) + 1) for held in sums]
    got = []
    for k, mask in enumerate(masks):
        pieces = [held[(k + 1) * n : (k + 2) * n].astype(bf16) for held, n in zip(sums, parts)]
        pieces += notes
        width = pieces[0].shape[-1]
        got.append(swap(jnp.concatenate([p.reshape(-1, width) for p in pieces], 0), mask << 1))
    return [held[:part] for held, part in zip(sums, parts)], notes, got


def reduce_done(totals, notes, got, *after):
    got = lax.optimization_barrier(tuple(got) + after)[: len(got)]
    joined = [[note] for note in notes]
    for block in got:
        start = 0
        for i, piece in enumerate(totals + notes):
            size = math.prod(piece.shape[:-1])
            part = block[start : start + size].reshape(piece.shape)
            start += size
            if i < len(totals):
                totals = totals[:i] + [totals[i] + part.astype(f32)] + totals[i + 1 :]
            else:
                joined[i - len(totals)].append(part)
    return totals, [jnp.concatenate(blocks, 0) for blocks in joined]


def hand_back_body(at, back_out, back_grad, _out, _grad, _after, out, grad, done, low, high, sems):
    done[...] = jnp.zeros_like(done)

    @pl.when(at[0] > 0)
    def _():
        loads = [
            pltpu.make_async_copy(back_grad.at[0], low.at[0], sems.at[0]),
            pltpu.make_async_copy(back_out.at[0], low.at[1], sems.at[1]),
        ]
        for load in loads:
            load.start()
        loads[0].wait()
        high[...] = low[0].astype(f32)
        loads[1].wait()
        stores = [
            pltpu.make_async_copy(high, grad.at[at[1]], sems.at[2]),
            pltpu.make_async_copy(low.at[1], out.at[at[1]], sems.at[3]),
        ]
        for store in stores:
            store.start()
        for store in stores:
            store.wait()


def hand_back(at, back_out, back_grad, own_out, own_grad, after):
    return pl.pallas_call(
        hand_back_body,
        grid_spec=pltpu.PrefetchScalarGridSpec(
            num_scalar_prefetch=1,
            grid=(1,),
            in_specs=[anywhere] * 5,
            out_specs=[anywhere] * 2 + [fixed((8, 128))],
            scratch_shapes=[
                pltpu.VMEM((2,) + own_grad.shape[1:], bf16),
                pltpu.VMEM(own_grad.shape[1:], f32),
                pltpu.SemaphoreType.DMA((4,)),
            ],
        ),
        out_shape=[
            shape_of(own_out.shape, bf16), shape_of(own_grad.shape, f32), shape_of((8, 128), f32),
        ],
        input_output_aliases={3: 0, 4: 1},
        name="hand_back",
    )(at, back_out, back_grad, own_out, own_grad, after)


def condition_body(at, steps, order, *refs):
    pieces, (left, blocks, cond, sems) = refs[:-4], refs[-4:]
    width = cond.shape[1]
    rows = width * steps // cond.shape[0]
    me = lax.axis_index("dp").astype(jnp.int32)
    base = at // 16 * 16
    fetch([piece.at[:, :, pl.ds(base, 16), :] for piece in pieces], blocks, sems)
    at -= base
    for core in range(2):
        for place, (part, other) in enumerate(order):
            start = (core * len(order) + place) * steps
            cond[start : start + steps] = blocks[part, core, other, at : at + steps].astype(f32)
    turned = pltpu.roll(cond[...], lax.rem(width - me * rows, width), 1)[:, :PAIR]
    lane = lax.broadcasted_iota(jnp.int32, turned.shape, 1)
    left[...] = jnp.where(lane < rows, turned, jnp.where(lane == rows, 1.0, 0.0)).astype(bf16)


def condition_columns(pieces, sizes, cond_row, steps):
    _, others, _, width = pieces[0].shape
    chips = len(pieces) * others
    order = []
    for place in range(chips):
        digits, rest = [], place
        for size in sizes:
            digits.append(rest % size)
            rest //= size
        other, low = 0, 1
        for digit, size in zip(reversed(digits[1:]), reversed(sizes[1:])):
            other += digit * low
            low *= size
        order.append((digits[0], other))
    return pl.pallas_call(
        functools.partial(condition_body, cond_row, steps, order),
        in_specs=[anywhere] * len(pieces),
        out_shape=shape_of((2 * chips * steps, PAIR), bf16),
        scratch_shapes=[
            pltpu.VMEM((len(pieces), 2, others, 16, width), bf16),
            pltpu.VMEM((2 * chips * steps, width), f32),
            pltpu.SemaphoreType.DMA((len(pieces),)),
        ],
        name="condition_columns",
    )(*pieces)


def result_body(
    sums1, sums2, left, mine1, other1, mine2, other2, _done,
    ada, b_ada, qkv, out, b_out, up, b_up, down, b_down, ada_sum,
):
    rows, width = out.shape
    ratio = up.shape[1] // width
    me = lax.axis_index("dp").astype(jnp.int32)
    for part in range(3):
        qkv[:, part * width : (part + 1) * width] = sums1[0, part * rows : (part + 1) * rows]
    out[...] = sums2[0, :rows]
    for part in range(ratio):
        up[:, part * width : (part + 1) * width] = sums2[
            0, (1 + part) * rows : (2 + part) * rows
        ]
    after = (1 + 2 * ratio) * rows
    down[...] = sums2[0, after - ratio * rows : after]
    for i, ref in enumerate((b_out, b_up, b_down)):
        size = ref.shape[1]
        line = sums2[0, after + i : after + i + 1]
        shift = lax.rem(width - lax.rem(me * size, width), width)
        ref[...] = pltpu.roll(line, shift, 1)[:, :size]
    half = left.shape[0] // 2
    start = 0
    for count, refs in ((2, (mine1, other1)), (4, (mine2, other2))):
        source = lax.broadcasted_iota(jnp.int32, (half, count * half), 1)
        target = lax.broadcasted_iota(jnp.int32, (half, count * half), 0)
        for part in range(count):
            pick = jnp.where(source == target * count + part, 1.0, 0.0).astype(bf16)
            total = 0.0
            for i, ref in enumerate(refs):
                picked = dot(pick, ref[...]).astype(bf16)
                total = total + dot(left[i * half : (i + 1) * half], picked, 0, 0)
            cols = slice((start + part) * width, (start + part + 1) * width)
            ada[:, cols] = total[:rows]
            ada_sum[:, cols] = total[rows : rows + 1]
        start += count
    b_ada[...] = pltpu.roll(ada_sum[...], lax.rem(6 * width - me * 6 * rows, 6 * width), 1)[
        :, : 6 * rows
    ]


def results(sums1, sums2, left, mine1, other1, mine2, other2, done, rows, ratio):
    width = sums1.shape[2]
    shapes = [
        (rows, 6 * width), (1, 6 * rows), (rows, 3 * width), (rows, width), (1, rows),
        (rows, ratio * width), (1, ratio * rows), (ratio * rows, width), (1, rows),
    ]
    return pl.pallas_call(
        result_body,
        out_shape=[shape_of(s, f32) for s in shapes],
        scratch_shapes=[pltpu.VMEM((1, 6 * width), f32)],
        name="results",
    )(sums1, sums2, left, mine1, other1, mine2, other2, done)


def body(
    fields, conditions, step_counts, cotangent,
    w_ada, b_ada, w_qkv, w_out, b_out, w_up, b_up, w_down, b_down,
):
    devices = lax.axis_size("dp")
    chips = devices // 2
    me = lax.axis_index("dp").astype(jnp.int32)
    chip, core = me >> 1, me & 1
    steps, length, width = fields.shape[1:]
    hidden_units = w_up.shape[1]
    ratio = hidden_units // width
    rows = width // devices
    fields, conditions, cotangent = fields[0], conditions[0], cotangent[0]
    groups = chip_groups(chips)

    count = step_counts[0]
    first, second = pack_shards(
        w_ada, w_qkv, w_out, w_up, w_down, b_ada, b_out, b_up, b_down
    )
    head = jnp.concatenate([conditions, jnp.full((4, width), count, bf16)], 0)
    other_head = swap(tie(head, first), 1)
    other_count = other_head[steps, 0].astype(jnp.int32)
    give = count - other_count >= 2
    take = (other_count - count >= 2).astype(jnp.int32)
    keep = count - give.astype(jnp.int32)
    flags = jnp.stack([keep, take, chip_order(chip, chips), core])
    far_cond = lax.dynamic_index_in_dim(other_head, other_count - 1, 0)
    cond = jnp.concatenate([conditions, jnp.zeros((8 - steps, width), bf16)], 0)
    cond = jnp.where((jnp.arange(8) == keep)[:, None] & (take > 0), far_cond, cond)
    cond_act = jax.nn.silu(cond.astype(f32)).astype(bf16)

    cond_row = (1 + 2 * ratio) * rows
    mine_a = first[None]
    mine_b = lax.dynamic_update_slice_in_dim(second, cond_act[:steps], cond_row, 0)[None]
    for group in groups[:-1]:
        pieces = lax.optimization_barrier((*gather_group(mine_a, group), cond_act, flags))[:-2]
        mine_a = jnp.concatenate(pieces, 0)
    far_x = swap(tie(lax.dynamic_index_in_dim(fields, count - 1, 0), mine_a), 1)
    far_g = swap(tie(lax.dynamic_index_in_dim(cotangent, count - 1, 0), mine_a), 1)
    for group in groups[:-1]:
        mine_b = jnp.concatenate(gather_group(tie(mine_b, far_x, far_g), group), 0)
    both_b = jnp.stack([mine_b, swap(tie(mine_b, mine_a), 1)])
    mine_a = gather_group(mine_a, groups[-1])
    other_a = [swap(piece, 1) for piece in mine_a]
    back_at = jnp.stack([give.astype(jnp.int32), count - 1])
    first_kernel = lax.optimization_barrier(
        (flags, both_b, far_x, far_g, cond_act, back_at)
    )
    back_at = first_kernel[5]
    qkv, expo, att, inv, mod, bias, full_qkv = attend_forward(
        first_kernel[0], fields, far_x, cond_act, mine_a, other_a, 8 + ratio
    )
    all_b = gather_group(first_kernel[1], groups[-1])
    all_b = lax.optimization_barrier((*all_b, mod))[:-1]
    own_out, far_out, grad_x1, grad_att, note2, keep2, send2 = feed_forward(
        flags, fields, far_x, cotangent, far_g, att, inv, mod, bias, all_b, hidden_units
    )

    up_groups = tuple(reversed(groups))
    late = up_groups[2:]
    masks = [[mask << 1 for mask in group_masks(group)] for group in up_groups]
    left = condition_columns(all_b, [len(m) + 1 for m in masks], cond_row, steps)
    got2 = tie(swap(send2.reshape(-1, width), 1), left)
    held2, note2, sends = stage(keep2, note2, [got2], len(masks[0]))
    gots = [swap(send, mask) for send, mask in zip(sends, masks[0])]
    back_out = swap(far_out, 1)
    g_first = first_pairs(tie(flags, held2), qkv, expo, att, grad_att)
    gots = lax.optimization_barrier((*gots, g_first))[:-1]
    held2, note2, sends = stage(held2, note2, gots, len(masks[1]))
    gots = [swap(send, mask) for send, mask in zip(sends, masks[1])]
    own_grad, far_grad, note1, keep1, send1 = finish(
        tie(flags, held2, back_out), fields, far_x, qkv, expo, att, grad_att, grad_x1, mod, full_qkv, g_first,
        chips,
    )
    got1 = swap(send1, 1)
    gots = lax.optimization_barrier((*gots, keep1))[:-1]
    held2, note2, sends = stage(held2, note2, gots, len(masks[2]) if late else 0)
    held1 = keep1 + got1.astype(f32)
    back_grad = swap(far_grad, 1)
    note1 = note1[None]

    going = reduce_start(up_groups[0], [held1], [note1])
    (held1,), (note1,) = reduce_done(*going, back_grad)
    own_out, own_grad, done = hand_back(
        back_at, back_out, back_grad, own_out, own_grad, held1
    )
    for i, group in enumerate(up_groups[1:]):
        if i > 0:
            gots = [swap(send, mask) for send, mask in zip(sends, masks[i + 1])]
            held2, note2, sends = stage(
                held2, note2, gots, len(masks[i + 2]) if i + 2 < len(masks) else 0
            )
        (held1,), (note1,) = reduce_done(*reduce_start(group, [held1], [note1]))
    note1 = note1.reshape(-1, width)
    other1, other2 = swap(note1, 1), swap(note2, 1)
    grads = results(held1, held2, left, note1, other1, note2, other2, done, rows, ratio)
    grads = [g[0] if i in (1, 4, 6, 8) else g for i, g in enumerate(grads)]

    return (own_out[None], own_grad[None], *grads)


def solution(mesh):
    item, matrix, vector = P("dp", None, None, None), P("dp", None), P("dp")
    return jax.shard_map(
        body,
        mesh=mesh,
        in_specs=(
            item, P("dp", None, None), vector, item,
            matrix, vector, matrix, matrix, vector, matrix, vector, matrix, vector,
        ),
        out_specs=(
            item, item, matrix, vector, matrix, matrix, vector, matrix, vector, matrix, vector,
        ),
        check_vma=False,
    )
```
